128 devices in a mesh: seq: 16 (over z, x), user: 8 (over y, core).
Axes of the slice: x: 4, y: 4, z: 4, core: 2. Of those that a mesh axis runs over, the one named last changes fastest.
Arguments:
- query: bfloat16 [8, 8192, 512], P('user', 'seq'), may hold values from -6 to 6
- key: bfloat16 [8, 8192, 512], P('user', 'seq'), may hold values from -6 to 6
- value: bfloat16 [8, 8192, 512], P('user', 'seq'), may hold values from -6 to 6
- gate: bfloat16 [8, 8192, 512], P('user', 'seq'), may hold values from -6 to 6
- history: bfloat16 [8, 8192, 128], P('user', 'seq'), may hold values from -6 to 6
- w_out: bfloat16 [512, 128], replicated, may hold values from -0.25 to 0.25
- table: bfloat16 [524288, 128], P(('seq', 'user')), may hold values from -0.5 to 0.5
- item_owner: int32 [8, 8192, 5], P('user', 'seq'), may hold values from 0 to 127, all different within a row; in each aligned block of 512 rows (0 to 511, 512 to 1023, ..., all dimensions but the last counted through in order) at most 30 rows name the same one
- item_row: int32 [8, 8192, 5], P('user', 'seq'), may hold values from 0 to 4095
- global_blocks: int32 [8, 2], P('user'), may hold values from 0 to 63, as said below
- lengths: int32 [8], replicated, may hold values from 2048 to 8192, as said below
Outputs:
- d_query: bfloat16 [8, 8192, 512], P('user', 'seq')
- d_key: bfloat16 [8, 8192, 512], P('user', 'seq')
- d_value: bfloat16 [8, 8192, 512], P('user', 'seq')
- d_gate: bfloat16 [8, 8192, 512], P('user', 'seq')
- table_grad: float32 [524288, 128], P(('seq', 'user'))
The draws below stay inside these ranges and needn't reach their ends.
Inputs may be any that keep to these rules, and one draw needn't show every extreme that they name: `item_owner`: in the events of one device (512 aligned events of one user), no owner is named by more than 30 entries, a bound that some block reaches; the 5 owners of one event differ. `global_blocks`: the 2 block numbers of one user differ; the first lies among the blocks of the first 512 events. `lengths`: some user's length is 8192.
All inputs are finite; a program needn't handle non-finite values.
Results may differ from the reference program's by a relative error of at most 0.023.
Values may be sent and summed in bfloat16 or wider, within the bound.
No kernel may reach another device: no remote copies, remote signals or barrier semaphores. Data moves between devices by JAX's collectives and lax.ppermute only.
A program may use at most 128 MiB of HBM per device.

```python
import math
import jax
import jax.numpy as jnp
import numpy as np
from jax import lax

HEADS = 8
HEAD_DIM = 64
D = 512
E = 128
BLK = 128
GLOB = 2
NEG = 4
LEN_DEV = 512
ROWS_DEV = 4096
SEQ_LEN = 8192
USERS = 8
NBLOCKS = 64
NITEMS = 524288
CAP = 30
DEVICES = 128


def draw_global_blocks(key, part):
    key = jax.random.fold_in(key, 11)
    first_key, second_key, pick_key = jax.random.split(key, 3)
    first = jax.random.randint(first_key, (USERS,), 0, LEN_DEV // BLK)
    offset = jax.random.randint(second_key, (USERS,), 0, NBLOCKS - 1)
    second = (first + 1 + offset) % NBLOCKS
    chosen = jax.random.randint(pick_key, (), 0, USERS)
    picked = jnp.arange(USERS) == chosen
    first = jnp.where(picked, 0, first)
    second = jnp.where(picked, NBLOCKS - 1, second)
    return jnp.stack([first, second], axis=1).astype(jnp.int32)


def draw_lengths(key, part):
    key = jax.random.fold_in(key, 23)
    first, second = jax.random.split(key)
    drawn = jax.random.randint(first, (USERS,), SEQ_LEN // 4, SEQ_LEN + 1)
    chosen = jax.random.randint(second, (), 0, USERS)
    return jnp.where(jnp.arange(USERS) == chosen, SEQ_LEN, drawn).astype(jnp.int32)


def place_ends(values, own_key, least, high):
    longest = values.shape.index(max(values.shape))
    spots = []
    for shift in (0, 1):
        where = [jax.random.randint(jax.random.fold_in(own_key, axis), (), 0, length) for axis, length in enumerate(values.shape)]
        where[longest] = (where[longest] + shift) % values.shape[longest]
        spots.append(tuple(where))
    return values.at[spots[0]].set(least).at[spots[1]].set(high)


def steps_of(key, extent, cuts, least, largest):
    loudness, own = 1.0, jax.random.fold_in(key, 6)
    for axis_at, blocks in cuts:
        steps = jnp.exp(jax.random.uniform(jax.random.fold_in(own, axis_at), (blocks,), jnp.float32, least / len(cuts), largest / len(cuts)))
        loudness = loudness * jnp.repeat(steps, extent[axis_at] // blocks).reshape([-1 if axis == axis_at else 1 for axis in range(len(extent))])
    return loudness


def assign_block(stream_key, own, number, rows, count, top, reach, skew):
    order = jax.random.permutation(stream_key, count)
    heavy_load, ordinary = portions_of(count, rows * top, reach, skew, True), portions_of(count, rows * top, reach, skew, False)
    places = jnp.arange(count)

    def named(tallies, turn):
        used = int((tallies > 0).sum())
        fixed = max(1, used // 4)
        shifted = fixed + (places - fixed + turn * (used - fixed)) % max(1, count - fixed)
        return jnp.zeros((count,), jnp.int32).at[order[jnp.where(places < fixed, places, shifted)]].set(jnp.asarray(tallies, jnp.int32))

    tallies = jnp.where(number % 4 == 0, named(heavy_load, number // 4), named(ordinary, number - number // 4 - 1))
    mixed = jax.random.permutation(jax.random.fold_in(own, 3), count)
    giver, receiver = mixed[0:count // 2 * 2:2], mixed[1:count // 2 * 2:2]
    margin = jnp.minimum(tallies[giver] - 1, reach - tallies[receiver]) // 2
    margin = jnp.where((giver == order[0]) | (receiver == order[0]) | (tallies[receiver] == 0), 0, jnp.maximum(margin, 0))
    shifted = jax.random.randint(jax.random.fold_in(own, 4), (count // 2,), 0, 1 << 20) % (margin + 1)
    tallies = tallies.at[giver].add(-shifted).at[receiver].add(shifted)
    members = jnp.searchsorted(jnp.cumsum(tallies), jnp.arange(rows * top), side="right").astype(jnp.int32)
    table = members.reshape(top, rows).T
    table = table[jax.random.permutation(jax.random.fold_in(own, 1), rows)]
    turn = jax.random.randint(jax.random.fold_in(own, 2), (rows, 1), 0, top)
    return jnp.take_along_axis(table, (jnp.arange(top)[None, :] + turn) % top, axis=1)


def portions_of(amount, total, limit, lean, full):
    portions = [(1 << 20) // math.isqrt(grade ** lean) + 1 for grade in range(1, amount + 1)]
    largest = limit if full else min(limit, max(-(-total // amount), total * portions[0] // sum(portions)))
    least = 1 if total - largest >= amount - 1 else 0
    counts, surplus = [largest] + [least] * (amount - 1), total - largest - least * (amount - 1)
    while surplus > 0:
        movable = [i for i in range(1, amount) if counts[i] < largest] or [i for i in range(1, amount) if counts[i] < limit]
        mass, remaining = sum([portions[i] for i in movable]), surplus
        for i in movable:
            more = min(limit - counts[i], max(1, remaining * portions[i] // mass), surplus)
            counts[i] = counts[i] + more
            surplus = surplus - more
    return np.array(counts)


def gaussian(stream_key, dims, scale, most, cuts=(), kind=jnp.bfloat16):
    loudness = steps_of(stream_key, dims, cuts, -0.22, 0.18) if cuts else 1.0
    values = jax.random.normal(stream_key, dims, jnp.float32) * scale * loudness
    return jnp.minimum(jnp.maximum(values, -most), most).astype(kind)


def setup_inputs(seed: int = 0) -> dict:
    streams_of = jax.random.split(jax.random.key(seed), 12)
    query = gaussian(streams_of[0], (USERS, SEQ_LEN, D), 1.0, 6.0, ((0, 8), (1, 16)))
    key = gaussian(streams_of[1], (USERS, SEQ_LEN, D), 1.0, 6.0, ((0, 8), (1, 16)))
    value = gaussian(streams_of[2], (USERS, SEQ_LEN, D), 1.0, 6.0, ((0, 8), (1, 16)))
    gate = gaussian(streams_of[3], (USERS, SEQ_LEN, D), 1.0, 6.0, ((0, 8), (1, 16)))
    history = gaussian(streams_of[4], (USERS, SEQ_LEN, E), 1.0, 6.0, ((0, 8), (1, 16)))
    w_out = gaussian(streams_of[5], (D, E), D ** -0.5, 0.25)
    table = gaussian(streams_of[6], (NITEMS, E), E ** -0.5, 0.5, ((0, 128),))
    item_owner_keys = jax.random.split(jax.random.fold_in(streams_of[7], 1), USERS * SEQ_LEN // LEN_DEV)
    item_owner_turns = jax.random.permutation(jax.random.fold_in(streams_of[7], 3), USERS * SEQ_LEN // LEN_DEV)
    item_owner = jax.vmap(lambda own, number: assign_block(jax.random.fold_in(streams_of[7], 2), own, number, LEN_DEV, DEVICES, NEG + 1, CAP, 2))(item_owner_keys, item_owner_turns).reshape((USERS, SEQ_LEN, NEG + 1))
    item_row = place_ends(jax.random.randint(streams_of[8], (USERS, SEQ_LEN, NEG + 1), 0, ROWS_DEV), jax.random.fold_in(streams_of[8], 1), 0, ROWS_DEV - 1).astype(jnp.int32)
    global_blocks = draw_global_blocks(jax.random.fold_in(streams_of[11], 71), 0)
    lengths = draw_lengths(jax.random.fold_in(streams_of[11], 71), 0)
    return dict(query=query, key=key, value=value, gate=gate, history=history, w_out=w_out, table=table, item_owner=item_owner, item_row=item_row, global_blocks=global_blocks, lengths=lengths)


def product(form, left, right):
    return jnp.einsum(form, left.astype(jnp.float32), right.astype(jnp.float32), precision=lax.Precision.HIGHEST)

def key_mask(block, gids, length):
    offs = jnp.arange(BLK, dtype=jnp.int32)
    q_pos = block * BLK + offs
    prev_pos = (block - 1) * BLK + offs
    own_pos = block * BLK + offs
    glob_pos = gids[:, None] * BLK + offs[None, :]
    prev_ok = (prev_pos >= 0) & (prev_pos < length)
    own_ok = (own_pos[None, :] <= q_pos[:, None]) & (own_pos[None, :] < length)
    glob_ok = ((gids[:, None] < block - 1) & (glob_pos < length)).reshape(-1)
    mask = jnp.concatenate([jnp.broadcast_to(prev_ok[None, :], (BLK, BLK)), own_ok, jnp.broadcast_to(glob_ok[None, :], (BLK, GLOB * BLK))], axis=1)
    return mask.astype(jnp.float32)

def split_heads(rows):
    return rows.reshape(rows.shape[0], HEADS, HEAD_DIM)

def attend_forward(q_blk, keys, mask):
    width = q_blk.shape[1]
    heads = split_heads(q_blk)
    kk = split_heads(keys[:, :width])
    vv = split_heads(keys[:, width:])
    scores = product('qhd,khd->hqk', heads, kk) * HEAD_DIM ** (-0.5)
    probs = (jax.nn.silu(scores) * mask[None]).astype(jnp.bfloat16)
    return product('hqk,khd->qhd', probs, vv).reshape(q_blk.shape[0], width)

def attend_backward(q_blk, keys, mask, grad_out):
    width = q_blk.shape[1]
    scale = HEAD_DIM ** (-0.5)
    heads = split_heads(q_blk)
    kk = split_heads(keys[:, :width])
    vv = split_heads(keys[:, width:])
    grads = split_heads(grad_out)
    scores = product('qhd,khd->hqk', heads, kk) * scale
    probs = (jax.nn.silu(scores) * mask[None]).astype(jnp.bfloat16)
    d_probs = product('qhd,khd->hqk', grads, vv)
    d_val = product('hqk,qhd->khd', probs, grads)
    sig = jax.nn.sigmoid(scores)
    d_scores = (d_probs * sig * (1.0 + scores * (1.0 - sig)) * mask[None] * scale).astype(jnp.bfloat16)
    d_q = product('hqk,khd->qhd', d_scores, kk)
    d_k = product('hqk,qhd->khd', d_scores, heads)
    count = keys.shape[0]
    return (d_q.reshape(q_blk.shape[0], width), jnp.concatenate([d_k.reshape(count, width), d_val.reshape(count, width)], axis=1))

def middle(attn, gate, history, w_out, emb, valid):
    mean = lax.optimization_barrier(jnp.mean(attn, axis=1, keepdims=True))
    centered = attn - mean
    var = lax.optimization_barrier(jnp.mean(centered * centered, axis=1, keepdims=True))
    inv = lax.rsqrt(var + 1e-05)
    normed = centered * inv
    gate_f = gate.astype(jnp.float32)
    gated = (normed * gate_f).astype(jnp.bfloat16)
    user_vec = product('rd,de->re', gated, w_out) + history.astype(jnp.float32)
    score = product('re,rje->rj', user_vec, emb)
    side = jax.nn.sigmoid(score[:, 1:] - score[:, :1]) * valid[:, None]
    coef = jnp.concatenate([-lax.optimization_barrier(jnp.sum(side, axis=1, keepdims=True)), side], axis=1)
    d_user = product('rj,rje->re', coef, emb).astype(jnp.bfloat16)
    d_emb = coef[:, :, None] * user_vec[:, None, :]
    d_gated = product('re,de->rd', d_user, w_out)
    d_gate = (d_gated * normed).astype(jnp.bfloat16)
    dn = d_gated * gate_f
    d_attn = (dn - lax.optimization_barrier(jnp.mean(dn, axis=1, keepdims=True)) - normed * lax.optimization_barrier(jnp.mean(dn * normed, axis=1, keepdims=True))) * inv
    return (d_attn.astype(jnp.bfloat16), d_gate, d_emb)

def reference(query, key, value, gate, history, w_out, table, item_owner, item_row, global_blocks, lengths):
    nblocks = SEQ_LEN // BLK
    blocks = jnp.arange(nblocks, dtype=jnp.int32)

    def per_user(table_grad, inputs):
        q_all, k_all, v_all, gate_all, hist, owner, row, gids, length = inputs
        width = q_all.shape[1]
        kv = jnp.concatenate([k_all, v_all], axis=1)

        def starts_of(b):
            starts = [jnp.maximum(b - 1, 0) * BLK, b * BLK]
            for index in range(GLOB):
                starts.append(gids[index] * BLK)
            return [s.astype(jnp.int32) for s in starts]

        def keys_of(b):
            return jnp.concatenate([lax.dynamic_slice_in_dim(kv, s, BLK, 0) for s in starts_of(b)], axis=0)

        def forward(b):
            q_blk = lax.dynamic_slice_in_dim(q_all, (b * BLK).astype(jnp.int32), BLK, 0)
            return attend_forward(q_blk, keys_of(b), key_mask(b, gids, length))
        attn = lax.map(forward, blocks).reshape(SEQ_LEN, width)
        ids = (owner * ROWS_DEV + row).astype(jnp.int32)
        emb = table[ids]
        valid = (jnp.arange(SEQ_LEN, dtype=jnp.int32) < length).astype(jnp.float32)
        d_attn, d_gate, d_emb = middle(attn, gate_all, hist, w_out, emb, valid)

        def backward(dkv, b):
            start = (b * BLK).astype(jnp.int32)
            q_blk = lax.dynamic_slice_in_dim(q_all, start, BLK, 0)
            grad_blk = lax.dynamic_slice_in_dim(d_attn, start, BLK, 0)
            d_q, d_keys = attend_backward(q_blk, keys_of(b), key_mask(b, gids, length), grad_blk)
            for index, place in enumerate(starts_of(b)):
                current = lax.dynamic_slice_in_dim(dkv, place, BLK, 0)
                dkv = lax.dynamic_update_slice_in_dim(dkv, current + d_keys[index * BLK:(index + 1) * BLK], place, 0)
            return (dkv, d_q.astype(jnp.bfloat16))
        dkv, d_q = lax.scan(backward, jnp.zeros((SEQ_LEN, 2 * width), jnp.float32), blocks)
        table_grad = table_grad.at[ids.reshape(-1)].add(d_emb.reshape(-1, E))
        outputs = (d_q.reshape(SEQ_LEN, width), dkv[:, :width].astype(jnp.bfloat16), dkv[:, width:].astype(jnp.bfloat16), d_gate)
        return (table_grad, outputs)
    start_grad = jnp.zeros((NITEMS, E), jnp.float32)
    table_grad, (d_query, d_key, d_value, d_gate) = lax.scan(per_user, start_grad, (query, key, value, gate, history, item_owner, item_row, global_blocks, lengths))
    return (d_query, d_key, d_value, d_gate, table_grad)
```

```python
import functools

import jax
import jax.numpy as jnp
from jax import lax
from jax.experimental import pallas as pl
from jax.experimental.pallas import tpu as pltpu
from jax.sharding import PartitionSpec as P

HEADS = 8
HEAD_DIM = 64
D = 512
E = 128
BLK = 128
GLOB = 2
ITEMS = 5
EVENTS = 512
NBD = EVENTS // BLK
PAIRS = HEADS // 2
NDEV = 128
NSEQ = 16
ROWS = 4096
SLOTS = 32
HI = 4
LO = ROWS // HI
BF = jnp.bfloat16
F32 = jnp.float32
VMEM_LIMIT = 56 * 1024 * 1024
SMEM_SPEC = pl.BlockSpec(memory_space=pltpu.SMEM)


def dot(a, b):
    return jnp.dot(a, b, preferred_element_type=F32)


def dot_nt(a, b):
    return lax.dot_general(a, b, (((1,), (1,)), ((), ())), preferred_element_type=F32)


def dot_tn(a, b):
    return lax.dot_general(a, b, (((0,), (0,)), ((), ())), preferred_element_type=F32)


def params(**more):
    return pltpu.CompilerParams(vmem_limit_bytes=VMEM_LIMIT, **more)


def whole(shape):
    return pl.BlockSpec(shape, lambda *_: (0,) * len(shape))


def iota(shape, dim):
    return lax.broadcasted_iota(jnp.int32, shape, dim)


def route_kernel(meta, owner, row, key, value, req, rank_out, pos_out, halo, cand):
    halo[0] = key[EVENTS - BLK :, :]
    halo[1] = value[EVENTS - BLK :, :]
    for g in range(GLOB):
        start = pl.multiple_of((meta[2 + g] % NBD) * BLK, BLK)
        cand[0, g * BLK : (g + 1) * BLK, :] = key[pl.ds(start, BLK), :]
        cand[1, g * BLK : (g + 1) * BLK, :] = value[pl.ds(start, BLK), :]
    dev = iota((NDEV, EVENTS), 0)
    rows = jnp.full((NDEV, EVENTS), -1, jnp.int32)
    for j in range(ITEMS):
        rows = jnp.where(owner[j] == dev, row[j], rows)
    hit = rows >= 0
    before = jnp.where(iota((EVENTS, EVENTS), 0) < iota((EVENTS, EVENTS), 1), 1.0, 0.0).astype(BF)
    rank = dot(jnp.where(hit, 1.0, 0.0).astype(BF), before)
    rank = jnp.where(hit, rank, -1.0)
    rank_out[...] = rank
    pos_out[...] = jnp.where(owner[0] == dev, 1.0, 0.0)
    plus = (rows + 1).astype(F32)
    lane = iota((NDEV, SLOTS), 1)
    asked = jnp.zeros((NDEV, SLOTS), F32)
    for k in range(SLOTS):
        column = jnp.sum(jnp.where(rank == k, plus, 0.0), axis=1, keepdims=True)
        asked = jnp.where(lane == k, column, asked)
    req[...] = asked.astype(jnp.int32) - 1


def route(meta, owner, row, key, value):
    return pl.pallas_call(
        route_kernel,
        out_shape=(
            jax.ShapeDtypeStruct((NDEV, SLOTS), jnp.int32),
            jax.ShapeDtypeStruct((NDEV, EVENTS), F32),
            jax.ShapeDtypeStruct((NDEV, EVENTS), F32),
            jax.ShapeDtypeStruct((2, BLK, D), BF),
            jax.ShapeDtypeStruct((2, GLOB * BLK, D), BF),
        ),
        in_specs=[SMEM_SPEC] + [pl.BlockSpec(memory_space=pltpu.VMEM)] * 4,
        out_specs=[pl.BlockSpec(memory_space=pltpu.VMEM)] * 5,
        compiler_params=params(),
        cost_estimate=pl.CostEstimate(flops=10**8, bytes_accessed=3 * 10**6, transcendentals=0),
        name="route",
    )(meta, owner, row, key, value)


def gather_kernel(asked, table, found):
    lo = asked[...] & (LO - 1)
    hi = asked[...] >> (LO.bit_length() - 1)
    wide = jnp.concatenate([table[h * LO : (h + 1) * LO, :] for h in range(HI)], axis=1)
    group = 16
    size = group * SLOTS
    lane = iota((size, E), 1)

    def spread(x, first):
        return jnp.concatenate(
            [jnp.broadcast_to(x[:, s : s + 1], (SLOTS, E)) for s in range(first, first + group)],
            axis=0,
        )

    for first in range(0, NDEV, group):
        low = spread(lo, first)
        high = spread(hi, first)
        onehot = jnp.concatenate(
            [jnp.where(low == lane + b * E, 1.0, 0.0).astype(BF) for b in range(LO // E)], axis=1
        )
        picked = dot(onehot, wide)
        out = jnp.zeros((size, E), F32)
        for h in range(HI):
            out = jnp.where(high == h, picked[:, h * E : (h + 1) * E], out)
        found[first * SLOTS : first * SLOTS + size, :] = out.astype(BF)


def gather(asked, table):
    return pl.pallas_call(
        gather_kernel,
        out_shape=jax.ShapeDtypeStruct((NDEV * SLOTS, E), BF),
        in_specs=[pl.BlockSpec(memory_space=pltpu.VMEM)] * 2,
        out_specs=pl.BlockSpec(memory_space=pltpu.VMEM),
        compiler_params=params(),
        cost_estimate=pl.CostEstimate(
            flops=2 * NDEV * SLOTS * ROWS * E, bytes_accessed=2 * 10**6, transcendentals=0
        ),
        name="gather_rows",
    )(asked, table)


def scatter_kernel(asked, slots, incoming, grad, spread):
    step = pl.program_id(0)
    shift = LO.bit_length() - 1

    @pl.when(step == 0)
    def _():
        hi = asked[...] >> shift
        group = 8
        size = group * SLOTS
        for first in range(0, NDEV, group):
            high = jnp.concatenate(
                [jnp.broadcast_to(hi[:, s : s + 1], (SLOTS, E)) for s in range(first, first + group)],
                axis=0,
            )
            part = incoming[first * SLOTS : first * SLOTS + size, :].astype(F32)
            for h in range(HI):
                spread[first * SLOTS : first * SLOTS + size, h * E : (h + 1) * E] = jnp.where(
                    high == h, part, 0.0
                ).astype(BF)

    size = LO // 4
    sub = iota((size, E), 0) + step * size
    lo = slots[...] & (LO - 1)
    onehot = jnp.concatenate(
        [
            jnp.where(sub == lo[i : i + 1, :], 1.0, 0.0).astype(BF)
            for i in range(NDEV * SLOTS // E)
        ],
        axis=1,
    )
    total = dot(onehot, spread[...])
    for h in range(HI):
        grad[h] = total[:, h * E : (h + 1) * E]


def scatter(asked, slots, incoming):
    count = NDEV * SLOTS
    return pl.pallas_call(
        scatter_kernel,
        grid=(4,),
        out_shape=jax.ShapeDtypeStruct((HI, LO, E), F32),
        in_specs=[whole((SLOTS, NDEV)), whole((count // E, E)), whole((count, E))],
        out_specs=pl.BlockSpec((HI, LO // 4, E), lambda i: (0, i, 0)),
        scratch_shapes=[pltpu.VMEM((count, HI * E), BF)],
        compiler_params=params(),
        cost_estimate=pl.CostEstimate(
            flops=2 * count * ROWS * E, bytes_accessed=3 * 10**6, transcendentals=0
        ),
        name="scatter_rows",
    )(asked, slots, incoming)


def head_masks():
    lane = iota((1, 2 * HEAD_DIM), 1)
    return [
        jnp.where(lane < HEAD_DIM, 1.0, 0.0).astype(BF),
        jnp.where(lane >= HEAD_DIM, 1.0, 0.0).astype(BF),
    ]


def forward_kernel(
    meta, q, k, v, halo, glob, gate, history, w_out, probs, slope, normed_out, inv_out, user, attn
):
    pair = pl.program_id(0)
    base, length = meta[0], meta[1]
    masks = head_masks()
    q16 = q[...] * jnp.asarray(1.0 / 16.0, BF)
    kx = jnp.concatenate([halo[0], k[...]], axis=0)
    vx = jnp.concatenate([halo[1], v[...]], axis=0)
    kg, vg = glob[0], glob[1]
    lane = iota((BLK, 2 * BLK), 1)
    sub = iota((BLK, 2 * BLK), 0)
    gid = jnp.where(lane < BLK, meta[2], meta[3])
    glob_pos = gid * BLK + lane % BLK
    near, far = [], []
    for i in range(NBD):
        pos = (base + i - 1) * BLK + lane
        near.append((pos >= 0) & (pos < length) & (lane <= sub + BLK))
        far.append((gid < base + i - 1) & (glob_pos < length))
    vx_m = [vx * m for m in masks]
    vg_both = jnp.concatenate([vg * m for m in masks], axis=0)

    def act(u, mask):
        w = jnp.where(mask, 1.0 + jnp.tanh(u), 0.0)
        p = u * w
        return p.astype(BF), (w + p * (2.0 - w)).astype(BF)

    for i in range(NBD):
        rows = slice(i * BLK, (i + 1) * BLK)
        keys = slice(i * BLK, (i + 2) * BLK)
        near_p, far_p = [], []
        for h in range(2):
            qm = q16[rows] * masks[h]
            p, f = act(dot_nt(qm, kx[keys]), near[i])
            probs[h, rows, : 2 * BLK] = p
            slope[h, rows, : 2 * BLK] = f
            near_p.append(p)
            p, f = act(dot_nt(qm, kg), far[i])
            probs[h, rows, 2 * BLK :] = p
            slope[h, rows, 2 * BLK :] = f
            far_p.append(p)
        near_v = jnp.concatenate([m[keys] for m in vx_m], axis=0)
        attn[pair, rows, :] = dot(jnp.concatenate(near_p, axis=1), near_v) + dot(
            jnp.concatenate(far_p, axis=1), vg_both
        )

    @pl.when(pair == PAIRS - 1)
    def _():
        step = 128
        for r in range(0, EVENTS, step):
            rows = slice(r, r + step)
            x = jnp.concatenate([attn[p, rows, :] for p in range(PAIRS)], axis=1)
            centered = x - jnp.mean(x, axis=1, keepdims=True)
            var = jnp.mean(centered * centered, axis=1, keepdims=True)
            inv = lax.rsqrt(var + 1e-05)
            normed = centered * inv
            normed_out[rows, :] = normed
            inv_out[rows, :] = inv
            gated = (normed * gate[rows, :].astype(F32)).astype(BF)
            user[rows, :] = dot(gated, w_out[...]) + history[rows, :].astype(F32)


def pair_block(rows):
    return pl.BlockSpec((rows, 2 * HEAD_DIM), lambda p: (0, p))


def pair_stack(rows):
    return pl.BlockSpec((2, rows, 2 * HEAD_DIM), lambda p: (0, 0, p))


def head_block():
    return pl.BlockSpec((2, EVENTS, (2 + GLOB) * BLK), lambda p: (p, 0, 0))


def forward(meta, q, k, v, halo, glob, gate, history, w_out):
    square = (HEADS, EVENTS, (2 + GLOB) * BLK)
    return pl.pallas_call(
        forward_kernel,
        grid=(PAIRS,),
        out_shape=(
            jax.ShapeDtypeStruct(square, BF),
            jax.ShapeDtypeStruct(square, BF),
            jax.ShapeDtypeStruct((EVENTS, D), F32),
            jax.ShapeDtypeStruct((EVENTS, 1), F32),
            jax.ShapeDtypeStruct((EVENTS, E), F32),
        ),
        in_specs=[SMEM_SPEC]
        + [pair_block(EVENTS)] * 3
        + [pair_stack(BLK), pair_stack(GLOB * BLK)]
        + [whole((EVENTS, D)), whole((EVENTS, E)), whole((D, E))],
        out_specs=[
            head_block(),
            head_block(),
            whole((EVENTS, D)),
            whole((EVENTS, 1)),
            whole((EVENTS, E)),
        ],
        scratch_shapes=[pltpu.VMEM((PAIRS, EVENTS, 2 * HEAD_DIM), F32)],
        compiler_params=params(),
        cost_estimate=pl.CostEstimate(
            flops=10**9, bytes_accessed=13 * 10**6, transcendentals=2 * 10**6
        ),
        name="attend_forward",
    )(meta, q, k, v, halo, glob, gate, history, w_out)


def backward_kernel(q, k, v, halo, glob, grad, probs, slope, d_q, d_k, d_v, edge, d_glob):
    masks = head_masks()
    sixteenth = jnp.asarray(1.0 / 16.0, BF)
    q16 = q[...] * sixteenth
    kx = jnp.concatenate([halo[0], k[...]], axis=0)
    vx = jnp.concatenate([halo[1], v[...]], axis=0)
    kg, vg = glob[0], glob[1]
    do = grad[...]
    q_t = [(q16 * m).T for m in masks]
    do_t = [(do * m).T for m in masks]
    kx_m = [kx * (m * sixteenth) for m in masks]
    kg_both = jnp.concatenate([kg * (m * sixteenth) for m in masks], axis=0)
    far_ds = [[], []]
    carry = None
    for i in range(NBD):
        rows = slice(i * BLK, (i + 1) * BLK)
        keys = slice(i * BLK, (i + 2) * BLK)
        near_ds, far_i = [], []
        for h in range(2):
            dom = do[rows] * masks[h]
            ds = dot_nt(dom, vx[keys]) * slope[h, rows, : 2 * BLK].astype(F32)
            near_ds.append(ds.astype(BF))
            ds = dot_nt(dom, vg) * slope[h, rows, 2 * BLK :].astype(F32)
            far_i.append(ds.astype(BF))
            far_ds[h].append(far_i[-1])
        near_k = jnp.concatenate([m[keys] for m in kx_m], axis=0)
        d_q[rows, :] = (
            dot(jnp.concatenate(near_ds, axis=1), near_k)
            + dot(jnp.concatenate(far_i, axis=1), kg_both)
        ).astype(BF)
        near_p = jnp.concatenate([probs[h, rows, : 2 * BLK] for h in range(2)], axis=0)
        dk = dot(
            jnp.concatenate([t[:, rows] for t in q_t], axis=1), jnp.concatenate(near_ds, axis=0)
        ).T
        dv = dot(jnp.concatenate([t[:, rows] for t in do_t], axis=1), near_p).T
        if i == 0:
            edge[0] = dk[:BLK].astype(BF)
            edge[1] = dv[:BLK].astype(BF)
        else:
            last = slice((i - 1) * BLK, i * BLK)
            d_k[last, :] = (carry[0] + dk[:BLK]).astype(BF)
            d_v[last, :] = (carry[1] + dv[:BLK]).astype(BF)
        carry = (dk[BLK:], dv[BLK:])
    last = slice((NBD - 1) * BLK, NBD * BLK)
    d_k[last, :] = carry[0].astype(BF)
    d_v[last, :] = carry[1].astype(BF)
    far_ds = jnp.concatenate(far_ds[0] + far_ds[1], axis=0)
    far_p = jnp.concatenate([probs[h, :, 2 * BLK :] for h in range(2)], axis=0)
    d_glob[0] = dot(jnp.concatenate(q_t, axis=1), far_ds).T.astype(BF)
    d_glob[1] = dot(jnp.concatenate(do_t, axis=1), far_p).T.astype(BF)


def backward(q, k, v, halo, glob, grad, probs, slope):
    rows = jax.ShapeDtypeStruct((EVENTS, D), BF)
    return pl.pallas_call(
        backward_kernel,
        grid=(PAIRS,),
        out_shape=(
            rows,
            rows,
            rows,
            jax.ShapeDtypeStruct((2, BLK, D), BF),
            jax.ShapeDtypeStruct((2, GLOB * BLK, D), BF),
        ),
        in_specs=[pair_block(EVENTS)] * 3
        + [pair_stack(BLK), pair_stack(GLOB * BLK), pair_block(EVENTS)]
        + [head_block()] * 2,
        out_specs=[pair_block(EVENTS)] * 3 + [pair_stack(BLK), pair_stack(GLOB * BLK)],
        compiler_params=params(),
        cost_estimate=pl.CostEstimate(
            flops=2 * 10**9, bytes_accessed=13 * 10**6, transcendentals=0
        ),
        name="attend_backward",
    )(q, k, v, halo, glob, grad, probs, slope)


def middle_kernel(
    meta, items, rank, pos, user, normed, inv, gate, w_out, outgoing, d_attn, d_gate, score
):
    user_b = user[...].astype(BF)
    user_t = user[...].T.astype(BF)
    group = 8
    size = group * SLOTS
    slot = iota((SLOTS, EVENTS), 0).astype(F32)
    for d in range(0, NDEV, group):
        s = dot(items[d * SLOTS : d * SLOTS + size, :], user_t)
        for r in range(group):
            own = rank[d + r : d + r + 1, :] == slot
            part = jnp.where(own, s[r * SLOTS : (r + 1) * SLOTS, :], 0.0)
            score[d + r : d + r + 1, :] = jnp.sum(part, axis=0, keepdims=True)
    first = pos[...]
    score0 = jnp.sum(first * score[...], axis=0, keepdims=True)
    event = meta[0] * BLK + iota((1, EVENTS), 1)
    valid = jnp.where(event < meta[1], 1.0, 0.0)
    other = (rank[...] >= 0.0) & (first == 0.0)
    side = jnp.where(other, jax.nn.sigmoid(score[...] - score0), 0.0) * valid
    coef = side - first * jnp.sum(side, axis=0, keepdims=True)
    score[...] = coef
    d_user_t = jnp.zeros((E, EVENTS), F32)
    for d in range(0, NDEV, group):
        c = jnp.concatenate(
            [
                jnp.where(rank[r : r + 1, :] == slot, score[r : r + 1, :], 0.0).astype(BF)
                for r in range(d, d + group)
            ],
            axis=0,
        )
        rows = slice(d * SLOTS, d * SLOTS + size)
        outgoing[rows, :] = dot(c, user_b).astype(BF)
        d_user_t = d_user_t + dot_tn(items[rows, :], c)
    d_user = d_user_t.T.astype(BF)
    step = 128
    for r in range(0, EVENTS, step):
        rows = slice(r, r + step)
        d_gated = dot_nt(d_user[rows], w_out[...])
        n = normed[rows, :]
        d_gate[rows, :] = (d_gated * n).astype(BF)
        dn = d_gated * gate[rows, :].astype(F32)
        d_attn[rows, :] = (
            (
                dn
                - jnp.mean(dn, axis=1, keepdims=True)
                - n * jnp.mean(dn * n, axis=1, keepdims=True)
            )
            * inv[rows, :]
        ).astype(BF)


def middle(meta, items, rank, pos, user, normed, inv, gate, w_out):
    return pl.pallas_call(
        middle_kernel,
        out_shape=(
            jax.ShapeDtypeStruct((NDEV * SLOTS, E), BF),
            jax.ShapeDtypeStruct((EVENTS, D), BF),
            jax.ShapeDtypeStruct((EVENTS, D), BF),
        ),
        in_specs=[SMEM_SPEC] + [pl.BlockSpec(memory_space=pltpu.VMEM)] * 8,
        out_specs=[pl.BlockSpec(memory_space=pltpu.VMEM)] * 3,
        scratch_shapes=[pltpu.VMEM((NDEV, EVENTS), F32)],
        compiler_params=params(),
        cost_estimate=pl.CostEstimate(
            flops=2 * 10**9, bytes_accessed=6 * 10**6, transcendentals=10**5
        ),
        name="ranking",
    )(meta, items, rank, pos, user, normed, inv, gate, w_out)


def finish_kernel(meta, d_k, d_v, edge, total, key_out, value_out):
    for which, (mine, out) in enumerate(((d_k, key_out), (d_v, value_out))):
        out[...] = mine[...]
        tail = slice(EVENTS - BLK, EVENTS)
        out[tail, :] = (mine[tail, :].astype(F32) + edge[which].astype(F32)).astype(BF)
        for g in range(GLOB):

            @pl.when(meta[2 + g] // NBD == meta[4])
            def _():
                place = pl.ds(pl.multiple_of((meta[2 + g] % NBD) * BLK, BLK), BLK)
                more = total[which, g * BLK : (g + 1) * BLK, :].astype(F32)
                out[place, :] = (out[place, :].astype(F32) + more).astype(BF)


def finish(meta, d_k, d_v, edge, total):
    rows = jax.ShapeDtypeStruct((EVENTS, D), BF)
    return pl.pallas_call(
        finish_kernel,
        out_shape=(rows, rows),
        in_specs=[SMEM_SPEC] + [pl.BlockSpec(memory_space=pltpu.VMEM)] * 4,
        out_specs=[pl.BlockSpec(memory_space=pltpu.VMEM)] * 2,
        compiler_params=params(),
        cost_estimate=pl.CostEstimate(flops=10**6, bytes_accessed=3 * 10**6, transcendentals=0),
        name="add_received",
    )(meta, d_k, d_v, edge, total)


def from_behind(block, axis, distance):
    devices = range(lax.axis_size(axis))
    route_pairs = [(i - distance, i) for i in devices if i - distance in devices]
    return lax.ppermute(block, axis, route_pairs)


def exchange(x, axis):
    return lax.all_to_all(x, axis, split_axis=0, concat_axis=0, tiled=True)


def on_device(
    query, key, value, gate, history, w_out, table, item_owner, item_row, global_blocks, lengths
):
    seq = lax.axis_index("seq")
    user_idx = lax.axis_index("user")
    length = lax.dynamic_slice_in_dim(lengths, user_idx, 1)
    gids = global_blocks[0]
    meta = jnp.concatenate([(seq * NBD).reshape(1), length, gids, seq.reshape(1)]).astype(jnp.int32)
    q, k, v = query[0], key[0], value[0]
    owner = item_owner[0].T.reshape(ITEMS, 1, EVENTS)
    row = item_row[0].T.reshape(ITEMS, 1, EVENTS)
    req, rank, pos, tail, cand = route(meta, owner, row, k, v)
    asked = exchange(req.reshape(NDEV, 1, SLOTS), ("seq", "user")).reshape(NDEV, SLOTS)
    halo = from_behind(tail, "seq", 1)
    pieces = exchange(cand.reshape(NSEQ, 2 * GLOB * BLK // NSEQ, D), "seq")
    holder = gids[(seq % (NSEQ // 2)) // (NSEQ // 4)] // NBD
    piece = lax.dynamic_index_in_dim(pieces, holder, 0, keepdims=True)
    glob = exchange(jnp.broadcast_to(piece, pieces.shape), "seq").reshape(2, GLOB * BLK, D)
    asked_t = asked.T
    found = gather(asked_t, table)
    items = exchange(found.reshape(NDEV, SLOTS, E), ("seq", "user")).reshape(NDEV * SLOTS, E)
    probs, slope, normed, inv, user = forward(meta, q, k, v, halo, glob, gate[0], history[0], w_out)
    outgoing, d_attn, d_gate = middle(meta, items, rank, pos, user, normed, inv, gate[0], w_out)
    incoming = exchange(outgoing.reshape(NDEV, SLOTS, E), ("seq", "user"))
    d_q, d_k, d_v, edge, d_glob = backward(q, k, v, halo, glob, d_attn, probs, slope)
    parts = exchange(d_glob.reshape(NSEQ, 2 * GLOB * BLK // NSEQ, D), "seq")
    part = jnp.sum(parts.astype(F32), axis=0, keepdims=True).astype(BF)
    total = exchange(jnp.broadcast_to(part, parts.shape), "seq").reshape(2, GLOB * BLK, D)
    back = from_behind(edge, "seq", -1)
    grad = scatter(asked_t, asked.reshape(NDEV * SLOTS // E, E), incoming.reshape(NDEV * SLOTS, E))
    d_key, d_value = finish(meta, d_k, d_v, back, total)
    return (d_q[None], d_key[None], d_value[None], d_gate[None], grad.reshape(ROWS, E))


def solution(mesh):
    return jax.shard_map(
        on_device,
        mesh=mesh,
        in_specs=(
            P("user", "seq", None),
            P("user", "seq", None),
            P("user", "seq", None),
            P("user", "seq", None),
            P("user", "seq", None),
            P(),
            P(("seq", "user"), None),
            P("user", "seq", None),
            P("user", "seq", None),
            P("user", None),
            P(),
        ),
        out_specs=(
            P("user", "seq", None),
            P("user", "seq", None),
            P("user", "seq", None),
            P("user", "seq", None),
            P(("seq", "user"), None),
        ),
        check_vma=False,
    )
```

```python
import functools

import jax
import jax.numpy as jnp
from jax import lax
from jax.experimental import pallas as pl
from jax.experimental.pallas import tpu as pltpu
from jax.sharding import PartitionSpec as P

HEADS = 8
HEAD_DIM = 64
D = 512
E = 128
BLK = 128
GLOB = 2
ITEMS = 5
EVENTS = 512
NBD = EVENTS // BLK
PAIRS = HEADS // 2
NDEV = 128
NSEQ = 16
CHUNKS = 2 * GLOB
ROWS = 4096
SLOTS = 32
FIRST = 64.0
HI = 4
LO = ROWS // HI
BF = jnp.bfloat16
F32 = jnp.float32
VMEM_LIMIT = 24 * 1024 * 1024
SMEM_SPEC = pl.BlockSpec(memory_space=pltpu.SMEM)
VMEM_SPEC = pl.BlockSpec(memory_space=pltpu.VMEM)
ANY_SPEC = pl.BlockSpec(memory_space=pl.ANY)
XSIZE = 4


def dot(a, b):
    return jnp.dot(a, b, preferred_element_type=F32)


def dot_nt(a, b):
    return lax.dot_general(a, b, (((1,), (1,)), ((), ())), preferred_element_type=F32)


def dot_tn(a, b):
    return lax.dot_general(a, b, (((0,), (0,)), ((), ())), preferred_element_type=F32)


def params(**more):
    return pltpu.CompilerParams(vmem_limit_bytes=VMEM_LIMIT, **more)


def fast(shape, dtype):
    return pltpu.VMEM(shape, dtype)


def slow(shape, dtype):
    return pltpu.HBM(shape, dtype)


def in_vmem(*arrays):
    return [pltpu.with_memory_space_constraint(x, pltpu.VMEM) for x in arrays]


def in_hbm(*arrays):
    return [pltpu.with_memory_space_constraint(x, pltpu.HBM) for x in arrays]


def whole(shape):
    return pl.BlockSpec(shape, lambda *_: (0,) * len(shape))


def iota(shape, dim):
    return lax.broadcasted_iota(jnp.int32, shape, dim)


def chunk_of(shift):
    return (lax.axis_index("seq") + shift) % XSIZE


def pieces_kernel(gids, key, value, halo, cand0, cand1, cand2, cand3, sems):
    seq = lax.axis_index("seq")
    tail = pl.ds(EVENTS - BLK, BLK)
    tails = [
        pltpu.make_async_copy(src.at[tail, :], halo.at[i], sems.at[CHUNKS + i])
        for i, src in enumerate((key, value))
    ]
    for copy in tails:
        copy.start()
    cases = []
    for d, out in enumerate((cand0, cand1, cand2, cand3)):
        c = chunk_of(d)
        gid = gids[0, c % GLOB]
        place = pl.ds(pl.multiple_of((gid % NBD) * BLK, BLK), BLK)
        held = gid // NBD == seq
        for i, src in enumerate((key, value)):
            copy = pltpu.make_async_copy(src.at[place, :], out, sems.at[d])
            cases.append((held & (c // GLOB == i), copy))

        @pl.when(jnp.logical_not(held))
        def _():
            out[...] = jnp.zeros((BLK, D), BF)

    for case, copy in cases:

        @pl.when(case)
        def _():
            copy.start()

    for case, copy in cases:

        @pl.when(case)
        def _():
            copy.wait()

    for copy in tails:
        copy.wait()


def pieces(gids, key, value):
    return pl.pallas_call(
        pieces_kernel,
        out_shape=(jax.ShapeDtypeStruct((2, BLK, D), BF),)
        + (jax.ShapeDtypeStruct((BLK, D), BF),) * CHUNKS,
        in_specs=[SMEM_SPEC] + [ANY_SPEC] * 2,
        out_specs=[VMEM_SPEC] * (1 + CHUNKS),
        scratch_shapes=[pltpu.SemaphoreType.DMA((CHUNKS + 2,))],
        compiler_params=params(),
        cost_estimate=pl.CostEstimate(flops=10**6, bytes_accessed=2 * 10**6, transcendentals=0),
        name="pieces",
    )(gids, *in_hbm(key, value))


def route_kernel(owner, row, req, code):
    dev = iota((NDEV, EVENTS), 0)
    rows = jnp.full((NDEV, EVENTS), -1, jnp.int32)
    for j in range(ITEMS):
        rows = jnp.where(owner[j] == dev, row[j], rows)
    hit = rows >= 0
    before = jnp.where(iota((EVENTS, EVENTS), 0) < iota((EVENTS, EVENTS), 1), 1.0, 0.0).astype(BF)
    rank = dot(jnp.where(hit, 1.0, 0.0).astype(BF), before)
    rank = jnp.where(hit, rank, -1.0)
    code[...] = jnp.where(owner[0] == dev, rank + FIRST, rank)
    plus = (rows + 1).astype(F32)
    lane = iota((NDEV, E), 1) - (lax.axis_index("user") % (E // SLOTS)) * SLOTS
    asked = jnp.zeros((NDEV, E), F32)
    for k in range(SLOTS):
        column = jnp.sum(jnp.where(rank == k, plus, 0.0), axis=1, keepdims=True)
        asked = jnp.where(lane == k, column, asked)
    req[...] = asked.astype(jnp.int32)


def route(owner, row):
    return pl.pallas_call(
        route_kernel,
        out_shape=(
            slow((NDEV, E), jnp.int32),
            slow((NDEV, EVENTS), F32),
        ),
        in_specs=[VMEM_SPEC] * 2,
        out_specs=[VMEM_SPEC] * 2,
        compiler_params=params(),
        cost_estimate=pl.CostEstimate(flops=10**8, bytes_accessed=10**6, transcendentals=0),
        name="route",
    )(*in_hbm(owner, row))


def slot_rows(asked, count):
    rows = asked[pl.ds(0, count, stride=4), :]
    for j in range(1, 4):
        rows = rows + asked[pl.ds(j, count, stride=4), :]
    return rows - 1


def slot_columns(rows):
    count = rows.shape[0]
    full = jnp.concatenate([rows.astype(F32), jnp.zeros((E - count, E), F32)], axis=0)
    return full.T[:, :count].astype(jnp.int32)


def spread_columns(x, first, count):
    return jnp.concatenate(
        [jnp.broadcast_to(x[:, i : i + 1], (E, E)) for i in range(first, first + count)], axis=0
    )


def gather_kernel(asked, table_far, found_far, table, found, sems):
    slabs = [slice(h * LO, (h + 1) * LO) for h in range(HI)]
    loads = [
        pltpu.make_async_copy(table_far.at[slab, :], table.at[slab, :], sems.at[h])
        for h, slab in enumerate(slabs)
    ]
    for load in loads:
        load.start()
    columns = slot_columns(slot_rows(asked, NDEV // 4))
    lo = columns & (LO - 1)
    hi = columns >> (LO.bit_length() - 1)
    group = 8
    size = group * E
    lane = iota((size, E), 1)
    sends = []
    for step in range(NDEV // 4 // group):
        low = spread_columns(lo, step * group, group)
        high = spread_columns(hi, step * group, group)
        onehot = jnp.concatenate(
            [jnp.where(low == lane + b * E, 1.0, 0.0).astype(BF) for b in range(LO // E)], axis=1
        )
        if step == 0:
            for load in loads:
                load.wait()
        picked = dot(onehot, jnp.concatenate([table[slab, :] for slab in slabs], axis=1))
        out = jnp.zeros((size, E), F32)
        for h in range(HI):
            out = jnp.where(high == h, picked[:, h * E : (h + 1) * E], out)
        rows = slice(step * size, (step + 1) * size)
        found[rows, :] = out.astype(BF)
        sends.append(
            pltpu.make_async_copy(found.at[rows, :], found_far.at[rows, :], sems.at[HI + step])
        )
        sends[-1].start()
    for send in sends:
        send.wait()


def gather(asked, table):
    return pl.pallas_call(
        gather_kernel,
        out_shape=slow((NDEV * SLOTS, E), BF),
        in_specs=[VMEM_SPEC, ANY_SPEC],
        out_specs=ANY_SPEC,
        scratch_shapes=[
            pltpu.VMEM((ROWS, E), BF),
            pltpu.VMEM((NDEV * SLOTS, E), BF),
            pltpu.SemaphoreType.DMA((HI + 4,)),
        ],
        compiler_params=params(),
        cost_estimate=pl.CostEstimate(
            flops=2 * NDEV * SLOTS * ROWS * E, bytes_accessed=2 * 10**6, transcendentals=0
        ),
        name="gather_rows",
    )(asked, *in_hbm(table))


HALVES = 2


def scatter_kernel(half, asked, incoming, *refs):
    grad, spread = refs[-2:]
    rows = slot_rows(asked, NDEV // 4)
    hi = slot_columns(rows) >> (LO.bit_length() - 1)
    group = 2
    size = group * E
    for first in range(0, NDEV // 4, group):
        high = spread_columns(hi, first, group)
        part = incoming[first * E : first * E + size, :].astype(F32)
        for h in range(HI):
            spread[first * E : first * E + size, h * E : (h + 1) * E] = jnp.where(
                high == h, part, 0.0
            ).astype(BF)
    size = LO // HALVES
    sub = iota((size, E), 0) + half * size
    lo = rows & (LO - 1)
    onehot = jnp.concatenate(
        [jnp.where(sub == lo[i : i + 1, :], 1.0, 0.0).astype(BF) for i in range(NDEV // 4)], axis=1
    )
    total = dot(onehot, spread[...])
    for h in range(HI):
        grad[h] = total[:, h * E : (h + 1) * E]


def scatter(half, asked, incoming, before=()):
    count = NDEV * SLOTS
    return pl.pallas_call(
        functools.partial(scatter_kernel, half),
        grid=(1,),
        out_shape=slow((HI, LO, E), F32),
        in_specs=[whole((NDEV, E)), whole((count, E))] + [ANY_SPEC] * len(before),
        out_specs=pl.BlockSpec((HI, LO // HALVES, E), lambda i: (0, half, 0)),
        scratch_shapes=[pltpu.VMEM((count, HI * E), BF)],
        input_output_aliases={2 + i: i for i in range(len(before))},
        compiler_params=params(),
        cost_estimate=pl.CostEstimate(
            flops=count * ROWS * E, bytes_accessed=2 * 10**6, transcendentals=0
        ),
        name="scatter_rows",
    )(asked, incoming, *in_hbm(*before))


def head_masks():
    lane = iota((1, 2 * HEAD_DIM), 1)
    return [
        jnp.where(lane < HEAD_DIM, 1.0, 0.0).astype(BF),
        jnp.where(lane >= HEAD_DIM, 1.0, 0.0).astype(BF),
    ]


def act(u, mask):
    w = jnp.where(mask, 1.0 + jnp.tanh(u), 0.0)
    p = u * w
    return p.astype(BF), (w + p * (2.0 - w)).astype(BF)


def near_forward_kernel(lengths, q, k, v, halo, probs, slope, attn):
    base = lax.axis_index("seq") * NBD
    length = lengths[lax.axis_index("user")]
    masks = head_masks()
    q16 = q[...] * jnp.asarray(1.0 / 16.0, BF)
    kx = jnp.concatenate([halo[0], k[...]], axis=0)
    vx = jnp.concatenate([halo[1], v[...]], axis=0)
    lane = iota((BLK, 2 * BLK), 1)
    sub = iota((BLK, 2 * BLK), 0)
    vx_m = [vx * m for m in masks]
    both = [jnp.concatenate([q16[i * BLK : (i + 1) * BLK] * m for m in masks]) for i in range(NBD)]
    logits = [dot_nt(both[i], kx[i * BLK : (i + 2) * BLK]) for i in range(NBD)]
    held = []
    for i in range(NBD):
        rows = slice(i * BLK, (i + 1) * BLK)
        at = (base + i - 1) * BLK + lane
        mask = (at >= 0) & (at < length) & (lane <= sub + BLK)
        parts = []
        for h in range(2):
            p, f = act(logits[i][h * BLK : (h + 1) * BLK], mask)
            probs[h, rows, :] = p
            slope[h, rows, :] = f
            parts.append(p)
        held.append(jnp.concatenate(parts, axis=1))
    for i in range(NBD):
        keys = slice(i * BLK, (i + 2) * BLK)
        attn[i * BLK : (i + 1) * BLK, :] = dot(
            held[i], jnp.concatenate([m[keys] for m in vx_m], axis=0)
        )


def unrotate(parts, scratch):
    for d in range(CHUNKS):
        scratch[chunk_of(CHUNKS - d)] = parts[d][...]
    keys = jnp.concatenate([scratch[g] for g in range(GLOB)], axis=0)
    values = jnp.concatenate([scratch[GLOB + g] for g in range(GLOB)], axis=0)
    return keys, values


def far_forward_kernel(
    lengths,
    gids,
    q,
    glob0,
    glob1,
    glob2,
    glob3,
    near,
    gate,
    history,
    w_out,
    probs,
    slope,
    normed_out,
    inv_out,
    user,
    attn,
    scratch,
):
    pair = pl.program_id(0)
    base = lax.axis_index("seq") * NBD
    length = lengths[lax.axis_index("user")]
    masks = head_masks()
    q16 = q[...] * jnp.asarray(1.0 / 16.0, BF)
    kg, vg = unrotate((glob0, glob1, glob2, glob3), scratch)
    lane = iota((BLK, 2 * BLK), 1)
    gid = jnp.where(lane < BLK, gids[0, 0], gids[0, 1])
    at = gid * BLK + lane % BLK
    vg_both = jnp.concatenate([vg * m for m in masks], axis=0)
    logits = dot_nt(jnp.concatenate([q16 * m for m in masks], axis=0), kg)
    held = []
    for i in range(NBD):
        rows = slice(i * BLK, (i + 1) * BLK)
        mask = (gid < base + i - 1) & (at < length)
        parts = []
        for h in range(2):
            p, f = act(logits[h * EVENTS + i * BLK : h * EVENTS + (i + 1) * BLK], mask)
            probs[h, rows, :] = p
            slope[h, rows, :] = f
            parts.append(p)
        held.append(jnp.concatenate(parts, axis=1))
    attn[pair] = near[...] + dot(jnp.concatenate(held, axis=0), vg_both)

    @pl.when(pair == PAIRS - 1)
    def _():
        step = 128
        for r in range(0, EVENTS, step):
            rows = slice(r, r + step)
            x = jnp.concatenate([attn[p, rows, :] for p in range(PAIRS)], axis=1)
            centered = x - jnp.mean(x, axis=1, keepdims=True)
            var = jnp.mean(centered * centered, axis=1, keepdims=True)
            inv = lax.rsqrt(var + 1e-05)
            normed = centered * inv
            normed_out[rows, :] = normed
            inv_out[rows, :] = inv
            gated = (normed * gate[rows, :].astype(F32)).astype(BF)
            user[rows, :] = dot(gated, w_out[...]) + history[rows, :].astype(F32)


def pair_block(rows):
    return pl.BlockSpec((rows, 2 * HEAD_DIM), lambda p: (0, p))


def pair_stack(rows):
    return pl.BlockSpec((2, rows, 2 * HEAD_DIM), lambda p: (0, 0, p))


def head_block():
    return pl.BlockSpec((2, EVENTS, 2 * BLK), lambda p: (p, 0, 0))


SQUARE = slow((HEADS, EVENTS, 2 * BLK), BF)


def near_forward(lengths, q, k, v, halo):
    return pl.pallas_call(
        near_forward_kernel,
        grid=(PAIRS,),
        out_shape=(SQUARE, SQUARE, fast((EVENTS, D), F32)),
        in_specs=[SMEM_SPEC] + [pair_block(EVENTS)] * 3 + [pair_stack(BLK)],
        out_specs=[head_block(), head_block(), pair_block(EVENTS)],
        compiler_params=params(),
        cost_estimate=pl.CostEstimate(
            flops=5 * 10**8, bytes_accessed=7 * 10**6, transcendentals=10**6
        ),
        name="near_forward",
    )(lengths, q, k, v, halo)


def far_forward(lengths, gids, q, glob, near, gate, history, w_out):
    return pl.pallas_call(
        far_forward_kernel,
        grid=(PAIRS,),
        out_shape=(
            SQUARE,
            SQUARE,
            slow((EVENTS, D), F32),
            slow((EVENTS, 1), F32),
            slow((EVENTS, E), F32),
        ),
        in_specs=[SMEM_SPEC] * 2
        + [pair_block(EVENTS)]
        + [pair_block(BLK)] * CHUNKS
        + [pair_block(EVENTS)]
        + [whole((EVENTS, D)), whole((EVENTS, E)), whole((D, E))],
        out_specs=[
            head_block(),
            head_block(),
            whole((EVENTS, D)),
            whole((EVENTS, 1)),
            whole((EVENTS, E)),
        ],
        scratch_shapes=[
            pltpu.VMEM((PAIRS, EVENTS, 2 * HEAD_DIM), F32),
            pltpu.VMEM((CHUNKS, BLK, 2 * HEAD_DIM), BF),
        ],
        compiler_params=params(),
        cost_estimate=pl.CostEstimate(
            flops=6 * 10**8, bytes_accessed=9 * 10**6, transcendentals=10**6
        ),
        name="far_forward",
    )(lengths, gids, q, *glob, *in_vmem(near), gate, history, w_out)


def far_backward_kernel(
    q, glob0, glob1, glob2, glob3, grad, probs, slope, d_q, out0, out1, out2, out3, scratch
):
    masks = head_masks()
    sixteenth = jnp.asarray(1.0 / 16.0, BF)
    q16 = q[...] * sixteenth
    kg, vg = unrotate((glob0, glob1, glob2, glob3), scratch)
    do = grad[...]
    q_t = jnp.concatenate([(q16 * m).T for m in masks], axis=1)
    do_t = jnp.concatenate([(do * m).T for m in masks], axis=1)
    kg_both = jnp.concatenate([kg * (m * sixteenth) for m in masks], axis=0)
    d_probs = dot_nt(jnp.concatenate([do * m for m in masks], axis=0), vg)
    ds = [
        (d_probs[h * EVENTS : (h + 1) * EVENTS] * slope[h].astype(F32)).astype(BF) for h in range(2)
    ]
    d_q[...] = dot(jnp.concatenate(ds, axis=1), kg_both)
    d_k = dot(q_t, jnp.concatenate(ds, axis=0)).T.astype(BF)
    d_v = dot(do_t, jnp.concatenate([probs[0], probs[1]], axis=0)).T.astype(BF)
    for g in range(GLOB):
        scratch[g] = d_k[g * BLK : (g + 1) * BLK]
        scratch[GLOB + g] = d_v[g * BLK : (g + 1) * BLK]
    for d, out in enumerate((out0, out1, out2, out3)):
        out[...] = scratch[chunk_of(d)]


def far_backward(q, glob, grad, probs, slope):
    return pl.pallas_call(
        far_backward_kernel,
        grid=(PAIRS,),
        out_shape=(fast((EVENTS, D), F32),)
        + (jax.ShapeDtypeStruct((BLK, D), BF),) * CHUNKS,
        in_specs=[pair_block(EVENTS)]
        + [pair_block(BLK)] * CHUNKS
        + [pair_block(EVENTS)]
        + [head_block()] * 2,
        out_specs=[pair_block(EVENTS)] + [pair_block(BLK)] * CHUNKS,
        scratch_shapes=[pltpu.VMEM((CHUNKS, BLK, 2 * HEAD_DIM), BF)],
        compiler_params=params(),
        cost_estimate=pl.CostEstimate(
            flops=10**9, bytes_accessed=7 * 10**6, transcendentals=0
        ),
        name="far_backward",
    )(*in_hbm(q), *glob, *in_hbm(grad, probs, slope))


def near_backward_kernel(q, k, v, halo, grad, probs, slope, far, d_q, d_k, d_v, edge):
    masks = head_masks()
    sixteenth = jnp.asarray(1.0 / 16.0, BF)
    q16 = q[...] * sixteenth
    kx = jnp.concatenate([halo[0], k[...]], axis=0)
    vx = jnp.concatenate([halo[1], v[...]], axis=0)
    do = grad[...]
    q_t = [(q16 * m).T for m in masks]
    do_t = [(do * m).T for m in masks]
    kx_m = [kx * (m * sixteenth) for m in masks]
    blocks = [slice(i * BLK, (i + 1) * BLK) for i in range(NBD)]
    windows = [slice(i * BLK, (i + 2) * BLK) for i in range(NBD)]
    d_probs = [
        dot_nt(jnp.concatenate([do[blocks[i]] * m for m in masks], axis=0), vx[windows[i]])
        for i in range(NBD)
    ]
    all_ds = [
        [
            (d_probs[i][h * BLK : (h + 1) * BLK] * slope[h, blocks[i], :].astype(F32)).astype(BF)
            for h in range(2)
        ]
        for i in range(NBD)
    ]
    carry = None
    for i in range(NBD):
        rows, keys, ds = blocks[i], windows[i], all_ds[i]
        near_k = jnp.concatenate([m[keys] for m in kx_m], axis=0)
        d_q[rows, :] = (far[rows, :] + dot(jnp.concatenate(ds, axis=1), near_k)).astype(BF)
        near_p = jnp.concatenate([probs[h, rows, :] for h in range(2)], axis=0)
        dk = dot(jnp.concatenate([t[:, rows] for t in q_t], axis=1), jnp.concatenate(ds, axis=0)).T
        dv = dot(jnp.concatenate([t[:, rows] for t in do_t], axis=1), near_p).T
        if i == 0:
            edge[0] = dk[:BLK].astype(BF)
            edge[1] = dv[:BLK].astype(BF)
        else:
            last = slice((i - 1) * BLK, i * BLK)
            d_k[last, :] = (carry[0] + dk[:BLK]).astype(BF)
            d_v[last, :] = (carry[1] + dv[:BLK]).astype(BF)
        carry = (dk[BLK:], dv[BLK:])
    last = slice((NBD - 1) * BLK, NBD * BLK)
    d_k[last, :] = carry[0].astype(BF)
    d_v[last, :] = carry[1].astype(BF)


def near_backward(q, k, v, halo, grad, probs, slope, far):
    rows = jax.ShapeDtypeStruct((EVENTS, D), BF)
    return pl.pallas_call(
        near_backward_kernel,
        grid=(PAIRS,),
        out_shape=(
            rows,
            slow((EVENTS, D), BF),
            slow((EVENTS, D), BF),
            jax.ShapeDtypeStruct((2, BLK, D), BF),
        ),
        in_specs=[pair_block(EVENTS)] * 3
        + [pair_stack(BLK), pair_block(EVENTS)]
        + [head_block()] * 2
        + [pair_block(EVENTS)],
        out_specs=[pair_block(EVENTS)] * 3 + [pair_stack(BLK)],
        compiler_params=params(),
        cost_estimate=pl.CostEstimate(
            flops=10**9, bytes_accessed=9 * 10**6, transcendentals=0
        ),
        name="near_backward",
    )(q, k, v, halo, grad, probs, slope, *in_vmem(far))


def middle_kernel(
    lengths,
    code,
    user,
    inv,
    w_out,
    items_far,
    normed_far,
    gate_far,
    out_far,
    attn_far,
    gated_far,
    score,
    items,
    normed,
    gate,
    outgoing,
    d_attn,
    d_gate,
    sems,
):
    parts = 4
    portion = NDEV * SLOTS // parts
    slices = [slice(i * portion, (i + 1) * portion) for i in range(parts)]
    item_loads = [
        pltpu.make_async_copy(items_far.at[rows, :], items.at[rows, :], sems.at[3 + i])
        for i, rows in enumerate(slices)
    ]
    loads = [
        pltpu.make_async_copy(normed_far, normed, sems.at[0]),
        pltpu.make_async_copy(gate_far, gate, sems.at[1]),
    ]
    for load in item_loads + loads:
        load.start()
    send = pltpu.make_async_copy(outgoing, out_far, sems.at[2])
    user_b = user[...].astype(BF)
    user_t = user[...].T.astype(BF)
    first = code[...] >= FIRST
    rank = jnp.where(first, code[...] - FIRST, code[...])
    group = 8
    size = group * SLOTS
    slot = iota((SLOTS, EVENTS), 0).astype(F32)
    for d in range(0, NDEV, group):
        if d * SLOTS % portion == 0:
            item_loads[d * SLOTS // portion].wait()
        s = dot(items[d * SLOTS : d * SLOTS + size, :], user_t)
        for r in range(group):
            own = rank[d + r : d + r + 1, :] == slot
            part = jnp.where(own, s[r * SLOTS : (r + 1) * SLOTS, :], 0.0)
            score[d + r : d + r + 1, :] = jnp.sum(part, axis=0, keepdims=True)
    score0 = jnp.sum(jnp.where(first, score[...], 0.0), axis=0, keepdims=True)
    event = lax.axis_index("seq") * EVENTS + iota((1, EVENTS), 1)
    valid = jnp.where(event < lengths[lax.axis_index("user")], 1.0, 0.0)
    other = (rank >= 0.0) & jnp.logical_not(first)
    side = jnp.where(other, jax.nn.sigmoid(score[...] - score0), 0.0) * valid
    coef = jnp.where(first, -jnp.sum(side, axis=0, keepdims=True), side)
    d_user_t = jnp.zeros((E, EVENTS), F32)
    for d in range(0, NDEV, group):
        c = jnp.concatenate(
            [
                jnp.where(rank[r : r + 1, :] == slot, coef[r : r + 1, :], 0.0).astype(BF)
                for r in range(d, d + group)
            ],
            axis=0,
        )
        rows = slice(d * SLOTS, d * SLOTS + size)
        outgoing[rows, :] = dot(c, user_b).astype(BF)
        d_user_t = d_user_t + dot_tn(items[rows, :], c)
    send.start()
    sends = [send]
    d_user = d_user_t.T.astype(BF)
    for load in loads:
        load.wait()
    step = 128
    for r in range(0, EVENTS, step):
        rows = slice(r, r + step)
        d_gated = dot_nt(d_user[rows], w_out[...])
        n = normed[rows, :]
        d_gate[rows, :] = (d_gated * n).astype(BF)
        dn = d_gated * gate[rows, :].astype(F32)
        d_attn[rows, :] = (
            (
                dn
                - jnp.mean(dn, axis=1, keepdims=True)
                - n * jnp.mean(dn * n, axis=1, keepdims=True)
            )
            * inv[rows, :]
        ).astype(BF)
        for i, (near, far) in enumerate(((d_attn, attn_far), (d_gate, gated_far))):
            copy = pltpu.make_async_copy(
                near.at[rows, :], far.at[rows, :], sems.at[3 + parts + 2 * (r // step) + i]
            )
            copy.start()
            sends.append(copy)
    for send in sends:
        send.wait()


def middle(lengths, items, code, user, normed, inv, gate, w_out):
    return pl.pallas_call(
        middle_kernel,
        out_shape=(
            slow((NDEV * SLOTS, E), BF),
            slow((EVENTS, D), BF),
            slow((EVENTS, D), BF),
        ),
        in_specs=[SMEM_SPEC] + [VMEM_SPEC] * 4 + [ANY_SPEC] * 3,
        out_specs=[ANY_SPEC] * 3,
        scratch_shapes=[
            pltpu.VMEM((NDEV, EVENTS), F32),
            pltpu.VMEM((NDEV * SLOTS, E), BF),
            pltpu.VMEM((EVENTS, D), F32),
            pltpu.VMEM((EVENTS, D), BF),
            pltpu.VMEM((NDEV * SLOTS, E), BF),
            pltpu.VMEM((EVENTS, D), BF),
            pltpu.VMEM((EVENTS, D), BF),
            pltpu.SemaphoreType.DMA((3 + 4 + 2 * EVENTS // 128,)),
        ],
        compiler_params=params(),
        cost_estimate=pl.CostEstimate(
            flops=2 * 10**9, bytes_accessed=6 * 10**6, transcendentals=10**5
        ),
        name="ranking",
    )(lengths, *in_hbm(code, user, inv, w_out, items, normed, gate))


def finish_kernel(gids, d_k, d_v, edge, glob0, glob1, glob2, glob3, key_out, value_out):
    seq = lax.axis_index("seq")
    outs = (key_out, value_out)
    for which, mine in enumerate((d_k, d_v)):
        outs[which][...] = mine[...]
        tail = slice(EVENTS - BLK, EVENTS)
        outs[which][tail, :] = (mine[tail, :].astype(F32) + edge[which].astype(F32)).astype(BF)
    for d, more in enumerate((glob0, glob1, glob2, glob3)):
        c = chunk_of(CHUNKS - d)
        gid = gids[0, c % GLOB]
        place = pl.ds(pl.multiple_of((gid % NBD) * BLK, BLK), BLK)
        for which in range(2):

            @pl.when((gid // NBD == seq) & (c // GLOB == which))
            def _():
                out = outs[which]
                out[place, :] = (out[place, :].astype(F32) + more[...].astype(F32)).astype(BF)


def finish(gids, d_k, d_v, edge, total):
    rows = jax.ShapeDtypeStruct((EVENTS, D), BF)
    return pl.pallas_call(
        finish_kernel,
        out_shape=(rows, rows),
        in_specs=[SMEM_SPEC] + [VMEM_SPEC] * (3 + CHUNKS),
        out_specs=[VMEM_SPEC] * 2,
        compiler_params=params(),
        cost_estimate=pl.CostEstimate(flops=10**6, bytes_accessed=3 * 10**6, transcendentals=0),
        name="add_received",
    )(gids, d_k, d_v, edge, *total)


def from_behind(block, axis, distance):
    devices = range(lax.axis_size(axis))
    route_pairs = [(i - distance, i) for i in devices if i - distance in devices]
    return lax.ppermute(block, axis, route_pairs)


def exchange(x, axis):
    return lax.all_to_all(x, axis, split_axis=0, concat_axis=0, tiled=True)


def around_x(x, distance):
    pairs = [(i, i // XSIZE * XSIZE + (i + distance) % XSIZE) for i in range(NSEQ)]
    return lax.ppermute(x, "seq", pairs)


def around_z(x, distance):
    return lax.ppermute(x, "seq", [(i, (i + distance * XSIZE) % NSEQ) for i in range(NSEQ)])


def add_all(parts):
    return sum(p.astype(F32) for p in parts).astype(BF)


def from_x(chunks):
    return [chunks[0]] + [around_x(chunks[d], d) for d in range(1, CHUNKS)]


def from_z(mine):
    return [mine] + [around_z(mine, d) for d in range(1, NSEQ // XSIZE)]


def share_x(mine):
    return [mine] + [around_x(mine, d) for d in range(1, CHUNKS)]


def together(*values):
    return lax.optimization_barrier(values)


def on_device(
    query, key, value, gate, history, w_out, table, item_owner, item_row, gids, lengths
):
    q, k, v = query[0], key[0], value[0]
    owner = jnp.transpose(item_owner, (2, 0, 1))
    row = jnp.transpose(item_row, (2, 0, 1))
    tail, *cand = pieces(gids, k, v)
    parts = from_x(cand)
    owner, _ = together(owner, cand[0])
    req, code = route(owner, row)
    req, *parts = together(req, *parts)
    mine = add_all(parts)
    req, mine = together(req, mine)
    parts = from_z(mine)
    asked = exchange(req.reshape(NDEV, 1, E), ("seq", "user")).reshape(NDEV, E)
    mine = add_all(parts)
    glob = share_x(mine)
    halo = from_behind(tail, "seq", 1)
    asked, _ = together(asked, mine)
    found = gather(asked, table)
    found, halo, *glob = together(found, halo, *glob)
    items = exchange(found.reshape(NDEV, SLOTS, E), ("seq", "user")).reshape(NDEV * SLOTS, E)
    near_p, near_f, near = near_forward(lengths, q, k, v, halo)
    far_p, far_f, normed, inv, user = far_forward(
        lengths, gids, q, glob, near, gate[0], history[0], w_out
    )
    outgoing, d_attn, d_gate = middle(lengths, items, code, user, normed, inv, gate[0], w_out)
    incoming = exchange(outgoing.reshape(NDEV, SLOTS, E), ("seq", "user"))
    far_q, *d_glob = far_backward(q, glob, d_attn, far_p, far_f)
    parts = from_x(d_glob)
    d_q, d_k, d_v, edge = near_backward(q, k, v, halo, d_attn, near_p, near_f, far_q)
    d_k, *parts = together(d_k, *parts)
    mine = add_all(parts)
    back = from_behind(edge, "seq", -1)
    incoming, mine = together(incoming.reshape(NDEV * SLOTS, E), mine)
    grad = scatter(0, asked, incoming)
    grad, *parts = together(grad, *from_z(mine))
    mine = add_all(parts)
    grad, mine = together(grad, mine)
    grad = scatter(1, asked, incoming, (grad,))
    grad, *total = together(grad, *share_x(mine))
    d_key, d_value = finish(gids, d_k, d_v, back, total)
    return (d_q[None], d_key[None], d_value[None], d_gate[None], grad.reshape(ROWS, E))


def solution(mesh):
    return jax.shard_map(
        on_device,
        mesh=mesh,
        in_specs=(
            P("user", "seq", None),
            P("user", "seq", None),
            P("user", "seq", None),
            P("user", "seq", None),
            P("user", "seq", None),
            P(),
            P(("seq", "user"), None),
            P("user", "seq", None),
            P("user", "seq", None),
            P("user", None),
            P(),
        ),
        out_specs=(
            P("user", "seq", None),
            P("user", "seq", None),
            P("user", "seq", None),
            P("user", "seq", None),
            P(("seq", "user"), None),
        ),
        check_vma=False,
    )
```

```python
import functools

import jax
import jax.numpy as jnp
from jax import lax
from jax.experimental import pallas as pl
from jax.experimental.pallas import tpu as pltpu
from jax.sharding import PartitionSpec as P

HEADS = 8
HEAD_DIM = 64
D = 512
E = 128
BLK = 128
GLOB = 2
ITEMS = 5
EVENTS = 512
NBD = EVENTS // BLK
PAIRS = HEADS // 2
NDEV = 128
NSEQ = 16
CHUNKS = 2 * GLOB
ROWS = 4096
SLOTS = 32
FIRST = 64.0
HI = 4
LO = ROWS // HI
BF = jnp.bfloat16
F32 = jnp.float32
VMEM_LIMIT = 24 * 1024 * 1024
SMEM_SPEC = pl.BlockSpec(memory_space=pltpu.SMEM)
VMEM_SPEC = pl.BlockSpec(memory_space=pltpu.VMEM)
ANY_SPEC = pl.BlockSpec(memory_space=pl.ANY)
XSIZE = 4


def dot(a, b):
    return jnp.dot(a, b, preferred_element_type=F32)


def dot_nt(a, b):
    return lax.dot_general(a, b, (((1,), (1,)), ((), ())), preferred_element_type=F32)


def dot_tn(a, b):
    return lax.dot_general(a, b, (((0,), (0,)), ((), ())), preferred_element_type=F32)


def params(**more):
    return pltpu.CompilerParams(vmem_limit_bytes=VMEM_LIMIT, **more)


def fast(shape, dtype):
    return pltpu.VMEM(shape, dtype)


def slow(shape, dtype):
    return pltpu.HBM(shape, dtype)


def in_vmem(*arrays):
    return [pltpu.with_memory_space_constraint(x, pltpu.VMEM) for x in arrays]


def in_hbm(*arrays):
    return [pltpu.with_memory_space_constraint(x, pltpu.HBM) for x in arrays]


def whole(shape):
    return pl.BlockSpec(shape, lambda *_: (0,) * len(shape))


def iota(shape, dim):
    return lax.broadcasted_iota(jnp.int32, shape, dim)


def chunk_of(shift):
    return (lax.axis_index("seq") + shift) % XSIZE


def pieces_kernel(gids, key, value, halo, cand0, cand1, cand2, cand3, sems):
    seq = lax.axis_index("seq")
    tail = pl.ds(EVENTS - BLK, BLK)
    tails = [
        pltpu.make_async_copy(src.at[tail, :], halo.at[i], sems.at[CHUNKS + i])
        for i, src in enumerate((key, value))
    ]
    for copy in tails:
        copy.start()
    cases = []
    for d, out in enumerate((cand0, cand1, cand2, cand3)):
        c = chunk_of(d)
        gid = gids[0, c % GLOB]
        place = pl.ds(pl.multiple_of((gid % NBD) * BLK, BLK), BLK)
        held = gid // NBD == seq
        for i, src in enumerate((key, value)):
            copy = pltpu.make_async_copy(src.at[place, :], out, sems.at[d])
            cases.append((held & (c // GLOB == i), copy))

        @pl.when(jnp.logical_not(held))
        def _():
            out[...] = jnp.zeros((BLK, D), BF)

    for case, copy in cases:

        @pl.when(case)
        def _():
            copy.start()

    for case, copy in cases:

        @pl.when(case)
        def _():
            copy.wait()

    for copy in tails:
        copy.wait()


def pieces(gids, key, value):
    return pl.pallas_call(
        pieces_kernel,
        out_shape=(jax.ShapeDtypeStruct((2, BLK, D), BF),)
        + (jax.ShapeDtypeStruct((BLK, D), BF),) * CHUNKS,
        in_specs=[SMEM_SPEC] + [ANY_SPEC] * 2,
        out_specs=[VMEM_SPEC] * (1 + CHUNKS),
        scratch_shapes=[pltpu.SemaphoreType.DMA((CHUNKS + 2,))],
        compiler_params=params(),
        cost_estimate=pl.CostEstimate(flops=10**6, bytes_accessed=2 * 10**6, transcendentals=0),
        name="pieces",
    )(*in_hbm(gids, key, value))


def route_kernel(owner, row, req, code):
    dev = iota((NDEV, EVENTS), 0)
    rows = jnp.full((NDEV, EVENTS), -1, jnp.int32)
    for j in range(ITEMS):
        rows = jnp.where(owner[j] == dev, row[j], rows)
    hit = rows >= 0
    before = jnp.where(iota((EVENTS, EVENTS), 0) < iota((EVENTS, EVENTS), 1), 1.0, 0.0).astype(BF)
    rank = dot(jnp.where(hit, 1.0, 0.0).astype(BF), before)
    rank = jnp.where(hit, rank, -1.0)
    code[...] = jnp.where(owner[0] == dev, rank + FIRST, rank).astype(BF)
    plus = (rows + 1).astype(F32)
    lane = iota((NDEV, E), 1) - (lax.axis_index("user") % (E // SLOTS)) * SLOTS
    asked = jnp.zeros((NDEV, E), F32)
    for k in range(SLOTS):
        column = jnp.sum(jnp.where(rank == k, plus, 0.0), axis=1, keepdims=True)
        asked = jnp.where(lane == k, column, asked)
    req[...] = asked.astype(jnp.int32)


def route(owner, row):
    return pl.pallas_call(
        route_kernel,
        out_shape=(
            slow((NDEV, E), jnp.int32),
            slow((NDEV, EVENTS), BF),
        ),
        in_specs=[VMEM_SPEC] * 2,
        out_specs=[VMEM_SPEC] * 2,
        compiler_params=params(),
        cost_estimate=pl.CostEstimate(flops=10**8, bytes_accessed=10**6, transcendentals=0),
        name="route",
    )(*in_hbm(owner, row))


def slot_rows(asked, count):
    rows = asked[pl.ds(0, count, stride=4), :]
    for j in range(1, 4):
        rows = rows + asked[pl.ds(j, count, stride=4), :]
    return rows - 1


def slot_columns(rows):
    count = rows.shape[0]
    full = jnp.concatenate([rows.astype(F32), jnp.zeros((E - count, E), F32)], axis=0)
    return full.T[:, :count].astype(jnp.int32)


def spread_columns(x, first, count):
    return jnp.concatenate(
        [jnp.broadcast_to(x[:, i : i + 1], (E, E)) for i in range(first, first + count)], axis=0
    )


def gather_kernel(asked, table_far, found_far, kept, table, found, sems):
    slabs = [slice(h * LO, (h + 1) * LO) for h in range(HI)]
    loads = [
        pltpu.make_async_copy(table_far.at[slab, :], table.at[slab, :], sems.at[h])
        for h, slab in enumerate(slabs)
    ]
    for load in loads:
        load.start()
    keep = pltpu.make_async_copy(asked, kept, sems.at[HI + 4])
    keep.start()
    columns = slot_columns(slot_rows(asked, NDEV // 4))
    lo = columns & (LO - 1)
    hi = columns >> (LO.bit_length() - 1)
    group = 8
    size = group * E
    lane = iota((size, E), 1)
    sends = []
    for step in range(NDEV // 4 // group):
        low = spread_columns(lo, step * group, group)
        high = spread_columns(hi, step * group, group)
        onehot = jnp.concatenate(
            [jnp.where(low == lane + b * E, 1.0, 0.0).astype(BF) for b in range(LO // E)], axis=1
        )
        if step == 0:
            for load in loads:
                load.wait()
        picked = dot(onehot, jnp.concatenate([table[slab, :] for slab in slabs], axis=1))
        out = jnp.zeros((size, E), F32)
        for h in range(HI):
            out = jnp.where(high == h, picked[:, h * E : (h + 1) * E], out)
        rows = slice(step * size, (step + 1) * size)
        found[rows, :] = out.astype(BF)
        sends.append(
            pltpu.make_async_copy(found.at[rows, :], found_far.at[rows, :], sems.at[HI + step])
        )
        sends[-1].start()
    for send in sends:
        send.wait()
    keep.wait()


def gather(asked, table):
    return pl.pallas_call(
        gather_kernel,
        out_shape=(slow((NDEV * SLOTS, E), BF), slow((NDEV, E), jnp.int32)),
        in_specs=[VMEM_SPEC, ANY_SPEC],
        out_specs=[ANY_SPEC] * 2,
        scratch_shapes=[
            pltpu.VMEM((ROWS, E), BF),
            pltpu.VMEM((NDEV * SLOTS, E), BF),
            pltpu.SemaphoreType.DMA((HI + 5,)),
        ],
        compiler_params=params(),
        cost_estimate=pl.CostEstimate(
            flops=2 * NDEV * SLOTS * ROWS * E, bytes_accessed=2 * 10**6, transcendentals=0
        ),
        name="gather_rows",
    )(*in_vmem(asked), *in_hbm(table))


HALVES = 2


def scatter_kernel(half, asked, incoming, *refs):
    grad, spread = refs[-2:]
    rows = slot_rows(asked, NDEV // 4)
    hi = slot_columns(rows) >> (LO.bit_length() - 1)
    group = 2
    size = group * E
    for first in range(0, NDEV // 4, group):
        high = spread_columns(hi, first, group)
        part = incoming[first * E : first * E + size, :].astype(F32)
        for h in range(HI):
            spread[first * E : first * E + size, h * E : (h + 1) * E] = jnp.where(
                high == h, part, 0.0
            ).astype(BF)
    size = LO // HALVES
    sub = iota((size, E), 0) + half * size
    lo = rows & (LO - 1)
    onehot = jnp.concatenate(
        [jnp.where(sub == lo[i : i + 1, :], 1.0, 0.0).astype(BF) for i in range(NDEV // 4)], axis=1
    )
    total = dot(onehot, spread[...])
    for h in range(HI):
        grad[h] = total[:, h * E : (h + 1) * E]


def scatter(half, asked, incoming, before=()):
    count = NDEV * SLOTS
    return pl.pallas_call(
        functools.partial(scatter_kernel, half),
        grid=(1,),
        out_shape=slow((HI, LO, E), F32),
        in_specs=[whole((NDEV, E)), whole((count, E))] + [ANY_SPEC] * len(before),
        out_specs=pl.BlockSpec((HI, LO // HALVES, E), lambda i: (0, half, 0)),
        scratch_shapes=[pltpu.VMEM((count, HI * E), BF)],
        input_output_aliases={2 + i: i for i in range(len(before))},
        compiler_params=params(),
        cost_estimate=pl.CostEstimate(
            flops=count * ROWS * E, bytes_accessed=2 * 10**6, transcendentals=0
        ),
        name="scatter_rows",
    )(asked, incoming, *in_hbm(*before))


def head_masks():
    lane = iota((1, 2 * HEAD_DIM), 1)
    return [
        jnp.where(lane < HEAD_DIM, 1.0, 0.0).astype(BF),
        jnp.where(lane >= HEAD_DIM, 1.0, 0.0).astype(BF),
    ]


def act(u, mask):
    w = jnp.where(mask, 1.0 + jnp.tanh(u), 0.0)
    p = u * w
    return p.astype(BF), (w + p * (2.0 - w)).astype(BF)


def near_forward_kernel(lengths, q, k, v, halo, probs, slope, attn):
    base = lax.axis_index("seq") * NBD
    length = lengths[lax.axis_index("user")]
    masks = head_masks()
    q16 = q[...] * jnp.asarray(1.0 / 16.0, BF)
    kx = jnp.concatenate([halo[0], k[...]], axis=0)
    vx = jnp.concatenate([halo[1], v[...]], axis=0)
    lane = iota((BLK, 2 * BLK), 1)
    sub = iota((BLK, 2 * BLK), 0)
    vx_m = [vx * m for m in masks]
    both = [jnp.concatenate([q16[i * BLK : (i + 1) * BLK] * m for m in masks]) for i in range(NBD)]
    logits = [dot_nt(both[i], kx[i * BLK : (i + 2) * BLK]) for i in range(NBD)]
    held = []
    for i in range(NBD):
        rows = slice(i * BLK, (i + 1) * BLK)
        at = (base + i - 1) * BLK + lane
        mask = (at >= 0) & (at < length) & (lane <= sub + BLK)
        parts = []
        for h in range(2):
            p, f = act(logits[i][h * BLK : (h + 1) * BLK], mask)
            probs[h, rows, :] = p
            slope[h, rows, :] = f
            parts.append(p)
        held.append(jnp.concatenate(parts, axis=1))
    for i in range(NBD):
        keys = slice(i * BLK, (i + 2) * BLK)
        attn[i * BLK : (i + 1) * BLK, :] = dot(
            held[i], jnp.concatenate([m[keys] for m in vx_m], axis=0)
        )


def unrotate(parts, scratch):
    for d in range(CHUNKS):
        scratch[chunk_of(CHUNKS - d)] = parts[d][...]
    keys = jnp.concatenate([scratch[g] for g in range(GLOB)], axis=0)
    values = jnp.concatenate([scratch[GLOB + g] for g in range(GLOB)], axis=0)
    return keys, values


def far_forward_kernel(
    lengths,
    gids,
    q,
    glob0,
    glob1,
    glob2,
    glob3,
    near,
    gate,
    history,
    w_out,
    probs,
    slope,
    normed_out,
    inv_out,
    user,
    attn,
    scratch,
):
    pair = pl.program_id(0)
    base = lax.axis_index("seq") * NBD
    length = lengths[lax.axis_index("user")]
    masks = head_masks()
    q16 = q[...] * jnp.asarray(1.0 / 16.0, BF)
    kg, vg = unrotate((glob0, glob1, glob2, glob3), scratch)
    lane = iota((BLK, 2 * BLK), 1)
    gid = jnp.where(lane < BLK, gids[0, 0], gids[0, 1])
    at = gid * BLK + lane % BLK
    vg_both = jnp.concatenate([vg * m for m in masks], axis=0)
    logits = dot_nt(jnp.concatenate([q16 * m for m in masks], axis=0), kg)
    held = []
    for i in range(NBD):
        rows = slice(i * BLK, (i + 1) * BLK)
        mask = (gid < base + i - 1) & (at < length)
        parts = []
        for h in range(2):
            p, f = act(logits[h * EVENTS + i * BLK : h * EVENTS + (i + 1) * BLK], mask)
            probs[h, rows, :] = p
            slope[h, rows, :] = f
            parts.append(p)
        held.append(jnp.concatenate(parts, axis=1))
    attn[pair] = near[...] + dot(jnp.concatenate(held, axis=0), vg_both)

    @pl.when(pair == PAIRS - 1)
    def _():
        step = 128
        for r in range(0, EVENTS, step):
            rows = slice(r, r + step)
            x = jnp.concatenate([attn[p, rows, :] for p in range(PAIRS)], axis=1)
            centered = x - jnp.mean(x, axis=1, keepdims=True)
            var = jnp.mean(centered * centered, axis=1, keepdims=True)
            inv = lax.rsqrt(var + 1e-05)
            normed = centered * inv
            normed_out[rows, :] = normed
            inv_out[rows, :] = inv
            gated = (normed * gate[rows, :].astype(F32)).astype(BF)
            user[rows, :] = (dot(gated, w_out[...]) + history[rows, :].astype(F32)).astype(BF)


def pair_block(rows):
    return pl.BlockSpec((rows, 2 * HEAD_DIM), lambda p: (0, p))


def pair_stack(rows):
    return pl.BlockSpec((2, rows, 2 * HEAD_DIM), lambda p: (0, 0, p))


def head_block():
    return pl.BlockSpec((2, EVENTS, 2 * BLK), lambda p: (p, 0, 0))


SQUARE = slow((HEADS, EVENTS, 2 * BLK), BF)


def near_forward(lengths, q, k, v, halo):
    return pl.pallas_call(
        near_forward_kernel,
        grid=(PAIRS,),
        out_shape=(SQUARE, SQUARE, fast((EVENTS, D), F32)),
        in_specs=[SMEM_SPEC] + [pair_block(EVENTS)] * 3 + [pair_stack(BLK)],
        out_specs=[head_block(), head_block(), pair_block(EVENTS)],
        compiler_params=params(),
        cost_estimate=pl.CostEstimate(
            flops=5 * 10**8, bytes_accessed=7 * 10**6, transcendentals=10**6
        ),
        name="near_forward",
    )(*in_hbm(lengths), q, k, v, halo)


def far_forward(lengths, gids, q, glob, near, gate, history, w_out):
    return pl.pallas_call(
        far_forward_kernel,
        grid=(PAIRS,),
        out_shape=(
            SQUARE,
            SQUARE,
            slow((EVENTS, D), F32),
            slow((EVENTS, 1), F32),
            slow((EVENTS, E), BF),
        ),
        in_specs=[SMEM_SPEC] * 2
        + [pair_block(EVENTS)]
        + [pair_block(BLK)] * CHUNKS
        + [pair_block(EVENTS)]
        + [whole((EVENTS, D)), whole((EVENTS, E)), whole((D, E))],
        out_specs=[
            head_block(),
            head_block(),
            whole((EVENTS, D)),
            whole((EVENTS, 1)),
            whole((EVENTS, E)),
        ],
        scratch_shapes=[
            pltpu.VMEM((PAIRS, EVENTS, 2 * HEAD_DIM), F32),
            pltpu.VMEM((CHUNKS, BLK, 2 * HEAD_DIM), BF),
        ],
        compiler_params=params(),
        cost_estimate=pl.CostEstimate(
            flops=6 * 10**8, bytes_accessed=9 * 10**6, transcendentals=10**6
        ),
        name="far_forward",
    )(*in_hbm(lengths, gids), q, *glob, *in_vmem(near), *in_hbm(gate, history, w_out))


def far_backward_kernel(
    q, glob0, glob1, glob2, glob3, grad, probs, slope, d_q, out0, out1, out2, out3, scratch
):
    masks = head_masks()
    sixteenth = jnp.asarray(1.0 / 16.0, BF)
    q16 = q[...] * sixteenth
    kg, vg = unrotate((glob0, glob1, glob2, glob3), scratch)
    do = grad[...]
    q_t = jnp.concatenate([(q16 * m).T for m in masks], axis=1)
    do_t = jnp.concatenate([(do * m).T for m in masks], axis=1)
    kg_both = jnp.concatenate([kg * (m * sixteenth) for m in masks], axis=0)
    d_probs = dot_nt(jnp.concatenate([do * m for m in masks], axis=0), vg)
    ds = [
        (d_probs[h * EVENTS : (h + 1) * EVENTS] * slope[h].astype(F32)).astype(BF) for h in range(2)
    ]
    d_q[...] = dot(jnp.concatenate(ds, axis=1), kg_both)
    d_k = dot(q_t, jnp.concatenate(ds, axis=0)).T.astype(BF)
    d_v = dot(do_t, jnp.concatenate([probs[0], probs[1]], axis=0)).T.astype(BF)
    for g in range(GLOB):
        scratch[g] = d_k[g * BLK : (g + 1) * BLK]
        scratch[GLOB + g] = d_v[g * BLK : (g + 1) * BLK]
    for d, out in enumerate((out0, out1, out2, out3)):
        out[...] = scratch[chunk_of(d)]


def far_backward(q, glob, grad, probs, slope):
    return pl.pallas_call(
        far_backward_kernel,
        grid=(PAIRS,),
        out_shape=(fast((EVENTS, D), F32),)
        + (jax.ShapeDtypeStruct((BLK, D), BF),) * CHUNKS,
        in_specs=[pair_block(EVENTS)]
        + [pair_block(BLK)] * CHUNKS
        + [pair_block(EVENTS)]
        + [head_block()] * 2,
        out_specs=[pair_block(EVENTS)] + [pair_block(BLK)] * CHUNKS,
        scratch_shapes=[pltpu.VMEM((CHUNKS, BLK, 2 * HEAD_DIM), BF)],
        compiler_params=params(),
        cost_estimate=pl.CostEstimate(
            flops=10**9, bytes_accessed=7 * 10**6, transcendentals=0
        ),
        name="far_backward",
    )(*in_hbm(q), *glob, *in_hbm(grad, probs, slope))


def near_backward_kernel(q, k, v, halo, grad, probs, slope, far, d_q, d_k, d_v, edge):
    masks = head_masks()
    sixteenth = jnp.asarray(1.0 / 16.0, BF)
    q16 = q[...] * sixteenth
    kx = jnp.concatenate([halo[0], k[...]], axis=0)
    vx = jnp.concatenate([halo[1], v[...]], axis=0)
    do = grad[...]
    q_t = [(q16 * m).T for m in masks]
    do_t = [(do * m).T for m in masks]
    kx_m = [kx * (m * sixteenth) for m in masks]
    blocks = [slice(i * BLK, (i + 1) * BLK) for i in range(NBD)]
    windows = [slice(i * BLK, (i + 2) * BLK) for i in range(NBD)]
    d_probs = [
        dot_nt(jnp.concatenate([do[blocks[i]] * m for m in masks], axis=0), vx[windows[i]])
        for i in range(NBD)
    ]
    all_ds = [
        [
            (d_probs[i][h * BLK : (h + 1) * BLK] * slope[h, blocks[i], :].astype(F32)).astype(BF)
            for h in range(2)
        ]
        for i in range(NBD)
    ]
    carry = None
    for i in range(NBD):
        rows, keys, ds = blocks[i], windows[i], all_ds[i]
        near_k = jnp.concatenate([m[keys] for m in kx_m], axis=0)
        d_q[rows, :] = (far[rows, :] + dot(jnp.concatenate(ds, axis=1), near_k)).astype(BF)
        near_p = jnp.concatenate([probs[h, rows, :] for h in range(2)], axis=0)
        dk = dot(jnp.concatenate([t[:, rows] for t in q_t], axis=1), jnp.concatenate(ds, axis=0)).T
        dv = dot(jnp.concatenate([t[:, rows] for t in do_t], axis=1), near_p).T
        if i == 0:
            edge[0] = dk[:BLK].astype(BF)
            edge[1] = dv[:BLK].astype(BF)
        else:
            last = slice((i - 1) * BLK, i * BLK)
            d_k[last, :] = (carry[0] + dk[:BLK]).astype(BF)
            d_v[last, :] = (carry[1] + dv[:BLK]).astype(BF)
        carry = (dk[BLK:], dv[BLK:])
    last = slice((NBD - 1) * BLK, NBD * BLK)
    d_k[last, :] = carry[0].astype(BF)
    d_v[last, :] = carry[1].astype(BF)


def near_backward(q, k, v, halo, grad, probs, slope, far):
    rows = jax.ShapeDtypeStruct((EVENTS, D), BF)
    return pl.pallas_call(
        near_backward_kernel,
        grid=(PAIRS,),
        out_shape=(
            rows,
            slow((EVENTS, D), BF),
            slow((EVENTS, D), BF),
            jax.ShapeDtypeStruct((2, BLK, D), BF),
        ),
        in_specs=[pair_block(EVENTS)] * 3
        + [pair_stack(BLK), pair_block(EVENTS)]
        + [head_block()] * 2
        + [pair_block(EVENTS)],
        out_specs=[pair_block(EVENTS)] * 3 + [pair_stack(BLK)],
        compiler_params=params(),
        cost_estimate=pl.CostEstimate(
            flops=10**9, bytes_accessed=9 * 10**6, transcendentals=0
        ),
        name="near_backward",
    )(q, k, v, halo, grad, probs, slope, *in_vmem(far))


def middle_kernel(
    lengths,
    items,
    code,
    user,
    normed_far,
    gate_far,
    inv_far,
    w_far,
    out_far,
    attn_far,
    gated_far,
    score,
    normed,
    gate,
    inv,
    w_out,
    outgoing,
    d_attn,
    d_gate,
    sems,
):
    loads = [
        pltpu.make_async_copy(normed_far, normed, sems.at[0]),
        pltpu.make_async_copy(gate_far, gate, sems.at[1]),
        pltpu.make_async_copy(inv_far, inv, sems.at[2]),
        pltpu.make_async_copy(w_far, w_out, sems.at[3]),
    ]
    for load in loads:
        load.start()
    sends = []

    def send(near, far, rows):
        copy = pltpu.make_async_copy(near.at[rows, :], far.at[rows, :], sems.at[4 + len(sends)])
        copy.start()
        sends.append(copy)

    portion = NDEV * SLOTS // 4
    user_b = user[...]
    user_t = user_b.T
    mark = code[...].astype(F32)
    first = mark >= FIRST
    rank = jnp.where(first, mark - FIRST, mark)
    group = 8
    size = group * SLOTS
    slot = iota((SLOTS, EVENTS), 0).astype(F32)
    for d in range(0, NDEV, group):
        s = dot(items[d * SLOTS : d * SLOTS + size, :], user_t)
        for r in range(group):
            own = rank[d + r : d + r + 1, :] == slot
            part = jnp.where(own, s[r * SLOTS : (r + 1) * SLOTS, :], 0.0)
            score[d + r : d + r + 1, :] = jnp.sum(part, axis=0, keepdims=True)
    score0 = jnp.sum(jnp.where(first, score[...], 0.0), axis=0, keepdims=True)
    event = lax.axis_index("seq") * EVENTS + iota((1, EVENTS), 1)
    valid = jnp.where(event < lengths[lax.axis_index("user")], 1.0, 0.0)
    other = (rank >= 0.0) & jnp.logical_not(first)
    side = jnp.where(other, jax.nn.sigmoid(score[...] - score0), 0.0) * valid
    coef = jnp.where(first, -jnp.sum(side, axis=0, keepdims=True), side)
    d_user_t = jnp.zeros((E, EVENTS), F32)
    for d in range(0, NDEV, group):
        c = jnp.concatenate(
            [
                jnp.where(rank[r : r + 1, :] == slot, coef[r : r + 1, :], 0.0).astype(BF)
                for r in range(d, d + group)
            ],
            axis=0,
        )
        rows = slice(d * SLOTS, d * SLOTS + size)
        outgoing[rows, :] = dot(c, user_b).astype(BF)
        d_user_t = d_user_t + dot_tn(items[rows, :], c)
        if rows.stop % portion == 0:
            send(outgoing, out_far, slice(rows.stop - portion, rows.stop))
    d_user = d_user_t.T.astype(BF)
    for load in loads:
        load.wait()
    step = 128
    for r in range(0, EVENTS, step):
        rows = slice(r, r + step)
        d_gated = dot_nt(d_user[rows], w_out[...])
        n = normed[rows, :]
        d_gate[rows, :] = (d_gated * n).astype(BF)
        dn = d_gated * gate[rows, :].astype(F32)
        d_attn[rows, :] = (
            (
                dn
                - jnp.mean(dn, axis=1, keepdims=True)
                - n * jnp.mean(dn * n, axis=1, keepdims=True)
            )
            * inv[rows, :]
        ).astype(BF)
        send(d_attn, attn_far, rows)
        send(d_gate, gated_far, rows)
    for copy in sends:
        copy.wait()


def middle(lengths, items, code, user, normed, inv, gate, w_out):
    return pl.pallas_call(
        middle_kernel,
        out_shape=(
            slow((NDEV * SLOTS, E), BF),
            slow((EVENTS, D), BF),
            slow((EVENTS, D), BF),
        ),
        in_specs=[SMEM_SPEC] + [VMEM_SPEC] * 3 + [ANY_SPEC] * 4,
        out_specs=[ANY_SPEC] * 3,
        scratch_shapes=[
            pltpu.VMEM((NDEV, EVENTS), F32),
            pltpu.VMEM((EVENTS, D), F32),
            pltpu.VMEM((EVENTS, D), BF),
            pltpu.VMEM((EVENTS, 1), F32),
            pltpu.VMEM((D, E), BF),
            pltpu.VMEM((NDEV * SLOTS, E), BF),
            pltpu.VMEM((EVENTS, D), BF),
            pltpu.VMEM((EVENTS, D), BF),
            pltpu.SemaphoreType.DMA((4 + 4 + 2 * EVENTS // 128,)),
        ],
        compiler_params=params(),
        cost_estimate=pl.CostEstimate(
            flops=2 * 10**9, bytes_accessed=6 * 10**6, transcendentals=10**5
        ),
        name="ranking",
    )(*in_hbm(lengths), *in_vmem(items), *in_hbm(code, user, normed, gate, inv, w_out))


def finish_kernel(gids, d_k, d_v, edge, glob0, glob1, glob2, glob3, key_out, value_out):
    seq = lax.axis_index("seq")
    outs = (key_out, value_out)
    for which, mine in enumerate((d_k, d_v)):
        outs[which][...] = mine[...]
        tail = slice(EVENTS - BLK, EVENTS)
        outs[which][tail, :] = (mine[tail, :].astype(F32) + edge[which].astype(F32)).astype(BF)
    for d, more in enumerate((glob0, glob1, glob2, glob3)):
        c = chunk_of(CHUNKS - d)
        gid = gids[0, c % GLOB]
        place = pl.ds(pl.multiple_of((gid % NBD) * BLK, BLK), BLK)
        for which in range(2):

            @pl.when((gid // NBD == seq) & (c // GLOB == which))
            def _():
                out = outs[which]
                out[place, :] = (out[place, :].astype(F32) + more[...].astype(F32)).astype(BF)


def finish(gids, d_k, d_v, edge, total):
    rows = jax.ShapeDtypeStruct((EVENTS, D), BF)
    return pl.pallas_call(
        finish_kernel,
        out_shape=(rows, rows),
        in_specs=[SMEM_SPEC] + [VMEM_SPEC] * (3 + CHUNKS),
        out_specs=[VMEM_SPEC] * 2,
        compiler_params=params(),
        cost_estimate=pl.CostEstimate(flops=10**6, bytes_accessed=3 * 10**6, transcendentals=0),
        name="add_received",
    )(*in_hbm(gids), d_k, d_v, edge, *total)


def from_behind(block, axis, distance):
    devices = range(lax.axis_size(axis))
    route_pairs = [(i - distance, i) for i in devices if i - distance in devices]
    return lax.ppermute(block, axis, route_pairs)


def exchange(x, axis):
    return lax.all_to_all(x, axis, split_axis=0, concat_axis=0, tiled=True)


def around_x(x, distance):
    pairs = [(i, i // XSIZE * XSIZE + (i + distance) % XSIZE) for i in range(NSEQ)]
    return lax.ppermute(x, "seq", pairs)


def around_z(x, distance):
    return lax.ppermute(x, "seq", [(i, (i + distance * XSIZE) % NSEQ) for i in range(NSEQ)])


def add_all(parts):
    return sum(p.astype(F32) for p in parts).astype(BF)


def from_x(chunks):
    return [chunks[0]] + [around_x(chunks[d], d) for d in range(1, CHUNKS)]


def from_z(mine):
    return [mine] + [around_z(mine, d) for d in range(1, NSEQ // XSIZE)]


def share_x(mine):
    return [mine] + [around_x(mine, d) for d in range(1, CHUNKS)]


def together(*values):
    return lax.optimization_barrier(values)


def on_device(
    query, key, value, gate, history, w_out, table, item_owner, item_row, gids, lengths
):
    q, k, v = query[0], key[0], value[0]
    owner = jnp.transpose(item_owner, (2, 0, 1))
    row = jnp.transpose(item_row, (2, 0, 1))
    tail, *cand = pieces(gids, k, v)
    parts = from_x(cand)
    owner, _ = together(owner, cand[0])
    req, code = route(owner, row)
    tail, _ = together(tail, req)
    halo = from_behind(tail, "seq", 1)
    req, *parts = together(req, *parts)
    mine = add_all(parts)
    parts = from_z(mine)
    req, halo, _ = together(req, halo, mine)
    asked = exchange(req.reshape(NDEV, 1, E), ("seq", "user")).reshape(NDEV, E)
    mine = add_all(parts)
    glob = share_x(mine)
    asked, _ = together(asked, mine)
    found, asked = gather(asked, table)
    found, *glob = together(found, *glob)
    items = exchange(found.reshape(NDEV, SLOTS, E), ("seq", "user")).reshape(NDEV * SLOTS, E)
    near_p, near_f, near = near_forward(lengths, q, k, v, halo)
    far_p, far_f, normed, inv, user = far_forward(
        lengths, gids, q, glob, near, gate[0], history[0], w_out
    )
    outgoing, d_attn, d_gate = middle(lengths, items, code, user, normed, inv, gate[0], w_out)
    incoming = exchange(outgoing.reshape(NDEV, SLOTS, E), ("seq", "user"))
    far_q, *d_glob = far_backward(q, glob, d_attn, far_p, far_f)
    parts = from_x(d_glob)
    d_q, d_k, d_v, edge = near_backward(q, k, v, halo, d_attn, near_p, near_f, far_q)
    d_k, *parts = together(d_k, *parts)
    mine = add_all(parts)
    back = from_behind(edge, "seq", -1)
    incoming, mine = together(incoming.reshape(NDEV * SLOTS, E), mine)
    grad = scatter(0, asked, incoming)
    grad, *parts = together(grad, *from_z(mine))
    mine = add_all(parts)
    grad, mine = together(grad, mine)
    grad = scatter(1, asked, incoming, (grad,))
    grad, *total = together(grad, *share_x(mine))
    d_key, d_value = finish(gids, d_k, d_v, back, total)
    return (d_q[None], d_key[None], d_value[None], d_gate[None], grad.reshape(ROWS, E))


def solution(mesh):
    return jax.shard_map(
        on_device,
        mesh=mesh,
        in_specs=(
            P("user", "seq", None),
            P("user", "seq", None),
            P("user", "seq", None),
            P("user", "seq", None),
            P("user", "seq", None),
            P(),
            P(("seq", "user"), None),
            P("user", "seq", None),
            P("user", "seq", None),
            P("user", None),
            P(),
        ),
        out_specs=(
            P("user", "seq", None),
            P("user", "seq", None),
            P("user", "seq", None),
            P("user", "seq", None),
            P(("seq", "user"), None),
        ),
        check_vma=False,
    )
```

```python
import functools

import jax
import jax.numpy as jnp
from jax import lax
from jax.experimental import pallas as pl
from jax.experimental.pallas import tpu as pltpu
from jax.sharding import PartitionSpec as P

HEADS = 8
HEAD_DIM = 64
D = 512
E = 128
BLK = 128
GLOB = 2
ITEMS = 5
EVENTS = 512
NBD = EVENTS // BLK
PAIRS = HEADS // 2
NDEV = 128
NSEQ = 16
CHUNKS = 2 * GLOB
ROWS = 4096
SLOTS = 32
FIRST = 64.0
HI = 4
LO = ROWS // HI
BF = jnp.bfloat16
F32 = jnp.float32
VMEM_LIMIT = 24 * 1024 * 1024
SMEM_SPEC = pl.BlockSpec(memory_space=pltpu.SMEM)
VMEM_SPEC = pl.BlockSpec(memory_space=pltpu.VMEM)
ANY_SPEC = pl.BlockSpec(memory_space=pl.ANY)
XSIZE = 4


def dot(a, b):
    return jnp.dot(a, b, preferred_element_type=F32)


def dot_nt(a, b):
    return lax.dot_general(a, b, (((1,), (1,)), ((), ())), preferred_element_type=F32)


def dot_tn(a, b):
    return lax.dot_general(a, b, (((0,), (0,)), ((), ())), preferred_element_type=F32)


def params(**more):
    return pltpu.CompilerParams(vmem_limit_bytes=VMEM_LIMIT, **more)


def fast(shape, dtype):
    return pltpu.VMEM(shape, dtype)


def slow(shape, dtype):
    return pltpu.HBM(shape, dtype)


def in_vmem(*arrays):
    return [pltpu.with_memory_space_constraint(x, pltpu.VMEM) for x in arrays]


def in_hbm(*arrays):
    return [pltpu.with_memory_space_constraint(x, pltpu.HBM) for x in arrays]


def whole(shape):
    return pl.BlockSpec(shape, lambda *_: (0,) * len(shape))


def iota(shape, dim):
    return lax.broadcasted_iota(jnp.int32, shape, dim)


def chunk_of(shift):
    return (lax.axis_index("seq") + shift) % XSIZE


def pieces_kernel(gids, key, value, halo, cand0, cand1, cand2, cand3, sems):
    seq = lax.axis_index("seq")
    tail = pl.ds(EVENTS - BLK, BLK)
    tails = [
        pltpu.make_async_copy(src.at[tail, :], halo.at[i], sems.at[CHUNKS + i])
        for i, src in enumerate((key, value))
    ]
    for copy in tails:
        copy.start()
    cases = []
    for d, out in enumerate((cand0, cand1, cand2, cand3)):
        c = chunk_of(d)
        gid = gids[0, c % GLOB]
        place = pl.ds(pl.multiple_of((gid % NBD) * BLK, BLK), BLK)
        held = gid // NBD == seq
        for i, src in enumerate((key, value)):
            copy = pltpu.make_async_copy(src.at[place, :], out, sems.at[d])
            cases.append((held & (c // GLOB == i), copy))

        @pl.when(jnp.logical_not(held))
        def _():
            out[...] = jnp.zeros((BLK, D), BF)

    for case, copy in cases:

        @pl.when(case)
        def _():
            copy.start()

    for case, copy in cases:

        @pl.when(case)
        def _():
            copy.wait()

    for copy in tails:
        copy.wait()


def pieces(gids, key, value):
    return pl.pallas_call(
        pieces_kernel,
        out_shape=(jax.ShapeDtypeStruct((2, BLK, D), BF),)
        + (jax.ShapeDtypeStruct((BLK, D), BF),) * CHUNKS,
        in_specs=[SMEM_SPEC] + [ANY_SPEC] * 2,
        out_specs=[VMEM_SPEC] * (1 + CHUNKS),
        scratch_shapes=[pltpu.SemaphoreType.DMA((CHUNKS + 2,))],
        compiler_params=params(),
        cost_estimate=pl.CostEstimate(flops=10**6, bytes_accessed=2 * 10**6, transcendentals=0),
        name="pieces",
    )(*in_hbm(gids, key, value))


def route_kernel(owner, row, req, code):
    dev = iota((NDEV, EVENTS), 0)
    rows = jnp.full((NDEV, EVENTS), -1, jnp.int32)
    for j in range(ITEMS):
        rows = jnp.where(owner[j] == dev, row[j], rows)
    hit = rows >= 0
    before = jnp.where(iota((EVENTS, EVENTS), 0) < iota((EVENTS, EVENTS), 1), 1.0, 0.0).astype(BF)
    rank = dot(jnp.where(hit, 1.0, 0.0).astype(BF), before)
    rank = jnp.where(hit, rank, -1.0)
    code[...] = jnp.where(owner[0] == dev, rank + FIRST, rank).astype(BF)
    plus = (rows + 1).astype(F32)
    lane = iota((NDEV, E), 1) - (lax.axis_index("user") % (E // SLOTS)) * SLOTS
    asked = jnp.zeros((NDEV, E), F32)
    for k in range(SLOTS):
        column = jnp.sum(jnp.where(rank == k, plus, 0.0), axis=1, keepdims=True)
        asked = jnp.where(lane == k, column, asked)
    req[...] = asked.astype(jnp.int32)


def route(owner, row):
    return pl.pallas_call(
        route_kernel,
        out_shape=(
            slow((NDEV, E), jnp.int32),
            slow((NDEV, EVENTS), BF),
        ),
        in_specs=[VMEM_SPEC] * 2,
        out_specs=[VMEM_SPEC] * 2,
        compiler_params=params(),
        cost_estimate=pl.CostEstimate(flops=10**8, bytes_accessed=10**6, transcendentals=0),
        name="route",
    )(*in_hbm(owner, row))


def slot_rows(asked, count):
    rows = asked[pl.ds(0, count, stride=4), :]
    for j in range(1, 4):
        rows = rows + asked[pl.ds(j, count, stride=4), :]
    return rows - 1


def slot_columns(rows):
    count = rows.shape[0]
    full = jnp.concatenate([rows.astype(F32), jnp.zeros((E - count, E), F32)], axis=0)
    return full.T[:, :count].astype(jnp.int32)


def spread_columns(x, first, count):
    return jnp.concatenate(
        [jnp.broadcast_to(x[:, i : i + 1], (E, E)) for i in range(first, first + count)], axis=0
    )


def gather_kernel(asked, table_far, found_far, kept, table, found, sems):
    slabs = [slice(h * LO, (h + 1) * LO) for h in range(HI)]
    loads = [
        pltpu.make_async_copy(table_far.at[slab, :], table.at[slab, :], sems.at[h])
        for h, slab in enumerate(slabs)
    ]
    for load in loads:
        load.start()
    keep = pltpu.make_async_copy(asked, kept, sems.at[HI + 4])
    keep.start()
    columns = slot_columns(slot_rows(asked, NDEV // 4))
    lo = columns & (LO - 1)
    hi = columns >> (LO.bit_length() - 1)
    group = 8
    size = group * E
    lane = iota((size, E), 1)
    sends = []
    for step in range(NDEV // 4 // group):
        low = spread_columns(lo, step * group, group)
        high = spread_columns(hi, step * group, group)
        onehot = jnp.concatenate(
            [jnp.where(low == lane + b * E, 1.0, 0.0).astype(BF) for b in range(LO // E)], axis=1
        )
        if step == 0:
            for load in loads:
                load.wait()
        picked = dot(onehot, jnp.concatenate([table[slab, :] for slab in slabs], axis=1))
        out = jnp.zeros((size, E), F32)
        for h in range(HI):
            out = jnp.where(high == h, picked[:, h * E : (h + 1) * E], out)
        rows = slice(step * size, (step + 1) * size)
        found[rows, :] = out.astype(BF)
        sends.append(
            pltpu.make_async_copy(found.at[rows, :], found_far.at[rows, :], sems.at[HI + step])
        )
        sends[-1].start()
    for send in sends:
        send.wait()
    keep.wait()


def gather(asked, table):
    return pl.pallas_call(
        gather_kernel,
        out_shape=(slow((NDEV * SLOTS, E), BF), slow((NDEV, E), jnp.int32)),
        in_specs=[VMEM_SPEC, ANY_SPEC],
        out_specs=[ANY_SPEC] * 2,
        scratch_shapes=[
            pltpu.VMEM((ROWS, E), BF),
            pltpu.VMEM((NDEV * SLOTS, E), BF),
            pltpu.SemaphoreType.DMA((HI + 5,)),
        ],
        compiler_params=params(),
        cost_estimate=pl.CostEstimate(
            flops=2 * NDEV * SLOTS * ROWS * E, bytes_accessed=2 * 10**6, transcendentals=0
        ),
        name="gather_rows",
    )(*in_vmem(asked), *in_hbm(table))


HALVES = 2


def scatter_kernel(half, asked, incoming, *refs):
    grad, spread = refs[-2:]
    rows = slot_rows(asked, NDEV // 4)
    hi = slot_columns(rows) >> (LO.bit_length() - 1)
    group = 2
    size = group * E
    for first in range(0, NDEV // 4, group):
        high = spread_columns(hi, first, group)
        part = incoming[first * E : first * E + size, :].astype(F32)
        for h in range(HI):
            spread[first * E : first * E + size, h * E : (h + 1) * E] = jnp.where(
                high == h, part, 0.0
            ).astype(BF)
    size = LO // HALVES
    sub = iota((size, E), 0) + half * size
    lo = rows & (LO - 1)
    onehot = jnp.concatenate(
        [jnp.where(sub == lo[i : i + 1, :], 1.0, 0.0).astype(BF) for i in range(NDEV // 4)], axis=1
    )
    total = dot(onehot, spread[...])
    for h in range(HI):
        grad[h] = total[:, h * E : (h + 1) * E]


def scatter(half, asked, incoming, before=()):
    count = NDEV * SLOTS
    return pl.pallas_call(
        functools.partial(scatter_kernel, half),
        grid=(1,),
        out_shape=slow((HI, LO, E), F32),
        in_specs=[whole((NDEV, E)), whole((count, E))] + [ANY_SPEC] * len(before),
        out_specs=pl.BlockSpec((HI, LO // HALVES, E), lambda i: (0, half, 0)),
        scratch_shapes=[pltpu.VMEM((count, HI * E), BF)],
        input_output_aliases={2 + i: i for i in range(len(before))},
        compiler_params=params(),
        cost_estimate=pl.CostEstimate(
            flops=count * ROWS * E, bytes_accessed=2 * 10**6, transcendentals=0
        ),
        name="scatter_rows",
    )(asked, incoming, *in_hbm(*before))


def head_masks():
    lane = iota((1, 2 * HEAD_DIM), 1)
    return [
        jnp.where(lane < HEAD_DIM, 1.0, 0.0).astype(BF),
        jnp.where(lane >= HEAD_DIM, 1.0, 0.0).astype(BF),
    ]


def act(u, mask):
    w = jnp.where(mask, 1.0 + jnp.tanh(u), 0.0)
    p = u * w
    return p.astype(BF), (w + p * (2.0 - w)).astype(BF)


def near_forward_kernel(lengths, q, k, v, halo, probs, slope, attn):
    base = lax.axis_index("seq") * NBD
    length = lengths[lax.axis_index("user")]
    masks = head_masks()
    q16 = q[...] * jnp.asarray(1.0 / 16.0, BF)
    kx = jnp.concatenate([halo[0], k[...]], axis=0)
    vx = jnp.concatenate([halo[1], v[...]], axis=0)
    lane = iota((BLK, 2 * BLK), 1)
    sub = iota((BLK, 2 * BLK), 0)
    vx_m = [vx * m for m in masks]
    both = [jnp.concatenate([q16[i * BLK : (i + 1) * BLK] * m for m in masks]) for i in range(NBD)]
    logits = [dot_nt(both[i], kx[i * BLK : (i + 2) * BLK]) for i in range(NBD)]
    held = []
    for i in range(NBD):
        rows = slice(i * BLK, (i + 1) * BLK)
        at = (base + i - 1) * BLK + lane
        mask = (at >= 0) & (at < length) & (lane <= sub + BLK)
        parts = []
        for h in range(2):
            p, f = act(logits[i][h * BLK : (h + 1) * BLK], mask)
            probs[h, rows, :] = p
            slope[h, rows, :] = f
            parts.append(p)
        held.append(jnp.concatenate(parts, axis=1))
    for i in range(NBD):
        keys = slice(i * BLK, (i + 2) * BLK)
        attn[i * BLK : (i + 1) * BLK, :] = dot(
            held[i], jnp.concatenate([m[keys] for m in vx_m], axis=0)
        )


def unrotate(parts, scratch):
    for d in range(CHUNKS):
        scratch[chunk_of(CHUNKS - d)] = parts[d][...]
    keys = jnp.concatenate([scratch[g] for g in range(GLOB)], axis=0)
    values = jnp.concatenate([scratch[GLOB + g] for g in range(GLOB)], axis=0)
    return keys, values


def far_forward_kernel(
    lengths,
    gids,
    q,
    glob0,
    glob1,
    glob2,
    glob3,
    near,
    gate,
    history,
    w_out,
    probs,
    slope,
    normed_out,
    inv_out,
    user,
    attn,
    scratch,
):
    pair = pl.program_id(0)
    base = lax.axis_index("seq") * NBD
    length = lengths[lax.axis_index("user")]
    masks = head_masks()
    q16 = q[...] * jnp.asarray(1.0 / 16.0, BF)
    kg, vg = unrotate((glob0, glob1, glob2, glob3), scratch)
    lane = iota((BLK, 2 * BLK), 1)
    gid = jnp.where(lane < BLK, gids[0, 0], gids[0, 1])
    at = gid * BLK + lane % BLK
    vg_both = jnp.concatenate([vg * m for m in masks], axis=0)
    logits = dot_nt(jnp.concatenate([q16 * m for m in masks], axis=0), kg)
    held = []
    for i in range(NBD):
        rows = slice(i * BLK, (i + 1) * BLK)
        mask = (gid < base + i - 1) & (at < length)
        parts = []
        for h in range(2):
            p, f = act(logits[h * EVENTS + i * BLK : h * EVENTS + (i + 1) * BLK], mask)
            probs[h, rows, :] = p
            slope[h, rows, :] = f
            parts.append(p)
        held.append(jnp.concatenate(parts, axis=1))
    attn[pair] = near[...] + dot(jnp.concatenate(held, axis=0), vg_both)

    @pl.when(pair == PAIRS - 1)
    def _():
        step = 128
        for r in range(0, EVENTS, step):
            rows = slice(r, r + step)
            x = jnp.concatenate([attn[p, rows, :] for p in range(PAIRS)], axis=1)
            centered = x - jnp.mean(x, axis=1, keepdims=True)
            var = jnp.mean(centered * centered, axis=1, keepdims=True)
            inv = lax.rsqrt(var + 1e-05)
            normed = centered * inv
            normed_out[rows, :] = normed
            inv_out[rows, :] = inv
            gated = (normed * gate[rows, :].astype(F32)).astype(BF)
            user[rows, :] = (dot(gated, w_out[...]) + history[rows, :].astype(F32)).astype(BF)


def pair_block(rows):
    return pl.BlockSpec((rows, 2 * HEAD_DIM), lambda p: (0, p))


def pair_stack(rows):
    return pl.BlockSpec((2, rows, 2 * HEAD_DIM), lambda p: (0, 0, p))


def head_block():
    return pl.BlockSpec((2, EVENTS, 2 * BLK), lambda p: (p, 0, 0))


SQUARE = slow((HEADS, EVENTS, 2 * BLK), BF)


def near_forward(lengths, q, k, v, halo):
    return pl.pallas_call(
        near_forward_kernel,
        grid=(PAIRS,),
        out_shape=(SQUARE, SQUARE, fast((EVENTS, D), F32)),
        in_specs=[SMEM_SPEC] + [pair_block(EVENTS)] * 3 + [pair_stack(BLK)],
        out_specs=[head_block(), head_block(), pair_block(EVENTS)],
        compiler_params=params(),
        cost_estimate=pl.CostEstimate(
            flops=5 * 10**8, bytes_accessed=7 * 10**6, transcendentals=10**6
        ),
        name="near_forward",
    )(*in_hbm(lengths), q, k, v, halo)


def far_forward(lengths, gids, q, glob, near, gate, history, w_out):
    return pl.pallas_call(
        far_forward_kernel,
        grid=(PAIRS,),
        out_shape=(
            SQUARE,
            SQUARE,
            slow((EVENTS, D), F32),
            slow((EVENTS, 1), F32),
            slow((EVENTS, E), BF),
        ),
        in_specs=[SMEM_SPEC] * 2
        + [pair_block(EVENTS)]
        + [pair_block(BLK)] * CHUNKS
        + [pair_block(EVENTS)]
        + [whole((EVENTS, D)), whole((EVENTS, E)), whole((D, E))],
        out_specs=[
            head_block(),
            head_block(),
            whole((EVENTS, D)),
            whole((EVENTS, 1)),
            whole((EVENTS, E)),
        ],
        scratch_shapes=[
            pltpu.VMEM((PAIRS, EVENTS, 2 * HEAD_DIM), F32),
            pltpu.VMEM((CHUNKS, BLK, 2 * HEAD_DIM), BF),
        ],
        compiler_params=params(),
        cost_estimate=pl.CostEstimate(
            flops=6 * 10**8, bytes_accessed=9 * 10**6, transcendentals=10**6
        ),
        name="far_forward",
    )(*in_hbm(lengths, gids), q, *glob, *in_vmem(near), *in_hbm(gate, history, w_out))


def far_backward_kernel(
    q, glob0, glob1, glob2, glob3, grad, probs, slope, d_q, out0, out1, out2, out3, scratch
):
    masks = head_masks()
    sixteenth = jnp.asarray(1.0 / 16.0, BF)
    q16 = q[...] * sixteenth
    kg, vg = unrotate((glob0, glob1, glob2, glob3), scratch)
    do = grad[...]
    q_t = jnp.concatenate([(q16 * m).T for m in masks], axis=1)
    do_t = jnp.concatenate([(do * m).T for m in masks], axis=1)
    kg_both = jnp.concatenate([kg * (m * sixteenth) for m in masks], axis=0)
    d_probs = dot_nt(jnp.concatenate([do * m for m in masks], axis=0), vg)
    ds = [
        (d_probs[h * EVENTS : (h + 1) * EVENTS] * slope[h].astype(F32)).astype(BF) for h in range(2)
    ]
    d_q[...] = dot(jnp.concatenate(ds, axis=1), kg_both)
    d_k = dot(q_t, jnp.concatenate(ds, axis=0)).T.astype(BF)
    d_v = dot(do_t, jnp.concatenate([probs[0], probs[1]], axis=0)).T.astype(BF)
    for g in range(GLOB):
        scratch[g] = d_k[g * BLK : (g + 1) * BLK]
        scratch[GLOB + g] = d_v[g * BLK : (g + 1) * BLK]
    for d, out in enumerate((out0, out1, out2, out3)):
        out[...] = scratch[chunk_of(d)]


def far_backward(q, glob, grad, probs, slope):
    return pl.pallas_call(
        far_backward_kernel,
        grid=(PAIRS,),
        out_shape=(fast((EVENTS, D), F32),)
        + (jax.ShapeDtypeStruct((BLK, D), BF),) * CHUNKS,
        in_specs=[pair_block(EVENTS)]
        + [pair_block(BLK)] * CHUNKS
        + [pair_block(EVENTS)]
        + [head_block()] * 2,
        out_specs=[pair_block(EVENTS)] + [pair_block(BLK)] * CHUNKS,
        scratch_shapes=[pltpu.VMEM((CHUNKS, BLK, 2 * HEAD_DIM), BF)],
        compiler_params=params(),
        cost_estimate=pl.CostEstimate(
            flops=10**9, bytes_accessed=7 * 10**6, transcendentals=0
        ),
        name="far_backward",
    )(*in_hbm(q), *glob, *in_hbm(grad, probs, slope))


def near_backward_kernel(q, k, v, halo, grad, probs, slope, far, d_q, d_k, d_v, edge):
    masks = head_masks()
    sixteenth = jnp.asarray(1.0 / 16.0, BF)
    q16 = q[...] * sixteenth
    kx = jnp.concatenate([halo[0], k[...]], axis=0)
    vx = jnp.concatenate([halo[1], v[...]], axis=0)
    do = grad[...]
    q_t = [(q16 * m).T for m in masks]
    do_t = [(do * m).T for m in masks]
    kx_m = [kx * (m * sixteenth) for m in masks]
    blocks = [slice(i * BLK, (i + 1) * BLK) for i in range(NBD)]
    windows = [slice(i * BLK, (i + 2) * BLK) for i in range(NBD)]
    d_probs = [
        dot_nt(jnp.concatenate([do[blocks[i]] * m for m in masks], axis=0), vx[windows[i]])
        for i in range(NBD)
    ]
    all_ds = [
        [
            (d_probs[i][h * BLK : (h + 1) * BLK] * slope[h, blocks[i], :].astype(F32)).astype(BF)
            for h in range(2)
        ]
        for i in range(NBD)
    ]
    carry = None
    for i in range(NBD):
        rows, keys, ds = blocks[i], windows[i], all_ds[i]
        near_k = jnp.concatenate([m[keys] for m in kx_m], axis=0)
        d_q[rows, :] = (far[rows, :] + dot(jnp.concatenate(ds, axis=1), near_k)).astype(BF)
        near_p = jnp.concatenate([probs[h, rows, :] for h in range(2)], axis=0)
        dk = dot(jnp.concatenate([t[:, rows] for t in q_t], axis=1), jnp.concatenate(ds, axis=0)).T
        dv = dot(jnp.concatenate([t[:, rows] for t in do_t], axis=1), near_p).T
        if i == 0:
            edge[0] = dk[:BLK].astype(BF)
            edge[1] = dv[:BLK].astype(BF)
        else:
            last = slice((i - 1) * BLK, i * BLK)
            d_k[last, :] = (carry[0] + dk[:BLK]).astype(BF)
            d_v[last, :] = (carry[1] + dv[:BLK]).astype(BF)
        carry = (dk[BLK:], dv[BLK:])
    last = slice((NBD - 1) * BLK, NBD * BLK)
    d_k[last, :] = carry[0].astype(BF)
    d_v[last, :] = carry[1].astype(BF)


def near_backward(q, k, v, halo, grad, probs, slope, far):
    rows = jax.ShapeDtypeStruct((EVENTS, D), BF)
    return pl.pallas_call(
        near_backward_kernel,
        grid=(PAIRS,),
        out_shape=(
            rows,
            slow((EVENTS, D), BF),
            slow((EVENTS, D), BF),
            jax.ShapeDtypeStruct((2, BLK, D), BF),
        ),
        in_specs=[pair_block(EVENTS)] * 3
        + [pair_stack(BLK), pair_block(EVENTS)]
        + [head_block()] * 2
        + [pair_block(EVENTS)],
        out_specs=[pair_block(EVENTS)] * 3 + [pair_stack(BLK)],
        compiler_params=params(),
        cost_estimate=pl.CostEstimate(
            flops=10**9, bytes_accessed=9 * 10**6, transcendentals=0
        ),
        name="near_backward",
    )(q, k, v, halo, grad, probs, slope, *in_vmem(far))


def middle_kernel(
    lengths,
    items,
    code,
    user,
    normed_far,
    gate_far,
    inv_far,
    w_far,
    out_far,
    attn_far,
    gated_far,
    score,
    normed,
    gate,
    inv,
    w_out,
    outgoing,
    d_attn,
    d_gate,
    sems,
):
    loads = [
        pltpu.make_async_copy(normed_far, normed, sems.at[0]),
        pltpu.make_async_copy(gate_far, gate, sems.at[1]),
        pltpu.make_async_copy(inv_far, inv, sems.at[2]),
        pltpu.make_async_copy(w_far, w_out, sems.at[3]),
    ]
    for load in loads:
        load.start()
    sends = []

    def send(near, far, rows):
        copy = pltpu.make_async_copy(near.at[rows, :], far.at[rows, :], sems.at[4 + len(sends)])
        copy.start()
        sends.append(copy)

    portion = NDEV * SLOTS // 4
    user_b = user[...]
    user_t = user_b.T
    mark = code[...].astype(F32)
    first = mark >= FIRST
    rank = jnp.where(first, mark - FIRST, mark)
    group = 8
    size = group * SLOTS
    slot = iota((SLOTS, EVENTS), 0).astype(F32)
    for d in range(0, NDEV, group):
        s = dot(items[d * SLOTS : d * SLOTS + size, :], user_t)
        for r in range(group):
            own = rank[d + r : d + r + 1, :] == slot
            part = jnp.where(own, s[r * SLOTS : (r + 1) * SLOTS, :], 0.0)
            score[d + r : d + r + 1, :] = jnp.sum(part, axis=0, keepdims=True)
    score0 = jnp.sum(jnp.where(first, score[...], 0.0), axis=0, keepdims=True)
    event = lax.axis_index("seq") * EVENTS + iota((1, EVENTS), 1)
    valid = jnp.where(event < lengths[lax.axis_index("user")], 1.0, 0.0)
    other = (rank >= 0.0) & jnp.logical_not(first)
    side = jnp.where(other, jax.nn.sigmoid(score[...] - score0), 0.0) * valid
    coef = jnp.where(first, -jnp.sum(side, axis=0, keepdims=True), side)
    d_user_t = jnp.zeros((E, EVENTS), F32)
    for d in range(0, NDEV, group):
        c = jnp.concatenate(
            [
                jnp.where(rank[r : r + 1, :] == slot, coef[r : r + 1, :], 0.0).astype(BF)
                for r in range(d, d + group)
            ],
            axis=0,
        )
        rows = slice(d * SLOTS, d * SLOTS + size)
        outgoing[rows, :] = dot(c, user_b).astype(BF)
        d_user_t = d_user_t + dot_tn(items[rows, :], c)
        if rows.stop % portion == 0:
            send(outgoing, out_far, slice(rows.stop - portion, rows.stop))
    d_user = d_user_t.T.astype(BF)
    for load in loads:
        load.wait()
    step = 128
    for r in range(0, EVENTS, step):
        rows = slice(r, r + step)
        d_gated = dot_nt(d_user[rows], w_out[...])
        n = normed[rows, :]
        d_gate[rows, :] = (d_gated * n).astype(BF)
        dn = d_gated * gate[rows, :].astype(F32)
        d_attn[rows, :] = (
            (
                dn
                - jnp.mean(dn, axis=1, keepdims=True)
                - n * jnp.mean(dn * n, axis=1, keepdims=True)
            )
            * inv[rows, :]
        ).astype(BF)
        send(d_attn, attn_far, rows)
        send(d_gate, gated_far, rows)
    for copy in sends:
        copy.wait()


def middle(lengths, items, code, user, normed, inv, gate, w_out):
    return pl.pallas_call(
        middle_kernel,
        out_shape=(
            slow((NDEV * SLOTS, E), BF),
            slow((EVENTS, D), BF),
            slow((EVENTS, D), BF),
        ),
        in_specs=[SMEM_SPEC] + [VMEM_SPEC] * 3 + [ANY_SPEC] * 4,
        out_specs=[ANY_SPEC] * 3,
        scratch_shapes=[
            pltpu.VMEM((NDEV, EVENTS), F32),
            pltpu.VMEM((EVENTS, D), F32),
            pltpu.VMEM((EVENTS, D), BF),
            pltpu.VMEM((EVENTS, 1), F32),
            pltpu.VMEM((D, E), BF),
            pltpu.VMEM((NDEV * SLOTS, E), BF),
            pltpu.VMEM((EVENTS, D), BF),
            pltpu.VMEM((EVENTS, D), BF),
            pltpu.SemaphoreType.DMA((4 + 4 + 2 * EVENTS // 128,)),
        ],
        compiler_params=params(),
        cost_estimate=pl.CostEstimate(
            flops=2 * 10**9, bytes_accessed=6 * 10**6, transcendentals=10**5
        ),
        name="ranking",
    )(*in_hbm(lengths), *in_vmem(items), *in_hbm(code, user, normed, gate, inv, w_out))


def finish_kernel(gids, d_k, d_v, edge, glob0, glob1, glob2, glob3, key_out, value_out):
    seq = lax.axis_index("seq")
    outs = (key_out, value_out)
    for which, mine in enumerate((d_k, d_v)):
        outs[which][...] = mine[...]
        tail = slice(EVENTS - BLK, EVENTS)
        outs[which][tail, :] = (mine[tail, :].astype(F32) + edge[which].astype(F32)).astype(BF)
    for d, more in enumerate((glob0, glob1, glob2, glob3)):
        c = chunk_of(CHUNKS - d)
        gid = gids[0, c % GLOB]
        place = pl.ds(pl.multiple_of((gid % NBD) * BLK, BLK), BLK)
        for which in range(2):

            @pl.when((gid // NBD == seq) & (c // GLOB == which))
            def _():
                out = outs[which]
                out[place, :] = (out[place, :].astype(F32) + more[...].astype(F32)).astype(BF)


def finish(gids, d_k, d_v, edge, total):
    rows = jax.ShapeDtypeStruct((EVENTS, D), BF)
    return pl.pallas_call(
        finish_kernel,
        out_shape=(rows, rows),
        in_specs=[SMEM_SPEC] + [VMEM_SPEC] * (3 + CHUNKS),
        out_specs=[VMEM_SPEC] * 2,
        compiler_params=params(),
        cost_estimate=pl.CostEstimate(flops=10**6, bytes_accessed=3 * 10**6, transcendentals=0),
        name="add_received",
    )(*in_hbm(gids), d_k, d_v, edge, *total)


def from_behind(block, axis, distance):
    size = lax.axis_size(axis)
    return lax.ppermute(block, axis, [(i, (i + distance) % size) for i in range(size)])


def exchange(x, axis):
    return lax.all_to_all(x, axis, split_axis=0, concat_axis=0, tiled=True)


def around_x(x, distance):
    pairs = [(i, i // XSIZE * XSIZE + (i + distance) % XSIZE) for i in range(NSEQ)]
    return lax.ppermute(x, "seq", pairs)


def around_z(x, distance):
    return lax.ppermute(x, "seq", [(i, (i + distance * XSIZE) % NSEQ) for i in range(NSEQ)])


def add_all(parts):
    return sum(p.astype(F32) for p in parts).astype(BF)


def from_x(chunks):
    return [chunks[0]] + [around_x(chunks[d], d) for d in range(1, CHUNKS)]


def from_z(mine):
    return [mine] + [around_z(mine, d) for d in range(1, NSEQ // XSIZE)]


def share_x(mine):
    return [mine] + [around_x(mine, d) for d in range(1, CHUNKS)]


def together(*values):
    return lax.optimization_barrier(values)


def on_device(
    query, key, value, gate, history, w_out, table, item_owner, item_row, gids, lengths
):
    q, k, v = query[0], key[0], value[0]
    owner = jnp.transpose(item_owner, (2, 0, 1))
    row = jnp.transpose(item_row, (2, 0, 1))
    tail, *cand = pieces(gids, k, v)
    parts = from_x(cand)
    owner, _ = together(owner, cand[0])
    req, code = route(owner, row)
    tail, _ = together(tail, req)
    halo = from_behind(tail, "seq", 1)
    req, *parts = together(req, *parts)
    mine = add_all(parts)
    parts = from_z(mine)
    req, halo, _ = together(req, halo, mine)
    asked = exchange(req.reshape(NDEV, 1, E), ("seq", "user")).reshape(NDEV, E)
    mine = add_all(parts)
    glob = share_x(mine)
    asked, _ = together(asked, mine)
    found, asked = gather(asked, table)
    found, *glob = together(found, *glob)
    items = exchange(found.reshape(NDEV, SLOTS, E), ("seq", "user")).reshape(NDEV * SLOTS, E)
    near_p, near_f, near = near_forward(lengths, q, k, v, halo)
    far_p, far_f, normed, inv, user = far_forward(
        lengths, gids, q, glob, near, gate[0], history[0], w_out
    )
    outgoing, d_attn, d_gate = middle(lengths, items, code, user, normed, inv, gate[0], w_out)
    incoming = exchange(outgoing.reshape(NDEV, SLOTS, E), ("seq", "user"))
    far_q, *d_glob = far_backward(q, glob, d_attn, far_p, far_f)
    parts = from_x(d_glob)
    d_q, d_k, d_v, edge = near_backward(q, k, v, halo, d_attn, near_p, near_f, far_q)
    d_k, *parts = together(d_k, *parts)
    mine = add_all(parts)
    back = from_behind(edge, "seq", -1)
    incoming, mine = together(incoming.reshape(NDEV * SLOTS, E), mine)
    grad = scatter(0, asked, incoming)
    grad, *parts = together(grad, *from_z(mine))
    mine = add_all(parts)
    grad, mine = together(grad, mine)
    grad = scatter(1, asked, incoming, (grad,))
    grad, *total = together(grad, *share_x(mine))
    d_key, d_value = finish(gids, d_k, d_v, back, total)
    return (d_q[None], d_key[None], d_value[None], d_gate[None], grad.reshape(ROWS, E))


def solution(mesh):
    return jax.shard_map(
        on_device,
        mesh=mesh,
        in_specs=(
            P("user", "seq", None),
            P("user", "seq", None),
            P("user", "seq", None),
            P("user", "seq", None),
            P("user", "seq", None),
            P(),
            P(("seq", "user"), None),
            P("user", "seq", None),
            P("user", "seq", None),
            P("user", None),
            P(),
        ),
        out_specs=(
            P("user", "seq", None),
            P("user", "seq", None),
            P("user", "seq", None),
            P("user", "seq", None),
            P(("seq", "user"), None),
        ),
        check_vma=False,
    )
```

```python
import functools

import jax
import jax.numpy as jnp
from jax import lax
from jax.experimental import pallas as pl
from jax.experimental.pallas import tpu as pltpu
from jax.sharding import PartitionSpec as P

HEADS = 8
HEAD_DIM = 64
D = 512
E = 128
BLK = 128
GLOB = 2
ITEMS = 5
EVENTS = 512
NBD = EVENTS // BLK
PAIRS = HEADS // 2
NDEV = 128
NSEQ = 16
CHUNKS = 2 * GLOB
ROWS = 4096
SLOTS = 32
FIRST = 64.0
HI = 4
LO = ROWS // HI
BF = jnp.bfloat16
F32 = jnp.float32
VMEM_LIMIT = 24 * 1024 * 1024
SMEM_SPEC = pl.BlockSpec(memory_space=pltpu.SMEM)
VMEM_SPEC = pl.BlockSpec(memory_space=pltpu.VMEM)
ANY_SPEC = pl.BlockSpec(memory_space=pl.ANY)
XSIZE = 4


def dot(a, b):
    return jnp.dot(a, b, preferred_element_type=F32)


def dot_nt(a, b):
    return lax.dot_general(a, b, (((1,), (1,)), ((), ())), preferred_element_type=F32)


def dot_tn(a, b):
    return lax.dot_general(a, b, (((0,), (0,)), ((), ())), preferred_element_type=F32)


def params(**more):
    return pltpu.CompilerParams(vmem_limit_bytes=VMEM_LIMIT, **more)


def fast(shape, dtype):
    return pltpu.VMEM(shape, dtype)


def slow(shape, dtype):
    return pltpu.HBM(shape, dtype)


def in_vmem(*arrays):
    return [pltpu.with_memory_space_constraint(x, pltpu.VMEM) for x in arrays]


def in_hbm(*arrays):
    return [pltpu.with_memory_space_constraint(x, pltpu.HBM) for x in arrays]


def whole(shape):
    return pl.BlockSpec(shape, lambda *_: (0,) * len(shape))


def iota(shape, dim):
    return lax.broadcasted_iota(jnp.int32, shape, dim)


def chunk_of(shift):
    return (lax.axis_index("seq") + shift) % XSIZE


def pieces_kernel(gids, key, value, halo, cand0, cand1, cand2, cand3, sems):
    seq = lax.axis_index("seq")
    tail = pl.ds(EVENTS - BLK, BLK)
    tails = [
        pltpu.make_async_copy(src.at[tail, :], halo.at[i], sems.at[CHUNKS + i])
        for i, src in enumerate((key, value))
    ]
    for copy in tails:
        copy.start()
    cases = []
    for d, out in enumerate((cand0, cand1, cand2, cand3)):
        c = chunk_of(d)
        gid = gids[0, c % GLOB]
        place = pl.ds(pl.multiple_of((gid % NBD) * BLK, BLK), BLK)
        held = gid // NBD == seq
        for i, src in enumerate((key, value)):
            copy = pltpu.make_async_copy(src.at[place, :], out, sems.at[d])
            cases.append((held & (c // GLOB == i), copy))

        @pl.when(jnp.logical_not(held))
        def _():
            out[...] = jnp.zeros((BLK, D), BF)

    for case, copy in cases:

        @pl.when(case)
        def _():
            copy.start()

    for case, copy in cases:

        @pl.when(case)
        def _():
            copy.wait()

    for copy in tails:
        copy.wait()


def pieces(gids, key, value):
    return pl.pallas_call(
        pieces_kernel,
        out_shape=(jax.ShapeDtypeStruct((2, BLK, D), BF),)
        + (jax.ShapeDtypeStruct((BLK, D), BF),) * CHUNKS,
        in_specs=[SMEM_SPEC] + [ANY_SPEC] * 2,
        out_specs=[VMEM_SPEC] * (1 + CHUNKS),
        scratch_shapes=[pltpu.SemaphoreType.DMA((CHUNKS + 2,))],
        compiler_params=params(),
        cost_estimate=pl.CostEstimate(flops=10**6, bytes_accessed=2 * 10**6, transcendentals=0),
        name="pieces",
    )(*in_hbm(gids, key, value))


def route_kernel(owner, row, req, code):
    dev = iota((NDEV, EVENTS), 0)
    rows = jnp.full((NDEV, EVENTS), -1, jnp.int32)
    for j in range(ITEMS):
        rows = jnp.where(owner[j] == dev, row[j], rows)
    hit = rows >= 0
    before = jnp.where(iota((EVENTS, EVENTS), 0) < iota((EVENTS, EVENTS), 1), 1.0, 0.0).astype(BF)
    rank = dot(jnp.where(hit, 1.0, 0.0).astype(BF), before)
    rank = jnp.where(hit, rank, -1.0)
    code[...] = jnp.where(owner[0] == dev, rank + FIRST, rank).astype(BF)
    plus = (rows + 1).astype(F32)
    lane = iota((NDEV, E), 1) - (lax.axis_index("user") % (E // SLOTS)) * SLOTS
    asked = jnp.zeros((NDEV, E), F32)
    for k in range(SLOTS):
        column = jnp.sum(jnp.where(rank == k, plus, 0.0), axis=1, keepdims=True)
        asked = jnp.where(lane == k, column, asked)
    req[...] = asked.astype(jnp.int32)


def route(owner, row):
    return pl.pallas_call(
        route_kernel,
        out_shape=(
            slow((NDEV, E), jnp.int32),
            slow((NDEV, EVENTS), BF),
        ),
        in_specs=[VMEM_SPEC] * 2,
        out_specs=[VMEM_SPEC] * 2,
        compiler_params=params(),
        cost_estimate=pl.CostEstimate(flops=10**8, bytes_accessed=10**6, transcendentals=0),
        name="route",
    )(*in_hbm(owner, row))


def slot_rows(asked, count):
    rows = asked[pl.ds(0, count, stride=4), :]
    for j in range(1, 4):
        rows = rows + asked[pl.ds(j, count, stride=4), :]
    return rows - 1


def slot_columns(rows):
    count = rows.shape[0]
    full = jnp.concatenate([rows.astype(F32), jnp.zeros((E - count, E), F32)], axis=0)
    return full.T[:, :count].astype(jnp.int32)


def spread_columns(x, first, count):
    return jnp.concatenate(
        [jnp.broadcast_to(x[:, i : i + 1], (E, E)) for i in range(first, first + count)], axis=0
    )


def gather_kernel(asked, table_far, found_far, kept, table, found, sems):
    slabs = [slice(h * LO, (h + 1) * LO) for h in range(HI)]
    loads = [
        pltpu.make_async_copy(table_far.at[slab, :], table.at[slab, :], sems.at[h])
        for h, slab in enumerate(slabs)
    ]
    for load in loads:
        load.start()
    keep = pltpu.make_async_copy(asked, kept, sems.at[HI + 8])
    keep.start()
    columns = slot_columns(slot_rows(asked, NDEV // 4))
    lo = columns & (LO - 1)
    hi = columns >> (LO.bit_length() - 1)
    group = 4
    size = group * E
    lane = iota((size, E), 1)
    sends = []
    for step in range(NDEV // 4 // group):
        low = spread_columns(lo, step * group, group)
        high = spread_columns(hi, step * group, group)
        onehot = jnp.concatenate(
            [jnp.where(low == lane + b * E, 1.0, 0.0).astype(BF) for b in range(LO // E)], axis=1
        )
        if step == 0:
            for load in loads:
                load.wait()
        picked = dot(onehot, jnp.concatenate([table[slab, :] for slab in slabs], axis=1))
        out = jnp.zeros((size, E), F32)
        for h in range(HI):
            out = jnp.where(high == h, picked[:, h * E : (h + 1) * E], out)
        rows = slice(step * size, (step + 1) * size)
        found[rows, :] = out.astype(BF)
        sends.append(
            pltpu.make_async_copy(found.at[rows, :], found_far.at[rows, :], sems.at[HI + step])
        )
        sends[-1].start()
    for send in sends:
        send.wait()
    keep.wait()


def gather(asked, table):
    return pl.pallas_call(
        gather_kernel,
        out_shape=(slow((NDEV * SLOTS, E), BF), slow((NDEV, E), jnp.int32)),
        in_specs=[VMEM_SPEC, ANY_SPEC],
        out_specs=[ANY_SPEC] * 2,
        scratch_shapes=[
            pltpu.VMEM((ROWS, E), BF),
            pltpu.VMEM((NDEV * SLOTS, E), BF),
            pltpu.SemaphoreType.DMA((HI + 9,)),
        ],
        compiler_params=params(),
        cost_estimate=pl.CostEstimate(
            flops=2 * NDEV * SLOTS * ROWS * E, bytes_accessed=2 * 10**6, transcendentals=0
        ),
        name="gather_rows",
    )(*in_vmem(asked), *in_hbm(table))


PORTION = LO // 2


def scatter_kernel(start, asked, incoming, *refs):
    grad, spread = refs[-2:]
    step = pl.program_id(0)
    rows = slot_rows(asked, NDEV // 4)
    @pl.when(step == 0)
    def _():
        hi = slot_columns(rows) >> (LO.bit_length() - 1)
        group = 2
        size = group * E
        for first in range(0, NDEV // 4, group):
            high = spread_columns(hi, first, group)
            part = incoming[first * E : first * E + size, :].astype(F32)
            for h in range(HI):
                spread[first * E : first * E + size, h * E : (h + 1) * E] = jnp.where(
                    high == h, part, 0.0
                ).astype(BF)

    size = PORTION
    sub = iota((size, E), 0) + (start + step) * size
    lo = rows & (LO - 1)
    onehot = jnp.concatenate(
        [jnp.where(sub == lo[i : i + 1, :], 1.0, 0.0).astype(BF) for i in range(NDEV // 4)], axis=1
    )
    total = dot(onehot, spread[...])
    for h in range(HI):
        grad[h] = total[:, h * E : (h + 1) * E]


def scatter(start, steps, asked, incoming, before=()):
    count = NDEV * SLOTS
    return pl.pallas_call(
        functools.partial(scatter_kernel, start),
        grid=(steps,),
        out_shape=slow((HI, LO, E), F32),
        in_specs=[whole((NDEV, E)), whole((count, E))] + [ANY_SPEC] * len(before),
        out_specs=pl.BlockSpec((HI, PORTION, E), lambda i: (0, start + i, 0)),
        scratch_shapes=[pltpu.VMEM((count, HI * E), BF)],
        input_output_aliases={2 + i: i for i in range(len(before))},
        compiler_params=params(),
        cost_estimate=pl.CostEstimate(
            flops=count * ROWS * E, bytes_accessed=2 * 10**6, transcendentals=0
        ),
        name="scatter_rows",
    )(asked, incoming, *in_hbm(*before))


def head_masks():
    lane = iota((1, 2 * HEAD_DIM), 1)
    return [
        jnp.where(lane < HEAD_DIM, 1.0, 0.0).astype(BF),
        jnp.where(lane >= HEAD_DIM, 1.0, 0.0).astype(BF),
    ]


def act(u, mask):
    w = jnp.where(mask, 1.0 + jnp.tanh(u), 0.0)
    p = u * w
    return p.astype(BF), (w + p * (2.0 - w)).astype(BF)


def near_forward_kernel(lengths, q, k, v, halo, probs, slope, attn):
    base = lax.axis_index("seq") * NBD
    length = lengths[lax.axis_index("user")]
    masks = head_masks()
    q16 = q[...] * jnp.asarray(1.0 / 16.0, BF)
    kx = jnp.concatenate([halo[0], k[...]], axis=0)
    vx = jnp.concatenate([halo[1], v[...]], axis=0)
    lane = iota((BLK, 2 * BLK), 1)
    sub = iota((BLK, 2 * BLK), 0)
    vx_m = [vx * m for m in masks]
    both = [jnp.concatenate([q16[i * BLK : (i + 1) * BLK] * m for m in masks]) for i in range(NBD)]
    logits = [dot_nt(both[i], kx[i * BLK : (i + 2) * BLK]) for i in range(NBD)]
    held = []
    for i in range(NBD):
        rows = slice(i * BLK, (i + 1) * BLK)
        at = (base + i - 1) * BLK + lane
        mask = (at >= 0) & (at < length) & (lane <= sub + BLK)
        parts = []
        for h in range(2):
            p, f = act(logits[i][h * BLK : (h + 1) * BLK], mask)
            probs[h, rows, :] = p
            slope[h, rows, :] = f
            parts.append(p)
        held.append(jnp.concatenate(parts, axis=1))
    for i in range(NBD):
        keys = slice(i * BLK, (i + 2) * BLK)
        attn[i * BLK : (i + 1) * BLK, :] = dot(
            held[i], jnp.concatenate([m[keys] for m in vx_m], axis=0)
        )


def unrotate(parts, scratch):
    for d in range(CHUNKS):
        scratch[chunk_of(CHUNKS - d)] = parts[d][...]
    keys = jnp.concatenate([scratch[g] for g in range(GLOB)], axis=0)
    values = jnp.concatenate([scratch[GLOB + g] for g in range(GLOB)], axis=0)
    return keys, values


def far_forward_kernel(
    lengths,
    gids,
    q,
    glob0,
    glob1,
    glob2,
    glob3,
    near,
    gate,
    history,
    w_out,
    probs,
    slope,
    normed_out,
    inv_out,
    user,
    attn,
    scratch,
):
    pair = pl.program_id(0)
    base = lax.axis_index("seq") * NBD
    length = lengths[lax.axis_index("user")]
    masks = head_masks()
    q16 = q[...] * jnp.asarray(1.0 / 16.0, BF)
    kg, vg = unrotate((glob0, glob1, glob2, glob3), scratch)
    lane = iota((BLK, 2 * BLK), 1)
    gid = jnp.where(lane < BLK, gids[0, 0], gids[0, 1])
    at = gid * BLK + lane % BLK
    vg_both = jnp.concatenate([vg * m for m in masks], axis=0)
    logits = dot_nt(jnp.concatenate([q16 * m for m in masks], axis=0), kg)
    held = []
    for i in range(NBD):
        rows = slice(i * BLK, (i + 1) * BLK)
        mask = (gid < base + i - 1) & (at < length)
        parts = []
        for h in range(2):
            p, f = act(logits[h * EVENTS + i * BLK : h * EVENTS + (i + 1) * BLK], mask)
            probs[h, rows, :] = p
            slope[h, rows, :] = f
            parts.append(p)
        held.append(jnp.concatenate(parts, axis=1))
    attn[pair] = near[...] + dot(jnp.concatenate(held, axis=0), vg_both)

    @pl.when(pair == PAIRS - 1)
    def _():
        step = 128
        for r in range(0, EVENTS, step):
            rows = slice(r, r + step)
            x = jnp.concatenate([attn[p, rows, :] for p in range(PAIRS)], axis=1)
            centered = x - jnp.mean(x, axis=1, keepdims=True)
            var = jnp.mean(centered * centered, axis=1, keepdims=True)
            inv = lax.rsqrt(var + 1e-05)
            normed = centered * inv
            normed_out[rows, :] = normed.astype(BF)
            inv_out[rows, :] = inv
            gated = (normed * gate[rows, :].astype(F32)).astype(BF)
            user[rows, :] = (dot(gated, w_out[...]) + history[rows, :].astype(F32)).astype(BF)


def pair_block(rows):
    return pl.BlockSpec((rows, 2 * HEAD_DIM), lambda p: (0, p))


def pair_stack(rows):
    return pl.BlockSpec((2, rows, 2 * HEAD_DIM), lambda p: (0, 0, p))


def head_block():
    return pl.BlockSpec((2, EVENTS, 2 * BLK), lambda p: (p, 0, 0))


SQUARE = slow((HEADS, EVENTS, 2 * BLK), BF)


def near_forward(lengths, q, k, v, halo):
    return pl.pallas_call(
        near_forward_kernel,
        grid=(PAIRS,),
        out_shape=(SQUARE, SQUARE, fast((EVENTS, D), F32)),
        in_specs=[SMEM_SPEC] + [pair_block(EVENTS)] * 3 + [pair_stack(BLK)],
        out_specs=[head_block(), head_block(), pair_block(EVENTS)],
        compiler_params=params(),
        cost_estimate=pl.CostEstimate(
            flops=5 * 10**8, bytes_accessed=7 * 10**6, transcendentals=10**6
        ),
        name="near_forward",
    )(*in_hbm(lengths), q, k, v, halo)


def far_forward(lengths, gids, q, glob, near, gate, history, w_out):
    return pl.pallas_call(
        far_forward_kernel,
        grid=(PAIRS,),
        out_shape=(
            SQUARE,
            SQUARE,
            slow((EVENTS, D), BF),
            slow((EVENTS, 1), F32),
            slow((EVENTS, E), BF),
        ),
        in_specs=[SMEM_SPEC] * 2
        + [pair_block(EVENTS)]
        + [pair_block(BLK)] * CHUNKS
        + [pair_block(EVENTS)]
        + [whole((EVENTS, D)), whole((EVENTS, E)), whole((D, E))],
        out_specs=[
            head_block(),
            head_block(),
            whole((EVENTS, D)),
            whole((EVENTS, 1)),
            whole((EVENTS, E)),
        ],
        scratch_shapes=[
            pltpu.VMEM((PAIRS, EVENTS, 2 * HEAD_DIM), F32),
            pltpu.VMEM((CHUNKS, BLK, 2 * HEAD_DIM), BF),
        ],
        compiler_params=params(),
        cost_estimate=pl.CostEstimate(
            flops=6 * 10**8, bytes_accessed=9 * 10**6, transcendentals=10**6
        ),
        name="far_forward",
    )(*in_hbm(lengths, gids), q, *glob, *in_vmem(near), *in_hbm(gate, history, w_out))


def far_backward_kernel(
    d_user,
    w_out,
    inv,
    normed,
    gate,
    q,
    glob0,
    glob1,
    glob2,
    glob3,
    probs,
    slope,
    d_q,
    out0,
    out1,
    out2,
    out3,
    attn_far,
    gate_far,
    scratch,
    d_attn,
    d_gate,
    sems,
):
    pair = pl.program_id(0)
    width = 2 * HEAD_DIM
    copies = [
        pltpu.make_async_copy(
            d_attn.at[p], attn_far.at[:, p * width : (p + 1) * width], sems.at[p]
        )
        for p in range(PAIRS)
    ] + [pltpu.make_async_copy(d_gate, gate_far, sems.at[PAIRS])]

    @pl.when(pair == 0)
    def _():
        step = 128
        for r in range(0, EVENTS, step):
            rows = slice(r, r + step)
            d_gated = dot_nt(d_user[rows, :], w_out[...])
            n = normed[rows, :].astype(F32)
            d_gate[rows, :] = (d_gated * n).astype(BF)
            dn = d_gated * gate[rows, :].astype(F32)
            result = (
                (
                    dn
                    - jnp.mean(dn, axis=1, keepdims=True)
                    - n * jnp.mean(dn * n, axis=1, keepdims=True)
                )
                * inv[rows, :]
            ).astype(BF)
            for p in range(PAIRS):
                d_attn[p, rows, :] = result[:, p * width : (p + 1) * width]
        for copy in copies:
            copy.start()

    masks = head_masks()
    sixteenth = jnp.asarray(1.0 / 16.0, BF)
    q16 = q[...] * sixteenth
    kg, vg = unrotate((glob0, glob1, glob2, glob3), scratch)
    do = d_attn[pair]
    q_t = jnp.concatenate([(q16 * m).T for m in masks], axis=1)
    do_t = jnp.concatenate([(do * m).T for m in masks], axis=1)
    kg_both = jnp.concatenate([kg * (m * sixteenth) for m in masks], axis=0)
    d_probs = dot_nt(jnp.concatenate([do * m for m in masks], axis=0), vg)
    ds = [
        (d_probs[h * EVENTS : (h + 1) * EVENTS] * slope[h].astype(F32)).astype(BF) for h in range(2)
    ]
    d_q[...] = dot(jnp.concatenate(ds, axis=1), kg_both)
    d_k = dot(q_t, jnp.concatenate(ds, axis=0)).T.astype(BF)
    d_v = dot(do_t, jnp.concatenate([probs[0], probs[1]], axis=0)).T.astype(BF)
    for g in range(GLOB):
        scratch[g] = d_k[g * BLK : (g + 1) * BLK]
        scratch[GLOB + g] = d_v[g * BLK : (g + 1) * BLK]
    for d, out in enumerate((out0, out1, out2, out3)):
        out[...] = scratch[chunk_of(d)]

    @pl.when(pair == PAIRS - 1)
    def _():
        for copy in copies:
            copy.wait()


def far_backward(d_user, w_out, inv, normed, gate, q, glob, probs, slope):
    return pl.pallas_call(
        far_backward_kernel,
        grid=(PAIRS,),
        out_shape=(fast((EVENTS, D), F32),)
        + (jax.ShapeDtypeStruct((BLK, D), BF),) * CHUNKS
        + (slow((EVENTS, D), BF),) * 2,
        in_specs=[
            whole((EVENTS, E)),
            whole((D, E)),
            whole((EVENTS, 1)),
            whole((EVENTS, D)),
            whole((EVENTS, D)),
            pair_block(EVENTS),
        ]
        + [pair_block(BLK)] * CHUNKS
        + [head_block()] * 2,
        out_specs=[pair_block(EVENTS)] + [pair_block(BLK)] * CHUNKS + [ANY_SPEC] * 2,
        scratch_shapes=[
            pltpu.VMEM((CHUNKS, BLK, 2 * HEAD_DIM), BF),
            pltpu.VMEM((PAIRS, EVENTS, 2 * HEAD_DIM), BF),
            pltpu.VMEM((EVENTS, D), BF),
            pltpu.SemaphoreType.DMA((PAIRS + 1,)),
        ],
        compiler_params=params(),
        cost_estimate=pl.CostEstimate(flops=10**9, bytes_accessed=7 * 10**6, transcendentals=0),
        name="far_backward",
    )(*in_hbm(d_user, w_out, inv, normed, gate, q), *glob, *in_hbm(probs, slope))


def near_backward_kernel(q, k, v, halo, grad, probs, slope, far, d_q, d_k, d_v, edge):
    masks = head_masks()
    sixteenth = jnp.asarray(1.0 / 16.0, BF)
    q16 = q[...] * sixteenth
    kx = jnp.concatenate([halo[0], k[...]], axis=0)
    vx = jnp.concatenate([halo[1], v[...]], axis=0)
    do = grad[...]
    q_t = [(q16 * m).T for m in masks]
    do_t = [(do * m).T for m in masks]
    kx_m = [kx * (m * sixteenth) for m in masks]
    blocks = [slice(i * BLK, (i + 1) * BLK) for i in range(NBD)]
    windows = [slice(i * BLK, (i + 2) * BLK) for i in range(NBD)]
    d_probs = [
        dot_nt(jnp.concatenate([do[blocks[i]] * m for m in masks], axis=0), vx[windows[i]])
        for i in range(NBD)
    ]
    all_ds = [
        [
            (d_probs[i][h * BLK : (h + 1) * BLK] * slope[h, blocks[i], :].astype(F32)).astype(BF)
            for h in range(2)
        ]
        for i in range(NBD)
    ]
    carry = None
    for i in range(NBD):
        rows, keys, ds = blocks[i], windows[i], all_ds[i]
        near_k = jnp.concatenate([m[keys] for m in kx_m], axis=0)
        d_q[rows, :] = (far[rows, :] + dot(jnp.concatenate(ds, axis=1), near_k)).astype(BF)
        near_p = jnp.concatenate([probs[h, rows, :] for h in range(2)], axis=0)
        dk = dot(jnp.concatenate([t[:, rows] for t in q_t], axis=1), jnp.concatenate(ds, axis=0)).T
        dv = dot(jnp.concatenate([t[:, rows] for t in do_t], axis=1), near_p).T
        if i == 0:
            edge[0] = dk[:BLK].astype(BF)
            edge[1] = dv[:BLK].astype(BF)
        else:
            last = slice((i - 1) * BLK, i * BLK)
            d_k[last, :] = (carry[0] + dk[:BLK]).astype(BF)
            d_v[last, :] = (carry[1] + dv[:BLK]).astype(BF)
        carry = (dk[BLK:], dv[BLK:])
    last = slice((NBD - 1) * BLK, NBD * BLK)
    d_k[last, :] = carry[0].astype(BF)
    d_v[last, :] = carry[1].astype(BF)


def near_backward(q, k, v, halo, grad, probs, slope, far):
    rows = jax.ShapeDtypeStruct((EVENTS, D), BF)
    return pl.pallas_call(
        near_backward_kernel,
        grid=(PAIRS,),
        out_shape=(
            rows,
            slow((EVENTS, D), BF),
            slow((EVENTS, D), BF),
            jax.ShapeDtypeStruct((2, BLK, D), BF),
        ),
        in_specs=[pair_block(EVENTS)] * 3
        + [pair_stack(BLK), pair_block(EVENTS)]
        + [head_block()] * 2
        + [pair_block(EVENTS)],
        out_specs=[pair_block(EVENTS)] * 3 + [pair_stack(BLK)],
        compiler_params=params(),
        cost_estimate=pl.CostEstimate(
            flops=10**9, bytes_accessed=9 * 10**6, transcendentals=0
        ),
        name="near_backward",
    )(q, k, v, halo, *in_hbm(grad), probs, slope, *in_vmem(far))


def middle_kernel(
    lengths, items, code, user, out_far, d_user, score, share, outgoing, sems
):
    sends = []
    portion = NDEV * SLOTS // 4
    user_b = user[...]
    user_t = user_b.T
    mark = code[...].astype(F32)
    first = mark >= FIRST
    rank = jnp.where(first, mark - FIRST, mark)
    group = 16
    size = group * SLOTS
    slot = iota((SLOTS, EVENTS), 0).astype(F32)
    for d in range(0, NDEV, group):
        s = dot(items[d * SLOTS : d * SLOTS + size, :], user_t)
        for r in range(group):
            own = rank[d + r : d + r + 1, :] == slot
            part = jnp.where(own, s[r * SLOTS : (r + 1) * SLOTS, :], 0.0)
            score[d + r : d + r + 1, :] = jnp.sum(part, axis=0, keepdims=True)
    score0 = jnp.sum(jnp.where(first, score[...], 0.0), axis=0, keepdims=True)
    event = lax.axis_index("seq") * EVENTS + iota((1, EVENTS), 1)
    valid = jnp.where(event < lengths[lax.axis_index("user")], 1.0, 0.0)
    other = (rank >= 0.0) & jnp.logical_not(first)
    side = jnp.where(other, jax.nn.sigmoid(score[...] - score0), 0.0) * valid
    coef = jnp.where(first, -jnp.sum(side, axis=0, keepdims=True), side)
    for d in range(0, NDEV, group):
        rows = slice(d * SLOTS, d * SLOTS + size)
        c = jnp.concatenate(
            [
                jnp.where(rank[r : r + 1, :] == slot, coef[r : r + 1, :], 0.0).astype(BF)
                for r in range(d, d + group)
            ],
            axis=0,
        )
        share[rows, :] = c
        outgoing[rows, :] = dot(c, user_b).astype(BF)
        if rows.stop % portion == 0:
            part = slice(rows.stop - portion, rows.stop)
            sends.append(
                pltpu.make_async_copy(
                    outgoing.at[part, :], out_far.at[part, :], sems.at[len(sends)]
                )
            )
            sends[-1].start()
    d_user[...] = dot_tn(items[...], share[...]).T.astype(BF)
    for copy in sends:
        copy.wait()


def middle(lengths, items, code, user):
    return pl.pallas_call(
        middle_kernel,
        out_shape=(slow((NDEV * SLOTS, E), BF), slow((EVENTS, E), BF)),
        in_specs=[SMEM_SPEC] + [VMEM_SPEC] * 3,
        out_specs=[ANY_SPEC, VMEM_SPEC],
        scratch_shapes=[
            pltpu.VMEM((NDEV, EVENTS), F32),
            pltpu.VMEM((NDEV * SLOTS, EVENTS), BF),
            pltpu.VMEM((NDEV * SLOTS, E), BF),
            pltpu.SemaphoreType.DMA((4,)),
        ],
        compiler_params=params(),
        cost_estimate=pl.CostEstimate(
            flops=2 * 10**9, bytes_accessed=6 * 10**6, transcendentals=10**5
        ),
        name="ranking",
    )(*in_hbm(lengths), *in_vmem(items), *in_hbm(code, user))


def finish_kernel(gids, d_k, d_v, edge, glob0, glob1, glob2, glob3, key_out, value_out):
    seq = lax.axis_index("seq")
    outs = (key_out, value_out)
    for which, mine in enumerate((d_k, d_v)):
        outs[which][...] = mine[...]
        tail = slice(EVENTS - BLK, EVENTS)
        outs[which][tail, :] = (mine[tail, :].astype(F32) + edge[which].astype(F32)).astype(BF)
    for d, more in enumerate((glob0, glob1, glob2, glob3)):
        c = chunk_of(CHUNKS - d)
        gid = gids[0, c % GLOB]
        place = pl.ds(pl.multiple_of((gid % NBD) * BLK, BLK), BLK)
        for which in range(2):

            @pl.when((gid // NBD == seq) & (c // GLOB == which))
            def _():
                out = outs[which]
                out[place, :] = (out[place, :].astype(F32) + more[...].astype(F32)).astype(BF)


def finish(gids, d_k, d_v, edge, total):
    rows = jax.ShapeDtypeStruct((EVENTS, D), BF)
    return pl.pallas_call(
        finish_kernel,
        out_shape=(rows, rows),
        in_specs=[SMEM_SPEC] + [VMEM_SPEC] * (3 + CHUNKS),
        out_specs=[VMEM_SPEC] * 2,
        compiler_params=params(),
        cost_estimate=pl.CostEstimate(flops=10**6, bytes_accessed=3 * 10**6, transcendentals=0),
        name="add_received",
    )(*in_hbm(gids), d_k, d_v, edge, *total)


def from_behind(block, axis, distance):
    size = lax.axis_size(axis)
    return lax.ppermute(block, axis, [(i, (i + distance) % size) for i in range(size)])


def exchange(x, axis):
    return lax.all_to_all(x, axis, split_axis=0, concat_axis=0, tiled=True)


def around_x(x, distance):
    pairs = [(i, i // XSIZE * XSIZE + (i + distance) % XSIZE) for i in range(NSEQ)]
    return lax.ppermute(x, "seq", pairs)


def around_z(x, distance):
    return lax.ppermute(x, "seq", [(i, (i + distance * XSIZE) % NSEQ) for i in range(NSEQ)])


def add_all(parts):
    return sum(p.astype(F32) for p in parts).astype(BF)


def from_x(chunks):
    return [chunks[0]] + [around_x(chunks[d], d) for d in range(1, CHUNKS)]


def from_z(mine):
    return [mine] + [around_z(mine, d) for d in range(1, NSEQ // XSIZE)]


def share_x(mine):
    return [mine] + [around_x(mine, d) for d in range(1, CHUNKS)]


def together(*values):
    return lax.optimization_barrier(values)


def on_device(
    query, key, value, gate, history, w_out, table, item_owner, item_row, gids, lengths
):
    q, k, v = query[0], key[0], value[0]
    owner = jnp.transpose(item_owner, (2, 0, 1))
    row = jnp.transpose(item_row, (2, 0, 1))
    tail, *cand = pieces(gids, k, v)
    parts = from_x(cand)
    owner, _ = together(owner, cand[0])
    req, code = route(owner, row)
    tail, _ = together(tail, req)
    halo = from_behind(tail, "seq", 1)
    req, *parts = together(req, *parts)
    mine = add_all(parts)
    parts = from_z(mine)
    req, halo, _ = together(req, halo, mine)
    asked = exchange(req.reshape(NDEV, 1, E), ("seq", "user")).reshape(NDEV, E)
    mine = add_all(parts)
    glob = share_x(mine)
    asked, _ = together(asked, mine)
    found, asked = gather(asked, table)
    found, *glob = together(found, *glob)
    items = exchange(found.reshape(NDEV, SLOTS, E), ("seq", "user")).reshape(NDEV * SLOTS, E)
    near_p, near_f, near = near_forward(lengths, q, k, v, halo)
    far_p, far_f, normed, inv, user = far_forward(
        lengths, gids, q, glob, near, gate[0], history[0], w_out
    )
    outgoing, d_user = middle(lengths, items, code, user)
    incoming = exchange(outgoing.reshape(NDEV, SLOTS, E), ("seq", "user"))
    far_q, *d_glob, d_attn, d_gate = far_backward(
        d_user, w_out, inv, normed, gate[0], q, glob, far_p, far_f
    )
    parts = from_x(d_glob)
    d_q, d_k, d_v, edge = near_backward(q, k, v, halo, d_attn, near_p, near_f, far_q)
    d_k, *parts = together(d_k, *parts)
    mine = add_all(parts)
    back = from_behind(edge, "seq", -1)
    incoming, mine = together(incoming.reshape(NDEV * SLOTS, E), mine)
    grad = scatter(0, 1, asked, incoming)
    grad, *parts = together(grad, *from_z(mine))
    mine = add_all(parts)
    grad, mine = together(grad, mine)
    grad = scatter(1, 1, asked, incoming, (grad,))
    grad, *total = together(grad, *share_x(mine))
    d_key, d_value = finish(gids, d_k, d_v, back, total)
    return (d_q[None], d_key[None], d_value[None], d_gate[None], grad.reshape(ROWS, E))


def solution(mesh):
    return jax.shard_map(
        on_device,
        mesh=mesh,
        in_specs=(
            P("user", "seq", None),
            P("user", "seq", None),
            P("user", "seq", None),
            P("user", "seq", None),
            P("user", "seq", None),
            P(),
            P(("seq", "user"), None),
            P("user", "seq", None),
            P("user", "seq", None),
            P("user", None),
            P(),
        ),
        out_specs=(
            P("user", "seq", None),
            P("user", "seq", None),
            P("user", "seq", None),
            P("user", "seq", None),
            P(("seq", "user"), None),
        ),
        check_vma=False,
    )
```

```python
import functools

import jax
import jax.numpy as jnp
from jax import lax
from jax.experimental import pallas as pl
from jax.experimental.pallas import tpu as pltpu
from jax.sharding import PartitionSpec as P

HEADS = 8
HEAD_DIM = 64
D = 512
E = 128
BLK = 128
GLOB = 2
ITEMS = 5
EVENTS = 512
NBD = EVENTS // BLK
PAIRS = HEADS // 2
NDEV = 128
NSEQ = 16
CHUNKS = 2 * GLOB
ROWS = 4096
SLOTS = 32
FIRST = 64.0
HI = 4
LO = ROWS // HI
BF = jnp.bfloat16
F32 = jnp.float32
VMEM_LIMIT = 24 * 1024 * 1024
SMEM_SPEC = pl.BlockSpec(memory_space=pltpu.SMEM)
VMEM_SPEC = pl.BlockSpec(memory_space=pltpu.VMEM)
ANY_SPEC = pl.BlockSpec(memory_space=pl.ANY)
XSIZE = 4


def dot(a, b):
    return jnp.dot(a, b, preferred_element_type=F32)


def dot_nt(a, b):
    return lax.dot_general(a, b, (((1,), (1,)), ((), ())), preferred_element_type=F32)


def dot_tn(a, b):
    return lax.dot_general(a, b, (((0,), (0,)), ((), ())), preferred_element_type=F32)


def params(**more):
    return pltpu.CompilerParams(vmem_limit_bytes=VMEM_LIMIT, **more)


def fast(shape, dtype):
    return pltpu.VMEM(shape, dtype)


def slow(shape, dtype):
    return pltpu.HBM(shape, dtype)


def in_vmem(*arrays):
    return [pltpu.with_memory_space_constraint(x, pltpu.VMEM) for x in arrays]


def in_hbm(*arrays):
    return [pltpu.with_memory_space_constraint(x, pltpu.HBM) for x in arrays]


def whole(shape):
    return pl.BlockSpec(shape, lambda *_: (0,) * len(shape))


def iota(shape, dim):
    return lax.broadcasted_iota(jnp.int32, shape, dim)


def chunk_of(shift):
    return (lax.axis_index("seq") + shift) % XSIZE


def pieces_kernel(gids, key, value, halo, cand0, cand1, cand2, cand3, sems):
    seq = lax.axis_index("seq")
    tail = pl.ds(EVENTS - BLK, BLK)
    tails = [
        pltpu.make_async_copy(src.at[tail, :], halo.at[i], sems.at[CHUNKS + i])
        for i, src in enumerate((key, value))
    ]
    for copy in tails:
        copy.start()
    cases = []
    for d, out in enumerate((cand0, cand1, cand2, cand3)):
        c = chunk_of(d)
        gid = gids[0, c % GLOB]
        place = pl.ds(pl.multiple_of((gid % NBD) * BLK, BLK), BLK)
        held = gid // NBD == seq
        for i, src in enumerate((key, value)):
            copy = pltpu.make_async_copy(src.at[place, :], out, sems.at[d])
            cases.append((held & (c // GLOB == i), copy))

        @pl.when(jnp.logical_not(held))
        def _():
            out[...] = jnp.zeros((BLK, D), BF)

    for case, copy in cases:

        @pl.when(case)
        def _():
            copy.start()

    for case, copy in cases:

        @pl.when(case)
        def _():
            copy.wait()

    for copy in tails:
        copy.wait()


def pieces(gids, key, value):
    return pl.pallas_call(
        pieces_kernel,
        out_shape=(jax.ShapeDtypeStruct((2, BLK, D), BF),)
        + (jax.ShapeDtypeStruct((BLK, D), BF),) * CHUNKS,
        in_specs=[SMEM_SPEC] + [ANY_SPEC] * 2,
        out_specs=[VMEM_SPEC] * (1 + CHUNKS),
        scratch_shapes=[pltpu.SemaphoreType.DMA((CHUNKS + 2,))],
        compiler_params=params(),
        cost_estimate=pl.CostEstimate(flops=10**6, bytes_accessed=2 * 10**6, transcendentals=0),
        name="pieces",
    )(*in_hbm(gids, key, value))


def route_kernel(owner, row, req, code):
    dev = iota((NDEV, EVENTS), 0)
    rows = jnp.full((NDEV, EVENTS), -1, jnp.int32)
    for j in range(ITEMS):
        rows = jnp.where(owner[j] == dev, row[j], rows)
    hit = rows >= 0
    before = jnp.where(iota((EVENTS, EVENTS), 0) < iota((EVENTS, EVENTS), 1), 1.0, 0.0).astype(BF)
    rank = dot(jnp.where(hit, 1.0, 0.0).astype(BF), before)
    rank = jnp.where(hit, rank, -1.0)
    code[...] = jnp.where(owner[0] == dev, rank + FIRST, rank).astype(BF)
    plus = (rows + 1).astype(F32)
    lane = iota((NDEV, E), 1) - (lax.axis_index("user") % (E // SLOTS)) * SLOTS
    asked = jnp.zeros((NDEV, E), F32)
    for k in range(SLOTS):
        column = jnp.sum(jnp.where(rank == k, plus, 0.0), axis=1, keepdims=True)
        asked = jnp.where(lane == k, column, asked)
    req[...] = asked.astype(jnp.int32)


def route(owner, row):
    return pl.pallas_call(
        route_kernel,
        out_shape=(
            slow((NDEV, E), jnp.int32),
            slow((NDEV, EVENTS), BF),
        ),
        in_specs=[VMEM_SPEC] * 2,
        out_specs=[VMEM_SPEC] * 2,
        compiler_params=params(),
        cost_estimate=pl.CostEstimate(flops=10**8, bytes_accessed=10**6, transcendentals=0),
        name="route",
    )(*in_hbm(owner, row))


def slot_rows(asked, count):
    rows = asked[pl.ds(0, count, stride=4), :]
    for j in range(1, 4):
        rows = rows + asked[pl.ds(j, count, stride=4), :]
    return rows - 1


def slot_columns(rows):
    count = rows.shape[0]
    full = jnp.concatenate([rows.astype(F32), jnp.zeros((E - count, E), F32)], axis=0)
    return full.T[:, :count].astype(jnp.int32)


def spread_columns(x, first, count):
    return jnp.concatenate(
        [jnp.broadcast_to(x[:, i : i + 1], (E, E)) for i in range(first, first + count)], axis=0
    )


def gather_kernel(asked, table_far, found_far, kept, table, found, sems):
    slabs = [slice(h * LO, (h + 1) * LO) for h in range(HI)]
    loads = [
        pltpu.make_async_copy(table_far.at[slab, :], table.at[slab, :], sems.at[h])
        for h, slab in enumerate(slabs)
    ]
    for load in loads:
        load.start()
    keep = pltpu.make_async_copy(asked, kept, sems.at[HI + 8])
    keep.start()
    columns = slot_columns(slot_rows(asked, NDEV // 4))
    lo = columns & (LO - 1)
    hi = columns >> (LO.bit_length() - 1)
    group = 4
    size = group * E
    lane = iota((size, E), 1)
    sends = []
    for step in range(NDEV // 4 // group):
        low = spread_columns(lo, step * group, group)
        high = spread_columns(hi, step * group, group)
        onehot = jnp.concatenate(
            [jnp.where(low == lane + b * E, 1.0, 0.0).astype(BF) for b in range(LO // E)], axis=1
        )
        if step == 0:
            for load in loads:
                load.wait()
        picked = dot(onehot, jnp.concatenate([table[slab, :] for slab in slabs], axis=1))
        out = jnp.zeros((size, E), F32)
        for h in range(HI):
            out = jnp.where(high == h, picked[:, h * E : (h + 1) * E], out)
        rows = slice(step * size, (step + 1) * size)
        found[rows, :] = out.astype(BF)
        sends.append(
            pltpu.make_async_copy(found.at[rows, :], found_far.at[rows, :], sems.at[HI + step])
        )
        sends[-1].start()
    for send in sends:
        send.wait()
    keep.wait()


def gather(asked, table):
    return pl.pallas_call(
        gather_kernel,
        out_shape=(slow((NDEV * SLOTS, E), BF), slow((NDEV, E), jnp.int32)),
        in_specs=[VMEM_SPEC, ANY_SPEC],
        out_specs=[ANY_SPEC] * 2,
        scratch_shapes=[
            pltpu.VMEM((ROWS, E), BF),
            pltpu.VMEM((NDEV * SLOTS, E), BF),
            pltpu.SemaphoreType.DMA((HI + 9,)),
        ],
        compiler_params=params(),
        cost_estimate=pl.CostEstimate(
            flops=2 * NDEV * SLOTS * ROWS * E, bytes_accessed=2 * 10**6, transcendentals=0
        ),
        name="gather_rows",
    )(*in_vmem(asked), *in_hbm(table))


PORTION = LO // 2


def scatter_kernel(start, asked, incoming, *refs):
    grad, spread = refs[-2:]
    step = pl.program_id(0)
    rows = slot_rows(asked, NDEV // 4)
    @pl.when(step == 0)
    def _():
        hi = slot_columns(rows) >> (LO.bit_length() - 1)
        group = 2
        size = group * E
        for first in range(0, NDEV // 4, group):
            high = spread_columns(hi, first, group)
            part = incoming[first * E : first * E + size, :].astype(F32)
            for h in range(HI):
                spread[first * E : first * E + size, h * E : (h + 1) * E] = jnp.where(
                    high == h, part, 0.0
                ).astype(BF)

    size = PORTION
    sub = iota((size, E), 0) + (start + step) * size
    lo = rows & (LO - 1)
    onehot = jnp.concatenate(
        [jnp.where(sub == lo[i : i + 1, :], 1.0, 0.0).astype(BF) for i in range(NDEV // 4)], axis=1
    )
    total = dot(onehot, spread[...])
    for h in range(HI):
        grad[h] = total[:, h * E : (h + 1) * E]


def scatter(start, steps, asked, incoming, before=()):
    count = NDEV * SLOTS
    return pl.pallas_call(
        functools.partial(scatter_kernel, start),
        grid=(steps,),
        out_shape=slow((HI, LO, E), F32),
        in_specs=[whole((NDEV, E)), whole((count, E))] + [ANY_SPEC] * len(before),
        out_specs=pl.BlockSpec((HI, PORTION, E), lambda i: (0, start + i, 0)),
        scratch_shapes=[pltpu.VMEM((count, HI * E), BF)],
        input_output_aliases={2 + i: i for i in range(len(before))},
        compiler_params=params(),
        cost_estimate=pl.CostEstimate(
            flops=count * ROWS * E, bytes_accessed=2 * 10**6, transcendentals=0
        ),
        name="scatter_rows",
    )(asked, incoming, *in_hbm(*before))


def head_masks():
    lane = iota((1, 2 * HEAD_DIM), 1)
    return [
        jnp.where(lane < HEAD_DIM, 1.0, 0.0).astype(BF),
        jnp.where(lane >= HEAD_DIM, 1.0, 0.0).astype(BF),
    ]


def act(u, mask):
    w = jnp.where(mask, 1.0 + jnp.tanh(u), 0.0)
    p = u * w
    return p.astype(BF), (w + p * (2.0 - w)).astype(BF)


def near_forward_kernel(lengths, q, k, v, halo, probs, slope, attn):
    base = lax.axis_index("seq") * NBD
    length = lengths[lax.axis_index("user")]
    masks = head_masks()
    q16 = q[...] * jnp.asarray(1.0 / 16.0, BF)
    kx = jnp.concatenate([halo[0], k[...]], axis=0)
    vx = jnp.concatenate([halo[1], v[...]], axis=0)
    lane = iota((BLK, 2 * BLK), 1)
    sub = iota((BLK, 2 * BLK), 0)
    vx_m = [vx * m for m in masks]
    both = [jnp.concatenate([q16[i * BLK : (i + 1) * BLK] * m for m in masks]) for i in range(NBD)]
    logits = [dot_nt(both[i], kx[i * BLK : (i + 2) * BLK]) for i in range(NBD)]
    held = []
    for i in range(NBD):
        rows = slice(i * BLK, (i + 1) * BLK)
        at = (base + i - 1) * BLK + lane
        mask = (at >= 0) & (at < length) & (lane <= sub + BLK)
        parts = []
        for h in range(2):
            p, f = act(logits[i][h * BLK : (h + 1) * BLK], mask)
            probs[h, rows, :] = p
            slope[h, rows, :] = f
            parts.append(p)
        held.append(jnp.concatenate(parts, axis=1))
    for i in range(NBD):
        keys = slice(i * BLK, (i + 2) * BLK)
        attn[i * BLK : (i + 1) * BLK, :] = dot(
            held[i], jnp.concatenate([m[keys] for m in vx_m], axis=0)
        )


def unrotate(parts, scratch):
    for d in range(CHUNKS):
        scratch[chunk_of(CHUNKS - d)] = parts[d][...]
    keys = jnp.concatenate([scratch[g] for g in range(GLOB)], axis=0)
    values = jnp.concatenate([scratch[GLOB + g] for g in range(GLOB)], axis=0)
    return keys, values


def far_forward_kernel(
    lengths,
    gids,
    q,
    glob0,
    glob1,
    glob2,
    glob3,
    near,
    gate,
    history,
    w_out,
    probs,
    slope,
    normed_out,
    inv_out,
    user,
    attn,
    scratch,
):
    pair = pl.program_id(0)
    base = lax.axis_index("seq") * NBD
    length = lengths[lax.axis_index("user")]
    masks = head_masks()
    q16 = q[...] * jnp.asarray(1.0 / 16.0, BF)
    kg, vg = unrotate((glob0, glob1, glob2, glob3), scratch)
    lane = iota((BLK, 2 * BLK), 1)
    gid = jnp.where(lane < BLK, gids[0, 0], gids[0, 1])
    at = gid * BLK + lane % BLK
    vg_both = jnp.concatenate([vg * m for m in masks], axis=0)
    logits = dot_nt(jnp.concatenate([q16 * m for m in masks], axis=0), kg)
    held = []
    for i in range(NBD):
        rows = slice(i * BLK, (i + 1) * BLK)
        mask = (gid < base + i - 1) & (at < length)
        parts = []
        for h in range(2):
            p, f = act(logits[h * EVENTS + i * BLK : h * EVENTS + (i + 1) * BLK], mask)
            probs[h, rows, :] = p
            slope[h, rows, :] = f
            parts.append(p)
        held.append(jnp.concatenate(parts, axis=1))
    attn[pair] = near[...] + dot(jnp.concatenate(held, axis=0), vg_both)

    @pl.when(pair == PAIRS - 1)
    def _():
        step = 128
        for r in range(0, EVENTS, step):
            rows = slice(r, r + step)
            x = jnp.concatenate([attn[p, rows, :] for p in range(PAIRS)], axis=1)
            centered = x - jnp.mean(x, axis=1, keepdims=True)
            var = jnp.mean(centered * centered, axis=1, keepdims=True)
            inv = lax.rsqrt(var + 1e-05)
            normed = centered * inv
            normed_out[rows, :] = normed.astype(BF)
            inv_out[rows, :] = inv
            gated = (normed * gate[rows, :].astype(F32)).astype(BF)
            vector = dot(gated, w_out[...]) + history[rows, :].astype(F32)
            rounded = vector.astype(BF)
            user[rows, :E] = rounded
            user[rows, E:] = (vector - rounded.astype(F32)).astype(BF)


def pair_block(rows):
    return pl.BlockSpec((rows, 2 * HEAD_DIM), lambda p: (0, p))


def pair_stack(rows):
    return pl.BlockSpec((2, rows, 2 * HEAD_DIM), lambda p: (0, 0, p))


def head_block():
    return pl.BlockSpec((2, EVENTS, 2 * BLK), lambda p: (p, 0, 0))


SQUARE = slow((HEADS, EVENTS, 2 * BLK), BF)


def near_forward(lengths, q, k, v, halo):
    return pl.pallas_call(
        near_forward_kernel,
        grid=(PAIRS,),
        out_shape=(SQUARE, SQUARE, fast((EVENTS, D), F32)),
        in_specs=[SMEM_SPEC] + [pair_block(EVENTS)] * 3 + [pair_stack(BLK)],
        out_specs=[head_block(), head_block(), pair_block(EVENTS)],
        compiler_params=params(),
        cost_estimate=pl.CostEstimate(
            flops=5 * 10**8, bytes_accessed=7 * 10**6, transcendentals=10**6
        ),
        name="near_forward",
    )(*in_hbm(lengths), q, k, v, halo)


def far_forward(lengths, gids, q, glob, near, gate, history, w_out):
    return pl.pallas_call(
        far_forward_kernel,
        grid=(PAIRS,),
        out_shape=(
            SQUARE,
            SQUARE,
            slow((EVENTS, D), BF),
            slow((EVENTS, 1), F32),
            slow((EVENTS, 2 * E), BF),
        ),
        in_specs=[SMEM_SPEC] * 2
        + [pair_block(EVENTS)]
        + [pair_block(BLK)] * CHUNKS
        + [pair_block(EVENTS)]
        + [whole((EVENTS, D)), whole((EVENTS, E)), whole((D, E))],
        out_specs=[
            head_block(),
            head_block(),
            whole((EVENTS, D)),
            whole((EVENTS, 1)),
            whole((EVENTS, 2 * E)),
        ],
        scratch_shapes=[
            pltpu.VMEM((PAIRS, EVENTS, 2 * HEAD_DIM), F32),
            pltpu.VMEM((CHUNKS, BLK, 2 * HEAD_DIM), BF),
        ],
        compiler_params=params(),
        cost_estimate=pl.CostEstimate(
            flops=6 * 10**8, bytes_accessed=9 * 10**6, transcendentals=10**6
        ),
        name="far_forward",
    )(*in_hbm(lengths, gids), q, *glob, *in_vmem(near), *in_hbm(gate, history, w_out))


def far_backward_kernel(
    d_user,
    w_out,
    inv,
    normed,
    gate,
    q,
    glob0,
    glob1,
    glob2,
    glob3,
    probs,
    slope,
    d_q,
    out0,
    out1,
    out2,
    out3,
    attn_far,
    gate_far,
    scratch,
    d_attn,
    d_gate,
    sems,
):
    pair = pl.program_id(0)
    width = 2 * HEAD_DIM
    copies = [
        pltpu.make_async_copy(
            d_attn.at[p], attn_far.at[:, p * width : (p + 1) * width], sems.at[p]
        )
        for p in range(PAIRS)
    ] + [pltpu.make_async_copy(d_gate, gate_far, sems.at[PAIRS])]

    @pl.when(pair == 0)
    def _():
        step = 128
        for r in range(0, EVENTS, step):
            rows = slice(r, r + step)
            d_gated = dot_nt(d_user[rows, :], w_out[...])
            n = normed[rows, :].astype(F32)
            d_gate[rows, :] = (d_gated * n).astype(BF)
            dn = d_gated * gate[rows, :].astype(F32)
            result = (
                (
                    dn
                    - jnp.mean(dn, axis=1, keepdims=True)
                    - n * jnp.mean(dn * n, axis=1, keepdims=True)
                )
                * inv[rows, :]
            ).astype(BF)
            for p in range(PAIRS):
                d_attn[p, rows, :] = result[:, p * width : (p + 1) * width]
        for copy in copies:
            copy.start()

    masks = head_masks()
    sixteenth = jnp.asarray(1.0 / 16.0, BF)
    q16 = q[...] * sixteenth
    kg, vg = unrotate((glob0, glob1, glob2, glob3), scratch)
    do = d_attn[pair]
    q_t = jnp.concatenate([(q16 * m).T for m in masks], axis=1)
    do_t = jnp.concatenate([(do * m).T for m in masks], axis=1)
    kg_both = jnp.concatenate([kg * (m * sixteenth) for m in masks], axis=0)
    d_probs = dot_nt(jnp.concatenate([do * m for m in masks], axis=0), vg)
    ds = [
        (d_probs[h * EVENTS : (h + 1) * EVENTS] * slope[h].astype(F32)).astype(BF) for h in range(2)
    ]
    d_q[...] = dot(jnp.concatenate(ds, axis=1), kg_both)
    d_k = dot(q_t, jnp.concatenate(ds, axis=0)).T.astype(BF)
    d_v = dot(do_t, jnp.concatenate([probs[0], probs[1]], axis=0)).T.astype(BF)
    for g in range(GLOB):
        scratch[g] = d_k[g * BLK : (g + 1) * BLK]
        scratch[GLOB + g] = d_v[g * BLK : (g + 1) * BLK]
    for d, out in enumerate((out0, out1, out2, out3)):
        out[...] = scratch[chunk_of(d)]

    @pl.when(pair == PAIRS - 1)
    def _():
        for copy in copies:
            copy.wait()


def far_backward(d_user, w_out, inv, normed, gate, q, glob, probs, slope):
    return pl.pallas_call(
        far_backward_kernel,
        grid=(PAIRS,),
        out_shape=(fast((EVENTS, D), F32),)
        + (jax.ShapeDtypeStruct((BLK, D), BF),) * CHUNKS
        + (slow((EVENTS, D), BF),) * 2,
        in_specs=[
            whole((EVENTS, E)),
            whole((D, E)),
            whole((EVENTS, 1)),
            whole((EVENTS, D)),
            whole((EVENTS, D)),
            pair_block(EVENTS),
        ]
        + [pair_block(BLK)] * CHUNKS
        + [head_block()] * 2,
        out_specs=[pair_block(EVENTS)] + [pair_block(BLK)] * CHUNKS + [ANY_SPEC] * 2,
        scratch_shapes=[
            pltpu.VMEM((CHUNKS, BLK, 2 * HEAD_DIM), BF),
            pltpu.VMEM((PAIRS, EVENTS, 2 * HEAD_DIM), BF),
            pltpu.VMEM((EVENTS, D), BF),
            pltpu.SemaphoreType.DMA((PAIRS + 1,)),
        ],
        compiler_params=params(),
        cost_estimate=pl.CostEstimate(flops=10**9, bytes_accessed=7 * 10**6, transcendentals=0),
        name="far_backward",
    )(*in_hbm(d_user, w_out, inv, normed, gate, q), *glob, *in_hbm(probs, slope))


def near_backward_kernel(q, k, v, halo, grad, probs, slope, far, d_q, d_k, d_v, edge):
    masks = head_masks()
    sixteenth = jnp.asarray(1.0 / 16.0, BF)
    q16 = q[...] * sixteenth
    kx = jnp.concatenate([halo[0], k[...]], axis=0)
    vx = jnp.concatenate([halo[1], v[...]], axis=0)
    do = grad[...]
    q_t = [(q16 * m).T for m in masks]
    do_t = [(do * m).T for m in masks]
    kx_m = [kx * (m * sixteenth) for m in masks]
    blocks = [slice(i * BLK, (i + 1) * BLK) for i in range(NBD)]
    windows = [slice(i * BLK, (i + 2) * BLK) for i in range(NBD)]
    d_probs = [
        dot_nt(jnp.concatenate([do[blocks[i]] * m for m in masks], axis=0), vx[windows[i]])
        for i in range(NBD)
    ]
    all_ds = [
        [
            (d_probs[i][h * BLK : (h + 1) * BLK] * slope[h, blocks[i], :].astype(F32)).astype(BF)
            for h in range(2)
        ]
        for i in range(NBD)
    ]
    carry = None
    for i in range(NBD):
        rows, keys, ds = blocks[i], windows[i], all_ds[i]
        near_k = jnp.concatenate([m[keys] for m in kx_m], axis=0)
        d_q[rows, :] = (far[rows, :] + dot(jnp.concatenate(ds, axis=1), near_k)).astype(BF)
        near_p = jnp.concatenate([probs[h, rows, :] for h in range(2)], axis=0)
        dk = dot(jnp.concatenate([t[:, rows] for t in q_t], axis=1), jnp.concatenate(ds, axis=0)).T
        dv = dot(jnp.concatenate([t[:, rows] for t in do_t], axis=1), near_p).T
        if i == 0:
            edge[0] = dk[:BLK].astype(BF)
            edge[1] = dv[:BLK].astype(BF)
        else:
            last = slice((i - 1) * BLK, i * BLK)
            d_k[last, :] = (carry[0] + dk[:BLK]).astype(BF)
            d_v[last, :] = (carry[1] + dv[:BLK]).astype(BF)
        carry = (dk[BLK:], dv[BLK:])
    last = slice((NBD - 1) * BLK, NBD * BLK)
    d_k[last, :] = carry[0].astype(BF)
    d_v[last, :] = carry[1].astype(BF)


def near_backward(q, k, v, halo, grad, probs, slope, far):
    rows = jax.ShapeDtypeStruct((EVENTS, D), BF)
    return pl.pallas_call(
        near_backward_kernel,
        grid=(PAIRS,),
        out_shape=(
            rows,
            slow((EVENTS, D), BF),
            slow((EVENTS, D), BF),
            jax.ShapeDtypeStruct((2, BLK, D), BF),
        ),
        in_specs=[pair_block(EVENTS)] * 3
        + [pair_stack(BLK), pair_block(EVENTS)]
        + [head_block()] * 2
        + [pair_block(EVENTS)],
        out_specs=[pair_block(EVENTS)] * 3 + [pair_stack(BLK)],
        compiler_params=params(),
        cost_estimate=pl.CostEstimate(
            flops=10**9, bytes_accessed=9 * 10**6, transcendentals=0
        ),
        name="near_backward",
    )(q, k, v, halo, *in_hbm(grad), probs, slope, *in_vmem(far))


def middle_kernel(
    lengths, items, code, user, out_far, d_user, score, share, outgoing, sems
):
    sends = []
    portion = NDEV * SLOTS // 4
    user_b = user[:, :E]
    user_t = user[...].T
    mark = code[...].astype(F32)
    first = mark >= FIRST
    rank = jnp.where(first, mark - FIRST, mark)
    group = 16
    size = group * SLOTS
    slot = iota((SLOTS, EVENTS), 0).astype(F32)
    for d in range(0, NDEV, group):
        rows = items[d * SLOTS : d * SLOTS + size, :]
        s = dot(jnp.concatenate([rows, rows], axis=1), user_t)
        for r in range(group):
            own = rank[d + r : d + r + 1, :] == slot
            part = jnp.where(own, s[r * SLOTS : (r + 1) * SLOTS, :], 0.0)
            score[d + r : d + r + 1, :] = jnp.sum(part, axis=0, keepdims=True)
    score0 = jnp.sum(jnp.where(first, score[...], 0.0), axis=0, keepdims=True)
    event = lax.axis_index("seq") * EVENTS + iota((1, EVENTS), 1)
    valid = jnp.where(event < lengths[lax.axis_index("user")], 1.0, 0.0)
    other = (rank >= 0.0) & jnp.logical_not(first)
    side = jnp.where(other, jax.nn.sigmoid(score[...] - score0), 0.0) * valid
    coef = jnp.where(first, -jnp.sum(side, axis=0, keepdims=True), side)
    for d in range(0, NDEV, group):
        rows = slice(d * SLOTS, d * SLOTS + size)
        c = jnp.concatenate(
            [
                jnp.where(rank[r : r + 1, :] == slot, coef[r : r + 1, :], 0.0).astype(BF)
                for r in range(d, d + group)
            ],
            axis=0,
        )
        share[rows, :] = c
        outgoing[rows, :] = dot(c, user_b).astype(BF)
        if rows.stop % portion == 0:
            part = slice(rows.stop - portion, rows.stop)
            sends.append(
                pltpu.make_async_copy(
                    outgoing.at[part, :], out_far.at[part, :], sems.at[len(sends)]
                )
            )
            sends[-1].start()
    d_user[...] = dot_tn(items[...], share[...]).T.astype(BF)
    for copy in sends:
        copy.wait()


def middle(lengths, items, code, user):
    return pl.pallas_call(
        middle_kernel,
        out_shape=(slow((NDEV * SLOTS, E), BF), slow((EVENTS, E), BF)),
        in_specs=[SMEM_SPEC] + [VMEM_SPEC] * 3,
        out_specs=[ANY_SPEC, VMEM_SPEC],
        scratch_shapes=[
            pltpu.VMEM((NDEV, EVENTS), F32),
            pltpu.VMEM((NDEV * SLOTS, EVENTS), BF),
            pltpu.VMEM((NDEV * SLOTS, E), BF),
            pltpu.SemaphoreType.DMA((4,)),
        ],
        compiler_params=params(),
        cost_estimate=pl.CostEstimate(
            flops=2 * 10**9, bytes_accessed=6 * 10**6, transcendentals=10**5
        ),
        name="ranking",
    )(*in_hbm(lengths), *in_vmem(items), *in_hbm(code, user))


def finish_kernel(gids, d_k, d_v, edge, glob0, glob1, glob2, glob3, key_out, value_out):
    seq = lax.axis_index("seq")
    outs = (key_out, value_out)
    for which, mine in enumerate((d_k, d_v)):
        outs[which][...] = mine[...]
        tail = slice(EVENTS - BLK, EVENTS)
        outs[which][tail, :] = (mine[tail, :].astype(F32) + edge[which].astype(F32)).astype(BF)
    for d, more in enumerate((glob0, glob1, glob2, glob3)):
        c = chunk_of(CHUNKS - d)
        gid = gids[0, c % GLOB]
        place = pl.ds(pl.multiple_of((gid % NBD) * BLK, BLK), BLK)
        for which in range(2):

            @pl.when((gid // NBD == seq) & (c // GLOB == which))
            def _():
                out = outs[which]
                out[place, :] = (out[place, :].astype(F32) + more[...].astype(F32)).astype(BF)


def finish(gids, d_k, d_v, edge, total):
    rows = jax.ShapeDtypeStruct((EVENTS, D), BF)
    return pl.pallas_call(
        finish_kernel,
        out_shape=(rows, rows),
        in_specs=[SMEM_SPEC] + [VMEM_SPEC] * (3 + CHUNKS),
        out_specs=[VMEM_SPEC] * 2,
        compiler_params=params(),
        cost_estimate=pl.CostEstimate(flops=10**6, bytes_accessed=3 * 10**6, transcendentals=0),
        name="add_received",
    )(*in_hbm(gids), d_k, d_v, edge, *total)


def from_behind(block, axis, distance):
    size = lax.axis_size(axis)
    return lax.ppermute(block, axis, [(i, (i + distance) % size) for i in range(size)])


def exchange(x, axis):
    return lax.all_to_all(x, axis, split_axis=0, concat_axis=0, tiled=True)


def around_x(x, distance):
    pairs = [(i, i // XSIZE * XSIZE + (i + distance) % XSIZE) for i in range(NSEQ)]
    return lax.ppermute(x, "seq", pairs)


def around_z(x, distance):
    return lax.ppermute(x, "seq", [(i, (i + distance * XSIZE) % NSEQ) for i in range(NSEQ)])


def add_all(parts):
    return sum(p.astype(F32) for p in parts).astype(BF)


def from_x(chunks):
    return [chunks[0]] + [around_x(chunks[d], d) for d in range(1, CHUNKS)]


def from_z(mine):
    return [mine] + [around_z(mine, d) for d in range(1, NSEQ // XSIZE)]


def share_x(mine):
    return [mine] + [around_x(mine, d) for d in range(1, CHUNKS)]


def together(*values):
    return lax.optimization_barrier(values)


def on_device(
    query, key, value, gate, history, w_out, table, item_owner, item_row, gids, lengths
):
    q, k, v = query[0], key[0], value[0]
    owner = jnp.transpose(item_owner, (2, 0, 1))
    row = jnp.transpose(item_row, (2, 0, 1))
    tail, *cand = pieces(gids, k, v)
    parts = from_x(cand)
    owner, _ = together(owner, cand[0])
    req, code = route(owner, row)
    tail, _ = together(tail, req)
    halo = from_behind(tail, "seq", 1)
    req, *parts = together(req, *parts)
    mine = add_all(parts)
    parts = from_z(mine)
    req, halo, _ = together(req, halo, mine)
    asked = exchange(req.reshape(NDEV, 1, E), ("seq", "user")).reshape(NDEV, E)
    mine = add_all(parts)
    glob = share_x(mine)
    asked, _ = together(asked, mine)
    found, asked = gather(asked, table)
    found, *glob = together(found, *glob)
    items = exchange(found.reshape(NDEV, SLOTS, E), ("seq", "user")).reshape(NDEV * SLOTS, E)
    near_p, near_f, near = near_forward(lengths, q, k, v, halo)
    far_p, far_f, normed, inv, user = far_forward(
        lengths, gids, q, glob, near, gate[0], history[0], w_out
    )
    outgoing, d_user = middle(lengths, items, code, user)
    incoming = exchange(outgoing.reshape(NDEV, SLOTS, E), ("seq", "user"))
    far_q, *d_glob, d_attn, d_gate = far_backward(
        d_user, w_out, inv, normed, gate[0], q, glob, far_p, far_f
    )
    parts = from_x(d_glob)
    d_q, d_k, d_v, edge = near_backward(q, k, v, halo, d_attn, near_p, near_f, far_q)
    d_k, *parts = together(d_k, *parts)
    mine = add_all(parts)
    back = from_behind(edge, "seq", -1)
    incoming, mine = together(incoming.reshape(NDEV * SLOTS, E), mine)
    grad = scatter(0, 1, asked, incoming)
    grad, *parts = together(grad, *from_z(mine))
    mine = add_all(parts)
    grad, mine = together(grad, mine)
    grad = scatter(1, 1, asked, incoming, (grad,))
    grad, *total = together(grad, *share_x(mine))
    d_key, d_value = finish(gids, d_k, d_v, back, total)
    return (d_q[None], d_key[None], d_value[None], d_gate[None], grad.reshape(ROWS, E))


def solution(mesh):
    return jax.shard_map(
        on_device,
        mesh=mesh,
        in_specs=(
            P("user", "seq", None),
            P("user", "seq", None),
            P("user", "seq", None),
            P("user", "seq", None),
            P("user", "seq", None),
            P(),
            P(("seq", "user"), None),
            P("user", "seq", None),
            P("user", "seq", None),
            P("user", None),
            P(),
        ),
        out_specs=(
            P("user", "seq", None),
            P("user", "seq", None),
            P("user", "seq", None),
            P("user", "seq", None),
            P(("seq", "user"), None),
        ),
        check_vma=False,
    )
```

```python
import functools

import jax
import jax.numpy as jnp
from jax import lax
from jax.experimental import pallas as pl
from jax.experimental.pallas import tpu as pltpu
from jax.sharding import PartitionSpec as P

HEADS = 8
HEAD_DIM = 64
D = 512
E = 128
BLK = 128
GLOB = 2
ITEMS = 5
EVENTS = 512
NBD = EVENTS // BLK
PAIRS = HEADS // 2
NDEV = 128
NSEQ = 16
CHUNKS = 2 * GLOB
ROWS = 4096
SLOTS = 32
FIRST = 64.0
HI = 4
LO = ROWS // HI
BF = jnp.bfloat16
F32 = jnp.float32
VMEM_LIMIT = 24 * 1024 * 1024
SMEM_SPEC = pl.BlockSpec(memory_space=pltpu.SMEM)
VMEM_SPEC = pl.BlockSpec(memory_space=pltpu.VMEM)
ANY_SPEC = pl.BlockSpec(memory_space=pl.ANY)
XSIZE = 4


def dot(a, b):
    return jnp.dot(a, b, preferred_element_type=F32)


def dot_nt(a, b):
    return lax.dot_general(a, b, (((1,), (1,)), ((), ())), preferred_element_type=F32)


def dot_tn(a, b):
    return lax.dot_general(a, b, (((0,), (0,)), ((), ())), preferred_element_type=F32)


def params(**more):
    return pltpu.CompilerParams(vmem_limit_bytes=VMEM_LIMIT, **more)


def fast(shape, dtype):
    return pltpu.VMEM(shape, dtype)


def slow(shape, dtype):
    return pltpu.HBM(shape, dtype)


def in_vmem(*arrays):
    return [pltpu.with_memory_space_constraint(x, pltpu.VMEM) for x in arrays]


def in_hbm(*arrays):
    return [pltpu.with_memory_space_constraint(x, pltpu.HBM) for x in arrays]


def whole(shape):
    return pl.BlockSpec(shape, lambda *_: (0,) * len(shape))


def iota(shape, dim):
    return lax.broadcasted_iota(jnp.int32, shape, dim)


def chunk_of(shift):
    return (lax.axis_index("seq") + shift) % XSIZE


def pieces_kernel(gids, key, value, halo, cand0, cand1, cand2, cand3, sems):
    seq = lax.axis_index("seq")
    tail = pl.ds(EVENTS - BLK, BLK)
    tails = [
        pltpu.make_async_copy(src.at[tail, :], halo.at[i], sems.at[CHUNKS + i])
        for i, src in enumerate((key, value))
    ]
    for copy in tails:
        copy.start()
    cases = []
    for d, out in enumerate((cand0, cand1, cand2, cand3)):
        c = chunk_of(d)
        gid = gids[0, c % GLOB]
        place = pl.ds(pl.multiple_of((gid % NBD) * BLK, BLK), BLK)
        held = gid // NBD == seq
        for i, src in enumerate((key, value)):
            copy = pltpu.make_async_copy(src.at[place, :], out, sems.at[d])
            cases.append((held & (c // GLOB == i), copy))

        @pl.when(jnp.logical_not(held))
        def _():
            out[...] = jnp.zeros((BLK, D), BF)

    for case, copy in cases:

        @pl.when(case)
        def _():
            copy.start()

    for case, copy in cases:

        @pl.when(case)
        def _():
            copy.wait()

    for copy in tails:
        copy.wait()


def pieces(gids, key, value):
    return pl.pallas_call(
        pieces_kernel,
        out_shape=(jax.ShapeDtypeStruct((2, BLK, D), BF),)
        + (jax.ShapeDtypeStruct((BLK, D), BF),) * CHUNKS,
        in_specs=[SMEM_SPEC] + [ANY_SPEC] * 2,
        out_specs=[VMEM_SPEC] * (1 + CHUNKS),
        scratch_shapes=[pltpu.SemaphoreType.DMA((CHUNKS + 2,))],
        compiler_params=params(),
        cost_estimate=pl.CostEstimate(flops=10**6, bytes_accessed=2 * 10**6, transcendentals=0),
        name="pieces",
    )(*in_hbm(gids, key, value))


def route_kernel(owner, row, req, code):
    dev = iota((NDEV, EVENTS), 0)
    rows = jnp.full((NDEV, EVENTS), -1, jnp.int32)
    for j in range(ITEMS):
        rows = jnp.where(owner[j] == dev, row[j], rows)
    hit = rows >= 0
    before = jnp.where(iota((EVENTS, EVENTS), 0) < iota((EVENTS, EVENTS), 1), 1.0, 0.0).astype(BF)
    rank = dot(jnp.where(hit, 1.0, 0.0).astype(BF), before)
    rank = jnp.where(hit, rank, -1.0)
    code[...] = jnp.where(owner[0] == dev, rank + FIRST, rank).astype(BF)
    plus = (rows + 1).astype(F32)
    lane = iota((NDEV, E), 1) - (lax.axis_index("user") % (E // SLOTS)) * SLOTS
    asked = jnp.zeros((NDEV, E), F32)
    for k in range(SLOTS):
        column = jnp.sum(jnp.where(rank == k, plus, 0.0), axis=1, keepdims=True)
        asked = jnp.where(lane == k, column, asked)
    req[...] = asked.astype(jnp.int32)


def route(owner, row):
    return pl.pallas_call(
        route_kernel,
        out_shape=(
            slow((NDEV, E), jnp.int32),
            slow((NDEV, EVENTS), BF),
        ),
        in_specs=[VMEM_SPEC] * 2,
        out_specs=[VMEM_SPEC] * 2,
        compiler_params=params(),
        cost_estimate=pl.CostEstimate(flops=10**8, bytes_accessed=10**6, transcendentals=0),
        name="route",
    )(*in_hbm(owner, row))


def slot_rows(asked, count):
    rows = asked[pl.ds(0, count, stride=4), :]
    for j in range(1, 4):
        rows = rows + asked[pl.ds(j, count, stride=4), :]
    return rows - 1


def slot_columns(rows):
    count = rows.shape[0]
    full = jnp.concatenate([rows.astype(F32), jnp.zeros((E - count, E), F32)], axis=0)
    return full.T[:, :count].astype(jnp.int32)


def spread_columns(x, first, count):
    return jnp.concatenate(
        [jnp.broadcast_to(x[:, i : i + 1], (E, E)) for i in range(first, first + count)], axis=0
    )


def gather_kernel(asked, table_far, found_far, kept, table, found, sems):
    slabs = [slice(h * LO, (h + 1) * LO) for h in range(HI)]
    loads = [
        pltpu.make_async_copy(table_far.at[slab, :], table.at[slab, :], sems.at[h])
        for h, slab in enumerate(slabs)
    ]
    for load in loads:
        load.start()
    keep = pltpu.make_async_copy(asked, kept, sems.at[HI + 8])
    keep.start()
    columns = slot_columns(slot_rows(asked, NDEV // 4))
    lo = columns & (LO - 1)
    hi = columns >> (LO.bit_length() - 1)
    group = 4
    size = group * E
    lane = iota((size, E), 1)
    sends = []
    for step in range(NDEV // 4 // group):
        low = spread_columns(lo, step * group, group)
        high = spread_columns(hi, step * group, group)
        onehot = jnp.concatenate(
            [jnp.where(low == lane + b * E, 1.0, 0.0).astype(BF) for b in range(LO // E)], axis=1
        )
        if step == 0:
            for load in loads:
                load.wait()
        picked = dot(onehot, jnp.concatenate([table[slab, :] for slab in slabs], axis=1))
        out = jnp.zeros((size, E), F32)
        for h in range(HI):
            out = jnp.where(high == h, picked[:, h * E : (h + 1) * E], out)
        rows = slice(step * size, (step + 1) * size)
        found[rows, :] = out.astype(BF)
        sends.append(
            pltpu.make_async_copy(found.at[rows, :], found_far.at[rows, :], sems.at[HI + step])
        )
        sends[-1].start()
    for send in sends:
        send.wait()
    keep.wait()


def gather(asked, table):
    return pl.pallas_call(
        gather_kernel,
        out_shape=(slow((NDEV * SLOTS, E), BF), slow((NDEV, E), jnp.int32)),
        in_specs=[VMEM_SPEC, ANY_SPEC],
        out_specs=[ANY_SPEC] * 2,
        scratch_shapes=[
            pltpu.VMEM((ROWS, E), BF),
            pltpu.VMEM((NDEV * SLOTS, E), BF),
            pltpu.SemaphoreType.DMA((HI + 9,)),
        ],
        compiler_params=params(),
        cost_estimate=pl.CostEstimate(
            flops=2 * NDEV * SLOTS * ROWS * E, bytes_accessed=2 * 10**6, transcendentals=0
        ),
        name="gather_rows",
    )(*in_vmem(asked), *in_hbm(table))


PORTION = LO // 2


def scatter_kernel(start, asked, incoming, *refs):
    grad, spread = refs[-2:]
    step = pl.program_id(0)
    rows = slot_rows(asked, NDEV // 4)
    @pl.when(step == 0)
    def _():
        hi = slot_columns(rows) >> (LO.bit_length() - 1)
        group = 2
        size = group * E
        for first in range(0, NDEV // 4, group):
            high = spread_columns(hi, first, group)
            part = incoming[first * E : first * E + size, :].astype(F32)
            for h in range(HI):
                spread[first * E : first * E + size, h * E : (h + 1) * E] = jnp.where(
                    high == h, part, 0.0
                ).astype(BF)

    size = PORTION
    sub = iota((size, E), 0) + (start + step) * size
    lo = rows & (LO - 1)
    onehot = jnp.concatenate(
        [jnp.where(sub == lo[i : i + 1, :], 1.0, 0.0).astype(BF) for i in range(NDEV // 4)], axis=1
    )
    total = dot(onehot, spread[...])
    for h in range(HI):
        grad[h] = total[:, h * E : (h + 1) * E]


def scatter(start, steps, asked, incoming, before=()):
    count = NDEV * SLOTS
    return pl.pallas_call(
        functools.partial(scatter_kernel, start),
        grid=(steps,),
        out_shape=slow((HI, LO, E), F32),
        in_specs=[whole((NDEV, E)), whole((count, E))] + [ANY_SPEC] * len(before),
        out_specs=pl.BlockSpec((HI, PORTION, E), lambda i: (0, start + i, 0)),
        scratch_shapes=[pltpu.VMEM((count, HI * E), BF)],
        input_output_aliases={2 + i: i for i in range(len(before))},
        compiler_params=params(),
        cost_estimate=pl.CostEstimate(
            flops=count * ROWS * E, bytes_accessed=2 * 10**6, transcendentals=0
        ),
        name="scatter_rows",
    )(asked, incoming, *in_hbm(*before))


def head_masks():
    lane = iota((1, 2 * HEAD_DIM), 1)
    return [
        jnp.where(lane < HEAD_DIM, 1.0, 0.0).astype(BF),
        jnp.where(lane >= HEAD_DIM, 1.0, 0.0).astype(BF),
    ]


def act(u, mask):
    w = jnp.where(mask, 1.0 + jnp.tanh(u), 0.0)
    p = u * w
    return p.astype(BF), (w + p * (2.0 - w)).astype(BF)


def near_forward_kernel(lengths, q, k, v, halo, probs, slope, attn):
    base = lax.axis_index("seq") * NBD
    length = lengths[lax.axis_index("user")]
    masks = head_masks()
    q16 = q[...] * jnp.asarray(1.0 / 16.0, BF)
    kx = jnp.concatenate([halo[0], k[...]], axis=0)
    vx = jnp.concatenate([halo[1], v[...]], axis=0)
    lane = iota((BLK, 2 * BLK), 1)
    sub = iota((BLK, 2 * BLK), 0)
    vx_m = [vx * m for m in masks]
    both = [jnp.concatenate([q16[i * BLK : (i + 1) * BLK] * m for m in masks]) for i in range(NBD)]
    logits = [dot_nt(both[i], kx[i * BLK : (i + 2) * BLK]) for i in range(NBD)]
    held = []
    for i in range(NBD):
        rows = slice(i * BLK, (i + 1) * BLK)
        at = (base + i - 1) * BLK + lane
        mask = (at >= 0) & (at < length) & (lane <= sub + BLK)
        parts = []
        for h in range(2):
            p, f = act(logits[i][h * BLK : (h + 1) * BLK], mask)
            probs[h, rows, :] = p
            slope[h, rows, :] = f
            parts.append(p)
        held.append(jnp.concatenate(parts, axis=1))
    for i in range(NBD):
        keys = slice(i * BLK, (i + 2) * BLK)
        attn[i * BLK : (i + 1) * BLK, :] = dot(
            held[i], jnp.concatenate([m[keys] for m in vx_m], axis=0)
        )


def unrotate(parts, scratch):
    for d in range(CHUNKS):
        scratch[chunk_of(CHUNKS - d)] = parts[d][...]
    keys = jnp.concatenate([scratch[g] for g in range(GLOB)], axis=0)
    values = jnp.concatenate([scratch[GLOB + g] for g in range(GLOB)], axis=0)
    return keys, values


def far_forward_kernel(
    lengths,
    gids,
    q,
    glob0,
    glob1,
    glob2,
    glob3,
    near,
    gate,
    history,
    w_out,
    probs,
    slope,
    normed_out,
    inv_out,
    user,
    attn,
    scratch,
):
    pair = pl.program_id(0)
    base = lax.axis_index("seq") * NBD
    length = lengths[lax.axis_index("user")]
    masks = head_masks()
    q16 = q[...] * jnp.asarray(1.0 / 16.0, BF)
    kg, vg = unrotate((glob0, glob1, glob2, glob3), scratch)
    lane = iota((BLK, 2 * BLK), 1)
    gid = jnp.where(lane < BLK, gids[0, 0], gids[0, 1])
    at = gid * BLK + lane % BLK
    vg_both = jnp.concatenate([vg * m for m in masks], axis=0)
    logits = dot_nt(jnp.concatenate([q16 * m for m in masks], axis=0), kg)
    held = []
    for i in range(NBD):
        rows = slice(i * BLK, (i + 1) * BLK)
        mask = (gid < base + i - 1) & (at < length)
        parts = []
        for h in range(2):
            p, f = act(logits[h * EVENTS + i * BLK : h * EVENTS + (i + 1) * BLK], mask)
            probs[h, rows, :] = p
            slope[h, rows, :] = f
            parts.append(p)
        held.append(jnp.concatenate(parts, axis=1))
    attn[pair] = near[...] + dot(jnp.concatenate(held, axis=0), vg_both)

    @pl.when(pair == PAIRS - 1)
    def _():
        step = 128
        for r in range(0, EVENTS, step):
            rows = slice(r, r + step)
            x = jnp.concatenate([attn[p, rows, :] for p in range(PAIRS)], axis=1)
            centered = x - jnp.mean(x, axis=1, keepdims=True)
            var = jnp.mean(centered * centered, axis=1, keepdims=True)
            inv = lax.rsqrt(var + 1e-05)
            normed = centered * inv
            normed_out[rows, :] = normed.astype(BF)
            inv_out[rows, :] = inv
            gated = (normed * gate[rows, :].astype(F32)).astype(BF)
            vector = dot(gated, w_out[...]) + history[rows, :].astype(F32)
            rounded = vector.astype(BF)
            user[rows, :E] = rounded
            user[rows, E:] = (vector - rounded.astype(F32)).astype(BF)


def pair_block(rows):
    return pl.BlockSpec((rows, 2 * HEAD_DIM), lambda p: (0, p))


def pair_stack(rows):
    return pl.BlockSpec((2, rows, 2 * HEAD_DIM), lambda p: (0, 0, p))


def head_block():
    return pl.BlockSpec((2, EVENTS, 2 * BLK), lambda p: (p, 0, 0))


SQUARE = slow((HEADS, EVENTS, 2 * BLK), BF)


def near_forward(lengths, q, k, v, halo):
    return pl.pallas_call(
        near_forward_kernel,
        grid=(PAIRS,),
        out_shape=(SQUARE, SQUARE, fast((EVENTS, D), F32)),
        in_specs=[SMEM_SPEC] + [pair_block(EVENTS)] * 3 + [pair_stack(BLK)],
        out_specs=[head_block(), head_block(), pair_block(EVENTS)],
        compiler_params=params(),
        cost_estimate=pl.CostEstimate(
            flops=5 * 10**8, bytes_accessed=7 * 10**6, transcendentals=10**6
        ),
        name="near_forward",
    )(*in_hbm(lengths), q, k, v, halo)


def far_forward(lengths, gids, q, glob, near, gate, history, w_out):
    return pl.pallas_call(
        far_forward_kernel,
        grid=(PAIRS,),
        out_shape=(
            SQUARE,
            SQUARE,
            slow((EVENTS, D), BF),
            slow((EVENTS, 1), F32),
            slow((EVENTS, 2 * E), BF),
        ),
        in_specs=[SMEM_SPEC] * 2
        + [pair_block(EVENTS)]
        + [pair_block(BLK)] * CHUNKS
        + [pair_block(EVENTS)]
        + [whole((EVENTS, D)), whole((EVENTS, E)), whole((D, E))],
        out_specs=[
            head_block(),
            head_block(),
            whole((EVENTS, D)),
            whole((EVENTS, 1)),
            whole((EVENTS, 2 * E)),
        ],
        scratch_shapes=[
            pltpu.VMEM((PAIRS, EVENTS, 2 * HEAD_DIM), F32),
            pltpu.VMEM((CHUNKS, BLK, 2 * HEAD_DIM), BF),
        ],
        compiler_params=params(),
        cost_estimate=pl.CostEstimate(
            flops=6 * 10**8, bytes_accessed=9 * 10**6, transcendentals=10**6
        ),
        name="far_forward",
    )(*in_hbm(lengths, gids), q, *glob, *in_vmem(near), *in_hbm(gate, history, w_out))


def far_backward_kernel(
    d_user,
    w_out,
    inv,
    normed,
    gate,
    q,
    glob0,
    glob1,
    glob2,
    glob3,
    probs,
    slope,
    d_q,
    out0,
    out1,
    out2,
    out3,
    attn_far,
    gate_far,
    scratch,
    d_attn,
    d_gate,
    sems,
):
    pair = pl.program_id(0)
    width = 2 * HEAD_DIM
    copies = [
        pltpu.make_async_copy(
            d_attn.at[p], attn_far.at[:, p * width : (p + 1) * width], sems.at[p]
        )
        for p in range(PAIRS)
    ] + [pltpu.make_async_copy(d_gate, gate_far, sems.at[PAIRS])]

    @pl.when(pair == 0)
    def _():
        step = 128
        for r in range(0, EVENTS, step):
            rows = slice(r, r + step)
            d_gated = dot_nt(d_user[rows, :], w_out[...])
            n = normed[rows, :].astype(F32)
            d_gate[rows, :] = (d_gated * n).astype(BF)
            dn = d_gated * gate[rows, :].astype(F32)
            result = (
                (
                    dn
                    - jnp.mean(dn, axis=1, keepdims=True)
                    - n * jnp.mean(dn * n, axis=1, keepdims=True)
                )
                * inv[rows, :]
            ).astype(BF)
            for p in range(PAIRS):
                d_attn[p, rows, :] = result[:, p * width : (p + 1) * width]
        for copy in copies:
            copy.start()

    masks = head_masks()
    sixteenth = jnp.asarray(1.0 / 16.0, BF)
    q16 = q[...] * sixteenth
    kg, vg = unrotate((glob0, glob1, glob2, glob3), scratch)
    do = d_attn[pair]
    q_t = jnp.concatenate([(q16 * m).T for m in masks], axis=1)
    do_t = jnp.concatenate([(do * m).T for m in masks], axis=1)
    kg_both = jnp.concatenate([kg * (m * sixteenth) for m in masks], axis=0)
    d_probs = dot_nt(jnp.concatenate([do * m for m in masks], axis=0), vg)
    ds = [
        (d_probs[h * EVENTS : (h + 1) * EVENTS] * slope[h].astype(F32)).astype(BF) for h in range(2)
    ]
    d_q[...] = dot(jnp.concatenate(ds, axis=1), kg_both)
    d_k = dot(q_t, jnp.concatenate(ds, axis=0)).T.astype(BF)
    d_v = dot(do_t, jnp.concatenate([probs[0], probs[1]], axis=0)).T.astype(BF)
    for g in range(GLOB):
        scratch[g] = d_k[g * BLK : (g + 1) * BLK]
        scratch[GLOB + g] = d_v[g * BLK : (g + 1) * BLK]
    for d, out in enumerate((out0, out1, out2, out3)):
        out[...] = scratch[chunk_of(d)]

    @pl.when(pair == PAIRS - 1)
    def _():
        for copy in copies:
            copy.wait()


def far_backward(d_user, w_out, inv, normed, gate, q, glob, probs, slope):
    return pl.pallas_call(
        far_backward_kernel,
        grid=(PAIRS,),
        out_shape=(fast((EVENTS, D), F32),)
        + (jax.ShapeDtypeStruct((BLK, D), BF),) * CHUNKS
        + (slow((EVENTS, D), BF),) * 2,
        in_specs=[
            whole((EVENTS, E)),
            whole((D, E)),
            whole((EVENTS, 1)),
            whole((EVENTS, D)),
            whole((EVENTS, D)),
            pair_block(EVENTS),
        ]
        + [pair_block(BLK)] * CHUNKS
        + [head_block()] * 2,
        out_specs=[pair_block(EVENTS)] + [pair_block(BLK)] * CHUNKS + [ANY_SPEC] * 2,
        scratch_shapes=[
            pltpu.VMEM((CHUNKS, BLK, 2 * HEAD_DIM), BF),
            pltpu.VMEM((PAIRS, EVENTS, 2 * HEAD_DIM), BF),
            pltpu.VMEM((EVENTS, D), BF),
            pltpu.SemaphoreType.DMA((PAIRS + 1,)),
        ],
        compiler_params=params(),
        cost_estimate=pl.CostEstimate(flops=10**9, bytes_accessed=7 * 10**6, transcendentals=0),
        name="far_backward",
    )(*in_hbm(d_user, w_out, inv, normed, gate, q), *glob, *in_hbm(probs, slope))


def near_backward_kernel(q, k, v, halo, grad, probs, slope, far, d_q, d_k, d_v, edge):
    masks = head_masks()
    sixteenth = jnp.asarray(1.0 / 16.0, BF)
    q16 = q[...] * sixteenth
    kx = jnp.concatenate([halo[0], k[...]], axis=0)
    vx = jnp.concatenate([halo[1], v[...]], axis=0)
    do = grad[...]
    q_t = [(q16 * m).T for m in masks]
    do_t = [(do * m).T for m in masks]
    kx_m = [kx * (m * sixteenth) for m in masks]
    blocks = [slice(i * BLK, (i + 1) * BLK) for i in range(NBD)]
    windows = [slice(i * BLK, (i + 2) * BLK) for i in range(NBD)]
    d_probs = [
        dot_nt(jnp.concatenate([do[blocks[i]] * m for m in masks], axis=0), vx[windows[i]])
        for i in range(NBD)
    ]
    all_ds = [
        [
            (d_probs[i][h * BLK : (h + 1) * BLK] * slope[h, blocks[i], :].astype(F32)).astype(BF)
            for h in range(2)
        ]
        for i in range(NBD)
    ]
    carry = None
    for i in range(NBD):
        rows, keys, ds = blocks[i], windows[i], all_ds[i]
        near_k = jnp.concatenate([m[keys] for m in kx_m], axis=0)
        d_q[rows, :] = (far[rows, :] + dot(jnp.concatenate(ds, axis=1), near_k)).astype(BF)
        near_p = jnp.concatenate([probs[h, rows, :] for h in range(2)], axis=0)
        dk = dot(jnp.concatenate([t[:, rows] for t in q_t], axis=1), jnp.concatenate(ds, axis=0)).T
        dv = dot(jnp.concatenate([t[:, rows] for t in do_t], axis=1), near_p).T
        if i == 0:
            edge[0] = dk[:BLK].astype(BF)
            edge[1] = dv[:BLK].astype(BF)
        else:
            last = slice((i - 1) * BLK, i * BLK)
            d_k[last, :] = (carry[0] + dk[:BLK]).astype(BF)
            d_v[last, :] = (carry[1] + dv[:BLK]).astype(BF)
        carry = (dk[BLK:], dv[BLK:])
    last = slice((NBD - 1) * BLK, NBD * BLK)
    d_k[last, :] = carry[0].astype(BF)
    d_v[last, :] = carry[1].astype(BF)


def near_backward(q, k, v, halo, grad, probs, slope, far):
    rows = jax.ShapeDtypeStruct((EVENTS, D), BF)
    return pl.pallas_call(
        near_backward_kernel,
        grid=(PAIRS,),
        out_shape=(
            rows,
            slow((EVENTS, D), BF),
            slow((EVENTS, D), BF),
            jax.ShapeDtypeStruct((2, BLK, D), BF),
        ),
        in_specs=[pair_block(EVENTS)] * 3
        + [pair_stack(BLK), pair_block(EVENTS)]
        + [head_block()] * 2
        + [pair_block(EVENTS)],
        out_specs=[pair_block(EVENTS)] * 3 + [pair_stack(BLK)],
        compiler_params=params(),
        cost_estimate=pl.CostEstimate(
            flops=10**9, bytes_accessed=9 * 10**6, transcendentals=0
        ),
        name="near_backward",
    )(q, k, v, halo, *in_hbm(grad), probs, slope, *in_vmem(far))


def middle_kernel(
    lengths, items, code, user, out_far, d_user, score, share, outgoing, sems
):
    sends = []
    portion = NDEV * SLOTS // 4
    user_b = user[:, :E]
    user_t = user[...].T
    mark = code[...].astype(F32)
    first = mark >= FIRST
    rank = jnp.where(first, mark - FIRST, mark)
    group = 16
    size = group * SLOTS
    slot = iota((SLOTS, EVENTS), 0).astype(F32)
    for d in range(0, NDEV, group):
        rows = items[d * SLOTS : d * SLOTS + size, :]
        s = dot(jnp.concatenate([rows, rows], axis=1), user_t)
        for r in range(group):
            own = rank[d + r : d + r + 1, :] == slot
            part = jnp.where(own, s[r * SLOTS : (r + 1) * SLOTS, :], 0.0)
            score[d + r : d + r + 1, :] = jnp.sum(part, axis=0, keepdims=True)
    score0 = jnp.sum(jnp.where(first, score[...], 0.0), axis=0, keepdims=True)
    event = lax.axis_index("seq") * EVENTS + iota((1, EVENTS), 1)
    valid = jnp.where(event < lengths[lax.axis_index("user")], 1.0, 0.0)
    other = (rank >= 0.0) & jnp.logical_not(first)
    side = jnp.where(other, jax.nn.sigmoid(score[...] - score0), 0.0) * valid
    coef = jnp.where(first, -jnp.sum(side, axis=0, keepdims=True), side)
    for d in range(0, NDEV, group):
        rows = slice(d * SLOTS, d * SLOTS + size)
        c = jnp.concatenate(
            [
                jnp.where(rank[r : r + 1, :] == slot, coef[r : r + 1, :], 0.0).astype(BF)
                for r in range(d, d + group)
            ],
            axis=0,
        )
        share[rows, :] = c
        outgoing[rows, :] = dot(c, user_b).astype(BF)
        if rows.stop % portion == 0:
            part = slice(rows.stop - portion, rows.stop)
            sends.append(
                pltpu.make_async_copy(
                    outgoing.at[part, :], out_far.at[part, :], sems.at[len(sends)]
                )
            )
            sends[-1].start()
    d_user[...] = dot_tn(items[...], share[...]).T.astype(BF)
    for copy in sends:
        copy.wait()


def middle(lengths, items, code, user):
    return pl.pallas_call(
        middle_kernel,
        out_shape=(slow((NDEV * SLOTS, E), BF), slow((EVENTS, E), BF)),
        in_specs=[SMEM_SPEC] + [VMEM_SPEC] * 3,
        out_specs=[ANY_SPEC, VMEM_SPEC],
        scratch_shapes=[
            pltpu.VMEM((NDEV, EVENTS), F32),
            pltpu.VMEM((NDEV * SLOTS, EVENTS), BF),
            pltpu.VMEM((NDEV * SLOTS, E), BF),
            pltpu.SemaphoreType.DMA((4,)),
        ],
        compiler_params=params(),
        cost_estimate=pl.CostEstimate(
            flops=2 * 10**9, bytes_accessed=6 * 10**6, transcendentals=10**5
        ),
        name="ranking",
    )(*in_hbm(lengths), *in_vmem(items), *in_hbm(code, user))


def finish_kernel(gids, d_k, d_v, edge, glob0, glob1, glob2, glob3, key_out, value_out):
    seq = lax.axis_index("seq")
    outs = (key_out, value_out)
    for which, mine in enumerate((d_k, d_v)):
        outs[which][...] = mine[...]
        tail = slice(EVENTS - BLK, EVENTS)
        outs[which][tail, :] = (mine[tail, :].astype(F32) + edge[which].astype(F32)).astype(BF)
    for d, more in enumerate((glob0, glob1, glob2, glob3)):
        c = chunk_of(CHUNKS - d)
        gid = gids[0, c % GLOB]
        place = pl.ds(pl.multiple_of((gid % NBD) * BLK, BLK), BLK)
        for which in range(2):

            @pl.when((gid // NBD == seq) & (c // GLOB == which))
            def _():
                out = outs[which]
                out[place, :] = (out[place, :].astype(F32) + more[...].astype(F32)).astype(BF)


def finish(gids, d_k, d_v, edge, total):
    rows = jax.ShapeDtypeStruct((EVENTS, D), BF)
    return pl.pallas_call(
        finish_kernel,
        out_shape=(rows, rows),
        in_specs=[SMEM_SPEC] + [VMEM_SPEC] * (3 + CHUNKS),
        out_specs=[VMEM_SPEC] * 2,
        compiler_params=params(),
        cost_estimate=pl.CostEstimate(flops=10**6, bytes_accessed=3 * 10**6, transcendentals=0),
        name="add_received",
    )(*in_hbm(gids), d_k, d_v, edge, *total)


def from_behind(block, axis, distance):
    size = lax.axis_size(axis)
    return lax.ppermute(block, axis, [(i, (i + distance) % size) for i in range(size)])


def exchange(x, axis):
    return lax.all_to_all(x, axis, split_axis=0, concat_axis=0, tiled=True)


def around_x(x, distance):
    pairs = [(i, i // XSIZE * XSIZE + (i + distance) % XSIZE) for i in range(NSEQ)]
    return lax.ppermute(x, "seq", pairs)


def around_z(x, distance):
    return lax.ppermute(x, "seq", [(i, (i + distance * XSIZE) % NSEQ) for i in range(NSEQ)])


def add_all(parts):
    return sum(p.astype(F32) for p in parts).astype(BF)


def from_x(chunks):
    return [chunks[0]] + [around_x(chunks[d], d) for d in range(1, CHUNKS)]


def from_z(mine):
    return [mine] + [around_z(mine, d) for d in range(1, NSEQ // XSIZE)]


def share_x(mine):
    return [mine] + [around_x(mine, d) for d in range(1, CHUNKS)]


def together(*values):
    return lax.optimization_barrier(values)


def on_device(
    query, key, value, gate, history, w_out, table, item_owner, item_row, gids, lengths
):
    q, k, v = query[0], key[0], value[0]
    owner = jnp.transpose(item_owner, (2, 0, 1))
    row = jnp.transpose(item_row, (2, 0, 1))
    tail, *cand = pieces(gids, k, v)
    parts = from_x(cand)
    owner, _ = together(owner, cand[0])
    req, code = route(owner, row)
    req, *parts = together(req, *parts)
    mine = add_all(parts)
    parts = from_z(mine)
    req, _ = together(req, mine)
    asked = exchange(req.reshape(NDEV, 1, E), ("seq", "user")).reshape(NDEV, E)
    mine = add_all(parts)
    glob = share_x(mine)
    tail, _ = together(tail, mine)
    halo = from_behind(tail, "seq", 1)
    asked, _ = together(asked, mine)
    found, asked = gather(asked, table)
    found, halo, *glob = together(found, halo, *glob)
    items = exchange(found.reshape(NDEV, SLOTS, E), ("seq", "user")).reshape(NDEV * SLOTS, E)
    near_p, near_f, near = near_forward(lengths, q, k, v, halo)
    far_p, far_f, normed, inv, user = far_forward(
        lengths, gids, q, glob, near, gate[0], history[0], w_out
    )
    outgoing, d_user = middle(lengths, items, code, user)
    incoming = exchange(outgoing.reshape(NDEV, SLOTS, E), ("seq", "user"))
    far_q, *d_glob, d_attn, d_gate = far_backward(
        d_user, w_out, inv, normed, gate[0], q, glob, far_p, far_f
    )
    parts = from_x(d_glob)
    d_q, d_k, d_v, edge = near_backward(q, k, v, halo, d_attn, near_p, near_f, far_q)
    d_k, *parts = together(d_k, *parts)
    mine = add_all(parts)
    back = from_behind(edge, "seq", -1)
    incoming, mine = together(incoming.reshape(NDEV * SLOTS, E), mine)
    grad = scatter(0, 1, asked, incoming)
    grad, *parts = together(grad, *from_z(mine))
    mine = add_all(parts)
    grad, mine = together(grad, mine)
    grad = scatter(1, 1, asked, incoming, (grad,))
    grad, *total = together(grad, *share_x(mine))
    d_key, d_value = finish(gids, d_k, d_v, back, total)
    return (d_q[None], d_key[None], d_value[None], d_gate[None], grad.reshape(ROWS, E))


def solution(mesh):
    return jax.shard_map(
        on_device,
        mesh=mesh,
        in_specs=(
            P("user", "seq", None),
            P("user", "seq", None),
            P("user", "seq", None),
            P("user", "seq", None),
            P("user", "seq", None),
            P(),
            P(("seq", "user"), None),
            P("user", "seq", None),
            P("user", "seq", None),
            P("user", None),
            P(),
        ),
        out_specs=(
            P("user", "seq", None),
            P("user", "seq", None),
            P("user", "seq", None),
            P("user", "seq", None),
            P(("seq", "user"), None),
        ),
        check_vma=False,
    )
```
